512 devices in a mesh: ha: 8 (over y_hi, x), sa: 64 (over z, y_lo, core).
Axes of the slice: x: 4, y: 4 (y_hi: 2, y_lo: 2; y = y_hi * 2 + y_lo), z: 16, core: 2. Of those that a mesh axis runs over, the one named last changes fastest.
Arguments:
- enc_query: bfloat16 [131072, 1024], P(('ha', 'sa'))
- enc_key: bfloat16 [131072, 1024], P(('ha', 'sa')), may hold values from -6 to 6
- enc_value: bfloat16 [131072, 1024], P(('ha', 'sa')), may hold values from -6 to 6
- enc_resid: bfloat16 [131072, 1024], P(('ha', 'sa')), may hold values from -24 to 24
- out_weight: bfloat16 [1024, 1024], P('sa'), may hold values from -0.1875 to 0.1875
- norm_gain: float32 [1024], replicated, may hold values from 0.25 to 1.75
- kv_weight: bfloat16 [1024, 8, 256], P(None, 'ha'), may hold values from -0.1875 to 0.1875
- cross_query: bfloat16 [64, 8, 1024], P(None, 'ha')
- span_ids: int32 [512], replicated, may hold values from 0 to 511, each once
- seg_lengths: int32 [512], replicated, may hold values from 1 to 256, as said below
Outputs:
- cross_out: float32 [64, 8, 1024], P('sa', 'ha')
The draws below stay inside these ranges and needn't reach their ends.
Inputs may be any that keep to these rules, and one draw needn't show every extreme that they name: `seg_lengths`: valid tokens of each segment; some segment is full.
All inputs are finite; a program needn't handle non-finite values.
Results may differ from the reference program's by a relative error of at most 0.015.
Values may be sent and summed in bfloat16 or wider, within the bound.
No kernel may reach another device: no remote copies, remote signals or barrier semaphores. Data moves between devices by JAX's collectives and lax.ppermute only.
A program may use at most 128 MiB of HBM per device.

```python
import math
import jax
import jax.numpy as jnp
from jax import lax

D_ENC = 1024
ENC_HEADS = 16
KV_HEADS = 8
GROUP = 8
HEAD = 128
SEG_LEN = 256
QTAIL = 64
SEGMENTS = 512


def draw_enc_query(key, part):
    key = jax.random.fold_in(key, 11)
    first = jax.random.fold_in(key, 0)
    values = jax.random.normal(first, (SEGMENTS * SEG_LEN, ENC_HEADS, D_ENC // ENC_HEADS), jnp.float32)
    factor = 2.0 * jnp.ones((SEGMENTS * SEG_LEN, ENC_HEADS, 1), jnp.float32)
    return (values * factor).reshape(SEGMENTS * SEG_LEN, D_ENC).astype(jnp.bfloat16)


def draw_cross_query(key, part):
    key = jax.random.fold_in(key, 12)
    first = jax.random.fold_in(key, 0)
    values = jax.random.normal(first, (QTAIL, KV_HEADS, GROUP, HEAD), jnp.float32)
    factor = 4.0 * jnp.ones((QTAIL, KV_HEADS, GROUP, 1), jnp.float32)
    return (values * factor).reshape(QTAIL, KV_HEADS, GROUP * HEAD).astype(jnp.bfloat16)


def draw_seg_lengths(key, part):
    key = jax.random.fold_in(key, 13)
    first, second = jax.random.split(key)
    ragged = jax.random.randint(first, (SEGMENTS,), 1, SEG_LEN + 1, jnp.int32)
    picked = jax.random.randint(second, (SEGMENTS,), 0, 3, jnp.int32) == 0
    result = jnp.where(picked, ragged, SEG_LEN).astype(jnp.int32)
    return result.at[0].set(SEG_LEN)


def draw_enc_resid(key, part):
    key = jax.random.fold_in(key, 14)
    first = jax.random.fold_in(key, 0)
    rows = jax.random.normal(first, (SEGMENTS * SEG_LEN, D_ENC), jnp.float32)
    values = jnp.clip(0.5 * rows, -3.0, 3.0)
    return values.astype(jnp.bfloat16)


def level_of(stream_key, shape, cuts, least, high):
    gain, own = 1.0, jax.random.fold_in(stream_key, 6)
    for axis_at, blocks in cuts:
        draws = jnp.exp(jax.random.uniform(jax.random.fold_in(own, axis_at), (blocks,), jnp.float32, least / len(cuts), high / len(cuts)))
        gain = gain * jnp.repeat(draws, shape[axis_at] // blocks).reshape([-1 if axis == axis_at else 1 for axis in range(len(shape))])
    return gain


def gaussian(rng, dims, spread, most, pieces=(), dtype=jnp.bfloat16):
    array = spread * jax.random.normal(rng, dims, jnp.float32)
    if pieces:
        array = array * level_of(rng, dims, pieces, -0.22, 0.18)
    return jnp.clip(array, -most, most).astype(dtype)


def setup_inputs(seed: int = 0) -> dict:
    key_list = jax.random.split(jax.random.key(seed), 11)
    return {
        "enc_query": draw_enc_query(jax.random.fold_in(key_list[10], 71), 0),
        "enc_key": gaussian(key_list[1], (SEGMENTS * SEG_LEN, D_ENC), 1.0, 6.0, ((0, 512),)),
        "enc_value": gaussian(key_list[2], (SEGMENTS * SEG_LEN, D_ENC), 1.0, 6.0, ((0, 512),)),
        "enc_resid": draw_enc_resid(jax.random.fold_in(key_list[10], 71), 0),
        "out_weight": gaussian(key_list[4], (D_ENC, D_ENC), D_ENC ** -0.5, 0.1875, ((0, 64),)),
        "norm_gain": jnp.clip(1.0 + 0.15 * jax.random.normal(key_list[5], (D_ENC,), jnp.float32), 0.25, 1.75),
        "kv_weight": gaussian(key_list[6], (D_ENC, KV_HEADS, 2 * HEAD), D_ENC ** -0.5, 0.1875, ((1, 8),)),
        "cross_query": draw_cross_query(jax.random.fold_in(key_list[10], 71), 0),
        "span_ids": jax.random.permutation(key_list[8], SEGMENTS).astype(jnp.int32),
        "seg_lengths": draw_seg_lengths(jax.random.fold_in(key_list[10], 71), 0),
    }


masked_value = -1e+30
query_block = 64

def encode_segment(pack, out_weight, norm_gain):
    query_seg, key_seg, value_seg, resid_seg, valid_len = pack
    head_dim = D_ENC // ENC_HEADS
    query_heads = query_seg.astype(jnp.float32).reshape(SEG_LEN, ENC_HEADS, head_dim)
    key_heads = key_seg.astype(jnp.float32).reshape(SEG_LEN, ENC_HEADS, head_dim)
    value_heads = value_seg.astype(jnp.float32).reshape(SEG_LEN, ENC_HEADS, head_dim)
    scores = jnp.einsum('qhd,khd->hqk', query_heads, key_heads) / math.sqrt(head_dim)
    keep = jnp.arange(SEG_LEN).astype(jnp.int32) < valid_len
    scores = jnp.where(keep[None, None, :], scores, masked_value)
    highest = lax.optimization_barrier(jnp.max(scores, axis=-1, keepdims=True))
    expo = jnp.exp(scores - highest)
    probs = (expo / lax.optimization_barrier(jnp.sum(expo, axis=-1, keepdims=True))).astype(jnp.bfloat16)
    probs = lax.optimization_barrier(probs).astype(jnp.float32)
    context = jnp.einsum('hqk,khd->qhd', probs, value_heads).astype(jnp.bfloat16).reshape(SEG_LEN, D_ENC)
    hidden = resid_seg.astype(jnp.float32) + jnp.dot(context, out_weight, preferred_element_type=jnp.float32)
    factor = lax.rsqrt(lax.optimization_barrier(jnp.mean(hidden * hidden, axis=-1, keepdims=True)) + 1e-05)
    return (hidden * factor * norm_gain.astype(jnp.float32)).astype(jnp.bfloat16)

def cross_block(query_rows, keys, values, keep_all):
    scores = jnp.einsum('qgd,rd->qgr', query_rows, keys) / math.sqrt(HEAD)
    scores = jnp.where(keep_all[None, None, :], scores, masked_value)
    highest = lax.optimization_barrier(jnp.max(scores, axis=-1, keepdims=True))
    expo = jnp.exp(scores - highest)
    total = lax.optimization_barrier(jnp.sum(expo, axis=-1))
    weights = lax.optimization_barrier(expo.astype(jnp.bfloat16)).astype(jnp.float32)
    summed = jnp.einsum('qgr,rd->qgd', weights, values)
    return summed / total[..., None]

def cross_head(pack, keep_all):
    query_head, keyval_head = pack
    keys = keyval_head[:, :HEAD].astype(jnp.float32)
    values = keyval_head[:, HEAD:].astype(jnp.float32)
    blocks = query_head.reshape(QTAIL // query_block, query_block, GROUP, HEAD)
    result = lax.map(lambda rows: cross_block(rows, keys, values, keep_all), blocks)
    return result.reshape(QTAIL, GROUP, HEAD)

def reference(enc_query, enc_key, enc_value, enc_resid, out_weight, norm_gain, kv_weight, cross_query, span_ids, seg_lengths):
    valid = seg_lengths[span_ids].astype(jnp.int32)
    shaped = lambda field: field.reshape(SEGMENTS, SEG_LEN, D_ENC)
    encoded = lax.map(lambda pack: encode_segment(pack, out_weight, norm_gain), (shaped(enc_query), shaped(enc_key), shaped(enc_value), shaped(enc_resid), valid))
    encoded = encoded.reshape(SEGMENTS * SEG_LEN, D_ENC)
    keyval = jnp.dot(encoded, kv_weight.reshape(D_ENC, KV_HEADS * 2 * HEAD), preferred_element_type=jnp.float32)
    keyval = keyval.astype(jnp.bfloat16).reshape(SEGMENTS * SEG_LEN, KV_HEADS, 2 * HEAD)
    keep_all = (jnp.arange(SEG_LEN).astype(jnp.int32)[None, :] < valid[:, None]).reshape(-1)
    queries = cross_query.astype(jnp.float32).reshape(QTAIL, KV_HEADS, GROUP, HEAD).transpose(1, 0, 2, 3)
    result = lax.map(lambda pack: cross_head(pack, keep_all), (queries, keyval.transpose(1, 0, 2)))
    return result.transpose(1, 0, 2, 3).reshape(QTAIL, KV_HEADS, GROUP * HEAD).astype(jnp.float32)
```

```python
import functools
import math

import jax
import jax.numpy as jnp
import numpy as np
from jax import lax
from jax.experimental import pallas as pl
from jax.experimental.pallas import tpu as pltpu
from jax.sharding import Mesh, PartitionSpec as P

D_ENC = 1024
ENC_HEADS = 16
ENC_HEAD = D_ENC // ENC_HEADS
KV_HEADS = 8
GROUP = 8
HEAD = 128
SEG_LEN = 256
QTAIL = 64
MASKED = -1e30

PARTS = ("yh", "x", "z", "yl", "c")
HA = ("yh", "x")
SA = ("z", "yl", "c")
PLANE = ("yh", "x", "yl")


def params(**kw):
    return pltpu.CompilerParams(vmem_limit_bytes=48 * 1024 * 1024, **kw)


def dot(a, b):
    return jnp.dot(a, b, preferred_element_type=jnp.float32)


def dot_t(a, b):
    return lax.dot_general(a, b, (((1,), (1,)), ((), ())), preferred_element_type=jnp.float32)


def encoder_attention_kernel(slot_ref, span_ref, len_ref, q_ref, k_ref, v_ref, o_ref):
    valid = len_ref[span_ref[slot_ref[0]]]
    keep = lax.broadcasted_iota(jnp.int32, (1, SEG_LEN), 1) < valid
    bias = jnp.where(keep, 0.0, MASKED).astype(jnp.float32)
    low = lax.broadcasted_iota(jnp.int32, (SEG_LEN, 2 * ENC_HEAD), 1) < ENC_HEAD
    for pair in range(ENC_HEADS // 2):
        cols = slice(pair * 2 * ENC_HEAD, (pair + 1) * 2 * ENC_HEAD)
        q, k, v = q_ref[:, cols], k_ref[:, cols], v_ref[:, cols]
        zero = jnp.zeros_like(k)
        parts = []
        for mine in (low, jnp.logical_not(low)):
            scores = dot_t(q, jnp.where(mine, k, zero)) * (1.0 / math.sqrt(ENC_HEAD)) + bias
            expo = jnp.exp(scores - jnp.max(scores, axis=-1, keepdims=True))
            probs = (expo * (1.0 / jnp.sum(expo, axis=-1, keepdims=True))).astype(jnp.bfloat16)
            parts.append(dot(probs, v))
        o_ref[:, cols] = jnp.where(low, parts[0], parts[1]).astype(jnp.bfloat16)


def encoder_attention(slot, span_ids, seg_lengths, q, k, v):
    smem = pl.BlockSpec(memory_space=pltpu.SMEM)
    vmem = pl.BlockSpec(memory_space=pltpu.VMEM)
    return pl.pallas_call(
        encoder_attention_kernel,
        out_shape=jax.ShapeDtypeStruct((SEG_LEN, D_ENC), jnp.bfloat16),
        in_specs=[smem, smem, smem, vmem, vmem, vmem],
        out_specs=vmem,
        compiler_params=params(),
        cost_estimate=pl.CostEstimate(
            flops=8 * SEG_LEN * SEG_LEN * D_ENC, bytes_accessed=8 * SEG_LEN * D_ENC,
            transcendentals=SEG_LEN * SEG_LEN * ENC_HEADS),
        name="encoder_attention",
    )(slot, span_ids, seg_lengths, q, k, v)


def encode_kernel(core_ref, ctx_ref, w_mine_ref, w_other_ref, resid_ref, gain_ref, kv_mine_ref,
                  kv_other_ref, o_ref, w_ref, enc_ref):
    core = core_ref[0]
    for part_ref, at in ((w_mine_ref, core), (w_other_ref, 1 - core)):
        for yh in range(2):
            for x in range(4):
                for yl in range(2):
                    ha = yh * 4 + x
                    row = pl.multiple_of(32 * yl + 16 * at, 16)
                    w_ref[:, pl.ds(row, 16), HEAD * ha:HEAD * (ha + 1)] = part_ref[ha * 2 + yl]
    weight = w_ref[...].reshape(D_ENC, D_ENC)
    hidden = resid_ref[...].astype(jnp.float32) + dot(ctx_ref[...], weight)
    factor = lax.rsqrt(jnp.mean(hidden * hidden, axis=-1, keepdims=True) + 1e-05)
    encoded = (hidden * factor * gain_ref[...]).astype(jnp.bfloat16)
    half = D_ENC // 2
    enc_ref[0] = encoded[:, :half]
    enc_ref[1] = encoded[:, half:]
    mine, other = enc_ref[core], enc_ref[1 - core]
    for h in range(KV_HEADS):
        o_ref[h] = (dot(mine, kv_mine_ref[h]) + dot(other, kv_other_ref[h])).astype(jnp.bfloat16)


def encode(core, ctx, w_mine, w_other, resid, gain, kv_mine, kv_other):
    smem = pl.BlockSpec(memory_space=pltpu.SMEM)
    vmem = pl.BlockSpec(memory_space=pltpu.VMEM)
    return pl.pallas_call(
        encode_kernel,
        out_shape=jax.ShapeDtypeStruct((KV_HEADS, SEG_LEN, 2 * HEAD), jnp.bfloat16),
        in_specs=[smem] + [vmem] * 7,
        out_specs=vmem,
        scratch_shapes=[pltpu.VMEM((16, 64, D_ENC), jnp.bfloat16),
                        pltpu.VMEM((2, SEG_LEN, D_ENC // 2), jnp.bfloat16)],
        compiler_params=params(),
        cost_estimate=pl.CostEstimate(
            flops=6 * SEG_LEN * D_ENC * D_ENC, bytes_accessed=8 * D_ENC * D_ENC, transcendentals=SEG_LEN),
        name="encode_keyval",
    )(core, ctx, w_mine, w_other, resid, gain, kv_mine, kv_other)


def cross_kernel(slots, first_ref, span_ref, len_ref, q_ref, kv_ref, o_ref):
    scale = 1.0 / math.sqrt(HEAD)
    lane = lax.broadcasted_iota(jnp.int32, (1, SEG_LEN), 1)
    bias = []
    for s in range(slots):
        valid = len_ref[span_ref[first_ref[0] + s * first_ref[1]]]
        bias.append(jnp.where(lane < valid, 0.0, MASKED).astype(jnp.float32))
    bias = jnp.concatenate(bias, axis=1)
    keys = kv_ref[:, :, :HEAD].reshape(slots * SEG_LEN, HEAD)
    values = kv_ref[:, :, HEAD:].reshape(slots * SEG_LEN, HEAD)
    rows = 128
    queries = rows // GROUP
    column = lax.broadcasted_iota(jnp.int32, (rows, HEAD), 1)
    for b in range(QTAIL // queries):
        q = q_ref[b * rows:(b + 1) * rows]
        scores = dot_t(q, keys) + bias
        top = jnp.max(scores, axis=-1, keepdims=True)
        expo = jnp.exp((scores - top) * scale)
        total = jnp.sum(expo, axis=-1, keepdims=True)
        average = dot(expo.astype(jnp.bfloat16), values) / total
        level = jnp.broadcast_to(top * scale + jnp.log(total), (rows, HEAD))
        high = level.astype(jnp.bfloat16).astype(jnp.float32)
        middle = (level - high).astype(jnp.bfloat16).astype(jnp.float32)
        rest = level - high - middle
        split = jnp.where(column == 0, high, jnp.where(column == 1, middle, rest))
        o_ref[b * queries:(b + 1) * queries, :GROUP] = average.reshape(queries, GROUP, HEAD).astype(jnp.bfloat16)
        o_ref[b * queries:(b + 1) * queries, GROUP:] = split.reshape(queries, GROUP, HEAD).astype(jnp.bfloat16)


def cross_attention(first, span_ids, seg_lengths, q, kv):
    smem = pl.BlockSpec(memory_space=pltpu.SMEM)
    vmem = pl.BlockSpec(memory_space=pltpu.VMEM)
    slots = kv.shape[0]
    return pl.pallas_call(
        functools.partial(cross_kernel, slots),
        out_shape=jax.ShapeDtypeStruct((QTAIL, 2 * GROUP, HEAD), jnp.bfloat16),
        in_specs=[smem, smem, smem, vmem, vmem],
        out_specs=vmem,
        compiler_params=params(),
        name="cross_attention",
    )(first, span_ids, seg_lengths, q, kv)


def merge_kernel(part_ref, o_ref):
    average = part_ref[:, :GROUP].astype(jnp.float32)
    pieces = part_ref[:, GROUP:, :3].astype(jnp.float32)
    level = jnp.sum(pieces, axis=-1, keepdims=True)
    weight = jnp.exp(level - jnp.max(level, axis=0, keepdims=True))
    o_ref[...] = jnp.sum(average * weight, axis=0) / jnp.sum(weight, axis=0)


def merge(parts):
    vmem = pl.BlockSpec(memory_space=pltpu.VMEM)
    return pl.pallas_call(
        merge_kernel,
        out_shape=jax.ShapeDtypeStruct((GROUP, HEAD), jnp.float32),
        in_specs=[vmem],
        out_specs=vmem,
        name="merge_partials",
    )(parts)


def spread(block, axes):
    count = lax.axis_size(axes)
    copies = jnp.broadcast_to(block[None], (count,) + block.shape)
    return lax.all_to_all(copies, axes, 0, 0, tiled=True)


def local(enc_query, enc_key, enc_value, enc_resid, out_weight, norm_gain, kv_weight, cross_query,
          span_ids, seg_lengths):
    ha = lax.axis_index(HA)
    sa = lax.axis_index(SA)
    sa_count = lax.axis_size(SA)
    core = lax.axis_index("c")

    swap = functools.partial(lax.ppermute, axis_name="c", perm=[(0, 1), (1, 0)])

    with jax.named_scope("gather_kv_weight"):
        half = D_ENC // 2
        kv_half = lax.dynamic_slice_in_dim(kv_weight.reshape(D_ENC, 2 * HEAD), core * half, half, 0)
        kv_mine = lax.all_gather(kv_half, HA)
        kv_other = swap(kv_mine)

    with jax.named_scope("gather_out_weight"):
        mine = lax.dynamic_slice_in_dim(out_weight, ha * HEAD, HEAD, 1)
        w_mine = spread(spread(mine, "z"), PLANE).reshape(16, 16, 16, HEAD)
        w_other = swap(w_mine)

    slot = (ha * sa_count + sa).reshape(1).astype(jnp.int32)
    context = encoder_attention(slot, span_ids, seg_lengths, enc_query, enc_key, enc_value)
    keyval = encode(core.reshape(1).astype(jnp.int32), context, w_mine, w_other, enc_resid,
                    norm_gain.reshape(1, D_ENC), kv_mine, kv_other)
    with jax.named_scope("exchange_keyval"):
        keyval = lax.all_to_all(keyval, HA, 0, 0, tiled=True)
    first = jnp.stack([sa, sa_count]).astype(jnp.int32)
    parts = cross_attention(first, span_ids, seg_lengths, cross_query.reshape(QTAIL * GROUP, HEAD), keyval)
    with jax.named_scope("exchange_partials"):
        parts = lax.all_to_all(parts, SA, 0, 0, tiled=True)
    return merge(parts).reshape(1, 1, GROUP * HEAD)


def solution(mesh):
    fine = Mesh(mesh.devices.reshape(2, 4, 16, 2, 2), PARTS)
    rows = P(PARTS, None)
    heads = P(None, HA, None)
    placed = (rows, rows, rows, rows, P(SA, None), P(), heads, heads, P(), P())
    return jax.shard_map(
        local, mesh=fine, in_specs=placed, out_specs=P(SA, HA, None), check_vma=False
    )
```

```python
import functools
import math

import jax
import jax.numpy as jnp
import numpy as np
from jax import lax
from jax.experimental import pallas as pl
from jax.experimental.pallas import tpu as pltpu
from jax.sharding import Mesh, PartitionSpec as P

D_ENC = 1024
ENC_HEADS = 16
ENC_HEAD = D_ENC // ENC_HEADS
KV_HEADS = 8
GROUP = 8
HEAD = 128
SEG_LEN = 256
QTAIL = 64
MASKED = -1e30

PARTS = ("yh", "x", "z", "yl", "c")
HA = ("yh", "x")
SA = ("z", "yl", "c")
PLANE = ("yh", "x", "yl")


def params(**kw):
    return pltpu.CompilerParams(vmem_limit_bytes=48 * 1024 * 1024, **kw)


def dot(a, b):
    return jnp.dot(a, b, preferred_element_type=jnp.float32)


def dot_t(a, b):
    return lax.dot_general(a, b, (((1,), (1,)), ((), ())), preferred_element_type=jnp.float32)


def encoder_attention_kernel(slot_ref, span_ref, len_ref, q_ref, k_ref, v_ref, o_ref):
    valid = len_ref[span_ref[slot_ref[0]]]
    keep = lax.broadcasted_iota(jnp.int32, (1, SEG_LEN), 1) < valid
    bias = jnp.where(keep, 0.0, MASKED).astype(jnp.float32)
    low = lax.broadcasted_iota(jnp.int32, (SEG_LEN, 2 * ENC_HEAD), 1) < ENC_HEAD
    for pair in range(ENC_HEADS // 2):
        cols = slice(pair * 2 * ENC_HEAD, (pair + 1) * 2 * ENC_HEAD)
        q, k, v = q_ref[:, cols], k_ref[:, cols], v_ref[:, cols]
        zero = jnp.zeros_like(k)
        parts = []
        for mine in (low, jnp.logical_not(low)):
            scores = dot_t(q, jnp.where(mine, k, zero)) * (1.0 / math.sqrt(ENC_HEAD)) + bias
            expo = jnp.exp(scores - jnp.max(scores, axis=-1, keepdims=True))
            probs = (expo * (1.0 / jnp.sum(expo, axis=-1, keepdims=True))).astype(jnp.bfloat16)
            parts.append(dot(probs, v))
        o_ref[:, cols] = jnp.where(low, parts[0], parts[1]).astype(jnp.bfloat16)


def encoder_attention(slot, span_ids, seg_lengths, q, k, v):
    smem = pl.BlockSpec(memory_space=pltpu.SMEM)
    vmem = pl.BlockSpec(memory_space=pltpu.VMEM)
    return pl.pallas_call(
        encoder_attention_kernel,
        out_shape=jax.ShapeDtypeStruct((SEG_LEN, D_ENC), jnp.bfloat16),
        in_specs=[smem, smem, smem, vmem, vmem, vmem],
        out_specs=vmem,
        compiler_params=params(),
        cost_estimate=pl.CostEstimate(
            flops=8 * SEG_LEN * SEG_LEN * D_ENC, bytes_accessed=8 * SEG_LEN * D_ENC,
            transcendentals=SEG_LEN * SEG_LEN * ENC_HEADS),
        name="encoder_attention",
    )(slot, span_ids, seg_lengths, q, k, v)


def encode_kernel(core_ref, ctx_ref, mine_ref, other_ref, resid_ref, gain_ref, kv_mine_ref,
                  kv_other_ref, o_ref, w_ref, enc_ref):
    core = core_ref[0]
    for part_ref, at in ((mine_ref, core), (other_ref, 1 - core)):
        for ha in range(KV_HEADS):
            for yl in range(2):
                row = pl.multiple_of(32 * yl + 16 * at, 16)
                w_ref[:, pl.ds(row, 16), HEAD * ha:HEAD * (ha + 1)] = (
                    part_ref[ha * 2 + yl, :256].reshape(16, 16, HEAD))
    weight = w_ref[...].reshape(D_ENC, D_ENC)
    hidden = resid_ref[...].astype(jnp.float32) + dot(ctx_ref[...], weight)
    factor = lax.rsqrt(jnp.mean(hidden * hidden, axis=-1, keepdims=True) + 1e-05)
    encoded = (hidden * factor * gain_ref[...]).astype(jnp.bfloat16)
    for piece in range(4):
        enc_ref[piece] = encoded[:, piece * 256:(piece + 1) * 256]
    near, far = enc_ref[core], enc_ref[1 - core]
    near_last, far_last = enc_ref[2 + core], enc_ref[3 - core]

    def first_rows(ref, h):
        return jnp.concatenate(
            [jnp.concatenate([ref[2 * h + yl, 256:384], ref[2 * h + yl, 384:]], axis=1) for yl in range(2)],
            axis=0)

    for h in range(KV_HEADS):
        total = dot(near, first_rows(mine_ref, h)) + dot(far, first_rows(other_ref, h))
        total += dot(near_last, kv_mine_ref[h]) + dot(far_last, kv_other_ref[h])
        o_ref[h] = total.astype(jnp.bfloat16)


def encode(core, ctx, mine, other, resid, gain, kv_mine, kv_other):
    smem = pl.BlockSpec(memory_space=pltpu.SMEM)
    vmem = pl.BlockSpec(memory_space=pltpu.VMEM)
    return pl.pallas_call(
        encode_kernel,
        out_shape=jax.ShapeDtypeStruct((KV_HEADS, SEG_LEN, 2 * HEAD), jnp.bfloat16),
        in_specs=[smem] + [vmem] * 7,
        out_specs=vmem,
        scratch_shapes=[pltpu.VMEM((16, 64, D_ENC), jnp.bfloat16),
                        pltpu.VMEM((4, SEG_LEN, 256), jnp.bfloat16)],
        compiler_params=params(),
        cost_estimate=pl.CostEstimate(
            flops=6 * SEG_LEN * D_ENC * D_ENC, bytes_accessed=8 * D_ENC * D_ENC, transcendentals=SEG_LEN),
        name="encode_keyval",
    )(core, ctx, mine, other, resid, gain, kv_mine, kv_other)


def cross_kernel(slots, first_ref, span_ref, len_ref, q_ref, kv_ref, o_ref):
    scale = 1.0 / math.sqrt(HEAD)
    lane = lax.broadcasted_iota(jnp.int32, (1, SEG_LEN), 1)
    bias = []
    for s in range(slots):
        valid = len_ref[span_ref[first_ref[0] + s * first_ref[1]]]
        bias.append(jnp.where(lane < valid, 0.0, MASKED).astype(jnp.float32))
    bias = jnp.concatenate(bias, axis=1)
    keys = kv_ref[:, :, :HEAD].reshape(slots * SEG_LEN, HEAD)
    values = kv_ref[:, :, HEAD:].reshape(slots * SEG_LEN, HEAD)
    rows = 2 * QTAIL
    column = lax.broadcasted_iota(jnp.int32, (rows, HEAD), 1)
    levels = jnp.zeros((rows, HEAD), jnp.float32)

    def put(at, block):
        block = block.reshape(2, QTAIL, HEAD)
        o_ref[:, :, at * HEAD:(at + 1) * HEAD] = jnp.stack([block[0], block[1]], axis=1).astype(jnp.bfloat16)

    for b in range(GROUP // 2):
        q = q_ref[b * rows:(b + 1) * rows]
        scores = dot_t(q, keys) + bias
        top = jnp.max(scores, axis=-1, keepdims=True)
        expo = jnp.exp((scores - top) * scale)
        total = jnp.sum(expo, axis=-1, keepdims=True)
        put(b, dot(expo.astype(jnp.bfloat16), values) / total)
        level = jnp.broadcast_to(top * scale + jnp.log(total), (rows, HEAD))
        high = level.astype(jnp.bfloat16).astype(jnp.float32)
        middle = (level - high).astype(jnp.bfloat16).astype(jnp.float32)
        rest = level - high - middle
        for k, part in enumerate((high, middle, rest)):
            levels = jnp.where(column == 3 * b + k, part, levels)
    put(GROUP // 2, levels)


def cross_attention(first, span_ids, seg_lengths, q, kv):
    smem = pl.BlockSpec(memory_space=pltpu.SMEM)
    vmem = pl.BlockSpec(memory_space=pltpu.VMEM)
    slots = kv.shape[0]
    return pl.pallas_call(
        functools.partial(cross_kernel, slots),
        out_shape=jax.ShapeDtypeStruct((QTAIL, 2, 640), jnp.bfloat16),
        in_specs=[smem, smem, smem, vmem, vmem],
        out_specs=vmem,
        compiler_params=params(),
        name="cross_attention",
    )(first, span_ids, seg_lengths, q, kv)


def merge_kernel(part_ref, o_ref):
    for b in range(GROUP // 2):
        level = jnp.sum(part_ref[:, :, 512 + 3 * b:515 + 3 * b].astype(jnp.float32), axis=-1, keepdims=True)
        weight = jnp.exp(level - jnp.max(level, axis=0, keepdims=True))
        average = part_ref[:, :, HEAD * b:HEAD * (b + 1)].astype(jnp.float32)
        o_ref[2 * b:2 * b + 2] = jnp.sum(average * weight, axis=0) / jnp.sum(weight, axis=0)


def merge(parts):
    vmem = pl.BlockSpec(memory_space=pltpu.VMEM)
    return pl.pallas_call(
        merge_kernel,
        out_shape=jax.ShapeDtypeStruct((GROUP, HEAD), jnp.float32),
        in_specs=[vmem],
        out_specs=vmem,
        name="merge_partials",
    )(parts)


def spread(block, axes):
    count = lax.axis_size(axes)
    copies = jnp.broadcast_to(block[None], (count,) + block.shape)
    return lax.all_to_all(copies, axes, 0, 0, tiled=True)


def local(enc_query, enc_key, enc_value, enc_resid, out_weight, norm_gain, kv_weight, cross_query,
          span_ids, seg_lengths):
    ha = lax.axis_index(HA)
    sa = lax.axis_index(SA)
    sa_count = lax.axis_size(SA)
    core = lax.axis_index("c")

    swap = functools.partial(lax.ppermute, axis_name="c", perm=[(0, 1), (1, 0)])

    yl = lax.axis_index("yl")

    with jax.named_scope("gather_weights"):
        over_z = spread(lax.dynamic_slice_in_dim(out_weight, ha * HEAD, HEAD, 1), "z")
        own = kv_weight.reshape(D_ENC, 2 * HEAD)
        first = lax.dynamic_slice_in_dim(own, core * 256 + yl * 128, 128, 0)
        last = lax.dynamic_slice_in_dim(own, 512 + core * 256, 256, 0)
        kv_mine = lax.all_gather(last, HA)
        block = jnp.concatenate([over_z.reshape(256, HEAD), first[:, :HEAD], first[:, HEAD:]], axis=0)
        mine = spread(block, PLANE)
        kv_mine, mine, enc_query = lax.optimization_barrier((kv_mine, mine, enc_query))
        other = swap(mine)
        kv_other = swap(kv_mine)

    slot = (ha * sa_count + sa).reshape(1).astype(jnp.int32)
    context = encoder_attention(slot, span_ids, seg_lengths, enc_query, enc_key, enc_value)
    keyval = encode(core.reshape(1).astype(jnp.int32), context, mine, other, enc_resid,
                    norm_gain.reshape(1, D_ENC), kv_mine, kv_other)
    with jax.named_scope("exchange_keyval"):
        keyval = lax.all_to_all(keyval, HA, 0, 0, tiled=True)
    first = jnp.stack([sa, sa_count]).astype(jnp.int32)
    query = cross_query.reshape(QTAIL, GROUP, HEAD).transpose(1, 0, 2).reshape(GROUP * QTAIL, HEAD)
    parts = cross_attention(first, span_ids, seg_lengths, query, keyval)
    with jax.named_scope("exchange_partials"):
        parts = lax.all_to_all(parts, SA, 0, 0, tiled=True)
    return merge(parts).reshape(1, 1, GROUP * HEAD)


def solution(mesh):
    fine = Mesh(mesh.devices.reshape(2, 4, 16, 2, 2), PARTS)
    rows = P(PARTS, None)
    heads = P(None, HA, None)
    placed = (rows, rows, rows, rows, P(SA, None), P(), heads, heads, P(), P())
    return jax.shard_map(
        local, mesh=fine, in_specs=placed, out_specs=P(SA, HA, None), check_vma=False
    )
```

```python
import functools
import math

import jax
import jax.numpy as jnp
import numpy as np
from jax import lax
from jax.experimental import pallas as pl
from jax.experimental.pallas import tpu as pltpu
from jax.sharding import Mesh, PartitionSpec as P

D_ENC = 1024
ENC_HEADS = 16
ENC_HEAD = D_ENC // ENC_HEADS
KV_HEADS = 8
GROUP = 8
HEAD = 128
SEG_LEN = 256
QTAIL = 64
MASKED = -1e30

PARTS = ("yh", "x", "z", "yl", "c")
HA = ("yh", "x")
SA = ("z", "yl", "c")
PLANE = ("yh", "x", "yl")


def params(**kw):
    return pltpu.CompilerParams(vmem_limit_bytes=48 * 1024 * 1024, **kw)


def dot(a, b):
    return jnp.dot(a, b, preferred_element_type=jnp.float32)


def dot_t(a, b):
    return lax.dot_general(a, b, (((1,), (1,)), ((), ())), preferred_element_type=jnp.float32)


def encoder_attention_kernel(slot_ref, span_ref, len_ref, q_ref, k_ref, v_ref, o_ref):
    valid = len_ref[span_ref[slot_ref[0]]]
    keep = lax.broadcasted_iota(jnp.int32, (1, SEG_LEN), 1) < valid
    bias = jnp.where(keep, 0.0, MASKED).astype(jnp.float32)
    low = lax.broadcasted_iota(jnp.int32, (SEG_LEN, 2 * ENC_HEAD), 1) < ENC_HEAD
    for pair in range(ENC_HEADS // 2):
        cols = slice(pair * 2 * ENC_HEAD, (pair + 1) * 2 * ENC_HEAD)
        q, k, v = q_ref[:, cols], k_ref[:, cols], v_ref[:, cols]
        zero = jnp.zeros_like(k)
        parts = []
        for mine in (low, jnp.logical_not(low)):
            scores = dot_t(q, jnp.where(mine, k, zero)) * (1.0 / math.sqrt(ENC_HEAD)) + bias
            expo = jnp.exp(scores - jnp.max(scores, axis=-1, keepdims=True))
            probs = (expo * (1.0 / jnp.sum(expo, axis=-1, keepdims=True))).astype(jnp.bfloat16)
            parts.append(dot(probs, v))
        o_ref[:, cols] = jnp.where(low, parts[0], parts[1]).astype(jnp.bfloat16)


def encoder_attention(slot, span_ids, seg_lengths, q, k, v):
    smem = pl.BlockSpec(memory_space=pltpu.SMEM)
    vmem = pl.BlockSpec(memory_space=pltpu.VMEM)
    return pl.pallas_call(
        encoder_attention_kernel,
        out_shape=jax.ShapeDtypeStruct((SEG_LEN, D_ENC), jnp.bfloat16),
        in_specs=[smem, smem, smem, vmem, vmem, vmem],
        out_specs=vmem,
        compiler_params=params(),
        cost_estimate=pl.CostEstimate(
            flops=8 * SEG_LEN * SEG_LEN * D_ENC, bytes_accessed=8 * SEG_LEN * D_ENC,
            transcendentals=SEG_LEN * SEG_LEN * ENC_HEADS),
        name="encoder_attention",
    )(slot, span_ids, seg_lengths, q, k, v)


def encode_kernel(place_ref, ctx_ref, mine_ref, other_ref, resid_ref, gain_ref, kv_mine_ref,
                  kv_other_ref, o_ref, w_ref, enc_ref):
    z, core = place_ref[0], place_ref[1]
    for part_ref, at in ((mine_ref, core), (other_ref, 1 - core)):
        for ha in range(KV_HEADS):
            plane = lax.rem(z + 32 - 2 * ha - at, 16)
            for yl in range(2):
                w_ref[pl.ds(pl.multiple_of(64 * plane + 32 * yl, 32), 32), :] = part_ref[ha * 2 + yl]
    hidden = resid_ref[...].astype(jnp.float32) + dot(ctx_ref[...], w_ref[...])
    factor = lax.rsqrt(jnp.mean(hidden * hidden, axis=-1, keepdims=True) + 1e-05)
    encoded = (hidden * factor * gain_ref[...]).astype(jnp.bfloat16)
    half = D_ENC // 2
    enc_ref[0] = encoded[:, :half]
    enc_ref[1] = encoded[:, half:]
    near, far = enc_ref[core], enc_ref[1 - core]
    for h in range(KV_HEADS):
        o_ref[h] = (dot(near, kv_mine_ref[h]) + dot(far, kv_other_ref[h])).astype(jnp.bfloat16)


def encode(place, ctx, mine, other, resid, gain, kv_mine, kv_other):
    smem = pl.BlockSpec(memory_space=pltpu.SMEM)
    vmem = pl.BlockSpec(memory_space=pltpu.VMEM)
    return pl.pallas_call(
        encode_kernel,
        out_shape=jax.ShapeDtypeStruct((KV_HEADS, SEG_LEN, 2 * HEAD), jnp.bfloat16),
        in_specs=[smem] + [vmem] * 7,
        out_specs=vmem,
        scratch_shapes=[pltpu.VMEM((D_ENC, D_ENC), jnp.bfloat16),
                        pltpu.VMEM((2, SEG_LEN, D_ENC // 2), jnp.bfloat16)],
        compiler_params=params(),
        cost_estimate=pl.CostEstimate(
            flops=6 * SEG_LEN * D_ENC * D_ENC, bytes_accessed=8 * D_ENC * D_ENC, transcendentals=SEG_LEN),
        name="encode_keyval",
    )(place, ctx, mine, other, resid, gain, kv_mine, kv_other)


def cross_kernel(slots, first_ref, span_ref, len_ref, q_ref, kv_ref, o_ref):
    scale = 1.0 / math.sqrt(HEAD)
    lane = lax.broadcasted_iota(jnp.int32, (1, SEG_LEN), 1)
    bias = []
    for s in range(slots):
        valid = len_ref[span_ref[first_ref[0] + s * first_ref[1]]]
        bias.append(jnp.where(lane < valid, 0.0, MASKED).astype(jnp.float32))
    bias = jnp.concatenate(bias, axis=1)
    keys = kv_ref[:, :, :HEAD].reshape(slots * SEG_LEN, HEAD)
    values = kv_ref[:, :, HEAD:].reshape(slots * SEG_LEN, HEAD)
    rows = 2 * QTAIL
    column = lax.broadcasted_iota(jnp.int32, (rows, HEAD), 1)
    levels = jnp.zeros((rows, HEAD), jnp.float32)

    def put(at, block):
        block = block.reshape(2, QTAIL, HEAD)
        o_ref[:, :, at * HEAD:(at + 1) * HEAD] = jnp.stack([block[0], block[1]], axis=1).astype(jnp.bfloat16)

    for b in range(GROUP // 2):
        q = q_ref[b * rows:(b + 1) * rows]
        scores = dot_t(q, keys) + bias
        top = jnp.max(scores, axis=-1, keepdims=True)
        expo = jnp.exp((scores - top) * scale)
        total = jnp.sum(expo, axis=-1, keepdims=True)
        put(b, dot(expo.astype(jnp.bfloat16), values) / total)
        level = jnp.broadcast_to(top * scale + jnp.log(total), (rows, HEAD))
        high = level.astype(jnp.bfloat16).astype(jnp.float32)
        middle = (level - high).astype(jnp.bfloat16).astype(jnp.float32)
        rest = level - high - middle
        for k, part in enumerate((high, middle, rest)):
            levels = jnp.where(column == 3 * b + k, part, levels)
    put(GROUP // 2, levels)


def cross_attention(first, span_ids, seg_lengths, q, kv):
    smem = pl.BlockSpec(memory_space=pltpu.SMEM)
    vmem = pl.BlockSpec(memory_space=pltpu.VMEM)
    slots = kv.shape[0]
    return pl.pallas_call(
        functools.partial(cross_kernel, slots),
        out_shape=jax.ShapeDtypeStruct((QTAIL, 2, 640), jnp.bfloat16),
        in_specs=[smem, smem, smem, vmem, vmem],
        out_specs=vmem,
        compiler_params=params(),
        name="cross_attention",
    )(first, span_ids, seg_lengths, q, kv)


def merge_kernel(part_ref, o_ref):
    for b in range(GROUP // 2):
        level = jnp.sum(part_ref[:, :, 512 + 3 * b:515 + 3 * b].astype(jnp.float32), axis=-1, keepdims=True)
        weight = jnp.exp(level - jnp.max(level, axis=0, keepdims=True))
        average = part_ref[:, :, HEAD * b:HEAD * (b + 1)].astype(jnp.float32)
        o_ref[2 * b:2 * b + 2] = jnp.sum(average * weight, axis=0) / jnp.sum(weight, axis=0)


def merge(parts):
    vmem = pl.BlockSpec(memory_space=pltpu.VMEM)
    return pl.pallas_call(
        merge_kernel,
        out_shape=jax.ShapeDtypeStruct((GROUP, HEAD), jnp.float32),
        in_specs=[vmem],
        out_specs=vmem,
        name="merge_partials",
    )(parts)


def spread(block, axes):
    count = lax.axis_size(axes)
    copies = jnp.broadcast_to(block[None], (count,) + block.shape)
    return lax.all_to_all(copies, axes, 0, 0, tiled=True)


def local(enc_query, enc_key, enc_value, enc_resid, out_weight, norm_gain, kv_weight, cross_query,
          span_ids, seg_lengths):
    ha = lax.axis_index(HA)
    sa = lax.axis_index(SA)
    sa_count = lax.axis_size(SA)
    core = lax.axis_index("c")

    yl, z = lax.axis_index("yl"), lax.axis_index("z")
    swap = functools.partial(lax.ppermute, axis_name="c", perm=[(0, 1), (1, 0)])

    with jax.named_scope("gather_kv_weight"):
        quarter = lax.dynamic_slice_in_dim(
            kv_weight.reshape(D_ENC, 2 * HEAD), core * 512 + yl * 256, 256, 0)
        kv_mine = spread(quarter, PLANE)
    with jax.named_scope("out_weight_over_z"):
        pair = lax.all_gather(out_weight, "c", axis=0, tiled=True)
        hops = []
        for ha_at in range(8):
            for z_at in range(16):
                for c_at in range(2):
                    there = (z_at + 2 * ha_at + c_at) % 16
                    hops.append(((ha_at * 16 + z_at) * 2 + c_at, (ha_at * 16 + there) * 2 + c_at))
        pair = lax.ppermute(pair, ("yh", "x", "z", "c"), hops)
    kv_mine, pair, enc_query = lax.optimization_barrier((kv_mine, pair, enc_query))
    with jax.named_scope("out_weight_over_plane"):
        w_mine = spread(pair, PLANE)
    kv_mine = kv_mine.reshape(KV_HEADS, D_ENC // 2, 2 * HEAD)
    with jax.named_scope("swap_kv_weight"):
        kv_other = swap(kv_mine)
    slot = (ha * sa_count + sa).reshape(1).astype(jnp.int32)
    context = encoder_attention(slot, span_ids, seg_lengths, enc_query, enc_key, enc_value)
    w_mine, kv_other, context = lax.optimization_barrier((w_mine, kv_other, context))
    with jax.named_scope("swap_out_weight"):
        w_other = swap(w_mine)
    place = jnp.stack([z, core]).astype(jnp.int32)
    keyval = encode(place, context, w_mine, w_other, enc_resid, norm_gain.reshape(1, D_ENC),
                    kv_mine, kv_other)
    with jax.named_scope("exchange_keyval"):
        keyval = lax.all_to_all(keyval, HA, 0, 0, tiled=True)
    first = jnp.stack([sa, sa_count]).astype(jnp.int32)
    query = cross_query.reshape(QTAIL, GROUP, HEAD).transpose(1, 0, 2).reshape(GROUP * QTAIL, HEAD)
    parts = cross_attention(first, span_ids, seg_lengths, query, keyval)
    with jax.named_scope("exchange_partials"):
        parts = lax.all_to_all(parts, SA, 0, 0, tiled=True)
    return merge(parts).reshape(1, 1, GROUP * HEAD)


def solution(mesh):
    fine = Mesh(mesh.devices.reshape(2, 4, 16, 2, 2), PARTS)
    rows = P(PARTS, None)
    heads = P(None, HA, None)
    placed = (rows, rows, rows, rows, P(SA, None), P(), heads, heads, P(), P())
    return jax.shard_map(
        local, mesh=fine, in_specs=placed, out_specs=P(SA, HA, None), check_vma=False
    )
```

```python
import functools
import math

import jax
import jax.numpy as jnp
import numpy as np
from jax import lax
from jax.experimental import pallas as pl
from jax.experimental.pallas import tpu as pltpu
from jax.sharding import Mesh, PartitionSpec as P

D_ENC = 1024
ENC_HEADS = 16
ENC_HEAD = D_ENC // ENC_HEADS
KV_HEADS = 8
GROUP = 8
HEAD = 128
SEG_LEN = 256
QTAIL = 64
MASKED = -1e30

PARTS = ("yh", "x", "z", "yl", "c")
HA = ("yh", "x")
SA = ("z", "yl", "c")
PLANE = ("yh", "x", "yl")


def params(mebibytes=20):
    return pltpu.CompilerParams(vmem_limit_bytes=mebibytes * 1024 * 1024)


def dot(a, b):
    return jnp.dot(a, b, preferred_element_type=jnp.float32)


def dot_t(a, b):
    return lax.dot_general(a, b, (((1,), (1,)), ((), ())), preferred_element_type=jnp.float32)


def encoder_attention_kernel(slot_ref, span_ref, len_ref, q_ref, k_ref, v_ref, o_ref):
    valid = len_ref[span_ref[slot_ref[0]]]
    keep = lax.broadcasted_iota(jnp.int32, (1, SEG_LEN), 1) < valid
    bias = jnp.where(keep, 0.0, MASKED).astype(jnp.float32)
    low = lax.broadcasted_iota(jnp.int32, (SEG_LEN, 2 * ENC_HEAD), 1) < ENC_HEAD
    for pair in range(ENC_HEADS // 2):
        cols = slice(pair * 2 * ENC_HEAD, (pair + 1) * 2 * ENC_HEAD)
        q, k, v = q_ref[:, cols], k_ref[:, cols], v_ref[:, cols]
        zero = jnp.zeros_like(k)
        parts = []
        for mine in (low, jnp.logical_not(low)):
            scores = dot_t(q, jnp.where(mine, k, zero)) * (1.0 / math.sqrt(ENC_HEAD)) + bias
            expo = jnp.exp(scores - jnp.max(scores, axis=-1, keepdims=True))
            probs = (expo * (1.0 / jnp.sum(expo, axis=-1, keepdims=True))).astype(jnp.bfloat16)
            parts.append(dot(probs, v))
        o_ref[:, cols] = jnp.where(low, parts[0], parts[1]).astype(jnp.bfloat16)


def encoder_attention(slot, span_ids, seg_lengths, q, k, v):
    smem = pl.BlockSpec(memory_space=pltpu.SMEM)
    vmem = pl.BlockSpec(memory_space=pltpu.VMEM)
    return pl.pallas_call(
        encoder_attention_kernel,
        out_shape=jax.ShapeDtypeStruct((SEG_LEN, D_ENC), jnp.bfloat16),
        in_specs=[smem, smem, smem, vmem, vmem, vmem],
        out_specs=vmem,
        compiler_params=params(),
        cost_estimate=pl.CostEstimate(
            flops=8 * SEG_LEN * SEG_LEN * D_ENC, bytes_accessed=8 * SEG_LEN * D_ENC,
            transcendentals=SEG_LEN * SEG_LEN * ENC_HEADS),
        name="encoder_attention",
    )(slot, span_ids, seg_lengths, q, k, v)


def encode_kernel(place_ref, gain_ref, ctx_ref, resid_ref, mine_ref, other_ref, *refs):
    kv_refs, o_ref = refs[:6], refs[6]
    w_ref, enc_ref, done_ref, hold_ref = refs[7:11]
    kv_bufs, w_sems, kv_sems, o_sems = refs[11:17], refs[17], refs[18], refs[19]
    z, core, odd = place_ref[0], place_ref[1], place_ref[2]

    copies = []
    for which, part_ref, at in ((0, mine_ref, core), (1, other_ref, 1 - core)):
        for ha in range(KV_HEADS):
            plane = lax.rem(z + 32 - 2 * ha - at, 16)
            for yl in range(2):
                for c in range(2):
                    row = pl.multiple_of(64 * plane + 32 * yl + 16 * c, 16)
                    copies.append(pltpu.make_async_copy(
                        part_ref.at[ha * 2 + yl, c], w_ref.at[:, pl.ds(row, 16)], w_sems.at[len(copies)]))
    copies.append(pltpu.make_async_copy(ctx_ref, hold_ref.at[0], w_sems.at[64]))
    copies.append(pltpu.make_async_copy(resid_ref, hold_ref.at[1], w_sems.at[65]))
    kv_copies = [pltpu.make_async_copy(kv_refs[i], kv_bufs[i], kv_sems.at[i]) for i in range(6)]
    for copy in copies + kv_copies:
        copy.start()
    for copy in copies:
        copy.wait()

    ctx = hold_ref[0]
    hidden = jnp.concatenate(
        [dot(ctx, jnp.concatenate([w_ref[2 * j], w_ref[2 * j + 1]], axis=1)) for j in range(4)], axis=1)
    hidden = hidden + hold_ref[1].astype(jnp.float32)
    factor = lax.rsqrt(jnp.mean(hidden * hidden, axis=-1, keepdims=True) + 1e-05)
    encoded = (hidden * factor * gain_ref[...]).astype(jnp.bfloat16)
    for piece in range(4):
        enc_ref[piece] = encoded[:, piece * 256:(piece + 1) * 256]
    near, far = 2 * core, 2 - 2 * core
    pieces = [enc_ref[near + odd], enc_ref[near + 1 - odd], enc_ref[far + odd], enc_ref[far + 1 - odd]]
    for copy in kv_copies:
        copy.wait()

    def rows(buf, h):
        return jnp.concatenate(
            [jnp.concatenate([buf[2 * h + yl, :128], buf[2 * h + yl, 128:]], axis=1) for yl in range(2)], axis=0)

    out_copies = []
    for h in range(KV_HEADS):
        side, at = divmod(h, KV_HEADS // 2)
        total = dot(pieces[0], rows(kv_bufs[0], h)) + dot(pieces[1], rows(kv_bufs[1 + side], at))
        total += dot(pieces[2], rows(kv_bufs[3], h)) + dot(pieces[3], rows(kv_bufs[4 + side], at))
        done_ref[h, :SEG_LEN] = total[:, :HEAD].astype(jnp.bfloat16)
        done_ref[h, SEG_LEN:] = total[:, HEAD:].astype(jnp.bfloat16)
        out_copies.append(pltpu.make_async_copy(done_ref.at[h], o_ref.at[h], o_sems.at[h]))
        out_copies[h].start()
    for copy in out_copies:
        copy.wait()


def encode(place, gain, ctx, resid, mine, other, kvs):
    smem = pl.BlockSpec(memory_space=pltpu.SMEM)
    vmem = pl.BlockSpec(memory_space=pltpu.VMEM)
    hbm = pl.BlockSpec(memory_space=pltpu.HBM)
    return pl.pallas_call(
        encode_kernel,
        out_shape=jax.ShapeDtypeStruct((KV_HEADS, 2 * SEG_LEN, HEAD), jnp.bfloat16),
        in_specs=[smem, vmem] + [hbm] * 10,
        out_specs=hbm,
        scratch_shapes=[pltpu.VMEM((8, D_ENC, HEAD), jnp.bfloat16),
                        pltpu.VMEM((4, SEG_LEN, 256), jnp.bfloat16),
                        pltpu.VMEM((KV_HEADS, 2 * SEG_LEN, HEAD), jnp.bfloat16),
                        pltpu.VMEM((2, SEG_LEN, D_ENC), jnp.bfloat16)]
        + [pltpu.VMEM(kv.shape, kv.dtype) for kv in kvs]
        + [pltpu.SemaphoreType.DMA((66,)), pltpu.SemaphoreType.DMA((6,)), pltpu.SemaphoreType.DMA((KV_HEADS,))],
        compiler_params=params(47),
        cost_estimate=pl.CostEstimate(
            flops=6 * SEG_LEN * D_ENC * D_ENC, bytes_accessed=8 * D_ENC * D_ENC, transcendentals=SEG_LEN),
        name="encode_keyval",
    )(place, gain, ctx, resid, mine, other, *kvs)


def cross_kernel(slots, first_ref, span_ref, len_ref, q_ref, kv_ref, o_ref):
    scale = 1.0 / math.sqrt(HEAD)
    lane = lax.broadcasted_iota(jnp.int32, (1, SEG_LEN), 1)
    bias = []
    for s in range(slots):
        valid = len_ref[span_ref[first_ref[0] + s * first_ref[1]]]
        bias.append(jnp.where(lane < valid, 0.0, MASKED).astype(jnp.float32))
    bias = jnp.concatenate(bias, axis=1)
    keys = kv_ref[:, :SEG_LEN].reshape(slots * SEG_LEN, HEAD)
    values = kv_ref[:, SEG_LEN:].reshape(slots * SEG_LEN, HEAD)
    rows = 2 * QTAIL
    column = lax.broadcasted_iota(jnp.int32, (rows, HEAD), 1)
    levels = jnp.zeros((rows, HEAD), jnp.float32)

    def put(at, block):
        block = block.reshape(2, QTAIL, HEAD)
        o_ref[:, :, at * HEAD:(at + 1) * HEAD] = jnp.stack([block[0], block[1]], axis=1).astype(jnp.bfloat16)

    for b in range(GROUP // 2):
        q = q_ref[b * rows:(b + 1) * rows]
        scores = dot_t(q, keys) + bias
        top = jnp.max(scores, axis=-1, keepdims=True)
        expo = jnp.exp((scores - top) * scale)
        total = jnp.sum(expo, axis=-1, keepdims=True)
        put(b, dot(expo.astype(jnp.bfloat16), values) / total)
        level = jnp.broadcast_to(top * scale + jnp.log(total), (rows, HEAD))
        high = level.astype(jnp.bfloat16).astype(jnp.float32)
        middle = (level - high).astype(jnp.bfloat16).astype(jnp.float32)
        rest = level - high - middle
        for k, part in enumerate((high, middle, rest)):
            levels = jnp.where(column == 3 * b + k, part, levels)
    put(GROUP // 2, levels)


def cross_attention(first, span_ids, seg_lengths, q, kv):
    smem = pl.BlockSpec(memory_space=pltpu.SMEM)
    vmem = pl.BlockSpec(memory_space=pltpu.VMEM)
    slots = kv.shape[0]
    return pl.pallas_call(
        functools.partial(cross_kernel, slots),
        out_shape=jax.ShapeDtypeStruct((QTAIL, 2, 640), jnp.bfloat16),
        in_specs=[smem, smem, smem, vmem, vmem],
        out_specs=vmem,
        compiler_params=params(),
        name="cross_attention",
    )(first, span_ids, seg_lengths, q, kv)


def merge_kernel(part_ref, o_ref):
    for b in range(GROUP // 2):
        level = jnp.sum(part_ref[:, :, 512 + 3 * b:515 + 3 * b].astype(jnp.float32), axis=-1, keepdims=True)
        weight = jnp.exp(level - jnp.max(level, axis=0, keepdims=True))
        average = part_ref[:, :, HEAD * b:HEAD * (b + 1)].astype(jnp.float32)
        o_ref[2 * b:2 * b + 2] = jnp.sum(average * weight, axis=0) / jnp.sum(weight, axis=0)


def merge(parts):
    vmem = pl.BlockSpec(memory_space=pltpu.VMEM)
    return pl.pallas_call(
        merge_kernel,
        out_shape=jax.ShapeDtypeStruct((GROUP, HEAD), jnp.float32),
        in_specs=[vmem],
        out_specs=vmem,
        name="merge_partials",
    )(parts)


def spread(block, axes):
    count = lax.axis_size(axes)
    copies = jnp.broadcast_to(block[None], (count,) + block.shape)
    return lax.all_to_all(copies, axes, 0, 0, tiled=True)


def local(enc_query, enc_key, enc_value, enc_resid, out_weight, norm_gain, kv_weight, cross_query,
          span_ids, seg_lengths):
    ha = lax.axis_index(HA)
    sa = lax.axis_index(SA)
    sa_count = lax.axis_size(SA)
    core = lax.axis_index("c")

    yl, z = lax.axis_index("yl"), lax.axis_index("z")
    swap = functools.partial(lax.ppermute, axis_name="c", perm=[(0, 1), (1, 0)])

    odd = lax.rem(z, 2)

    with jax.named_scope("gather_kv_weight"):
        eighth = lax.dynamic_slice_in_dim(
            kv_weight.reshape(D_ENC, 2 * HEAD), core * 512 + odd * 256 + yl * 128, 128, 0)
        kv_mine = spread(jnp.concatenate([eighth[:, :HEAD], eighth[:, HEAD:]], axis=0), PLANE)
    with jax.named_scope("out_weight_over_z"):
        pair = lax.all_gather(out_weight.reshape(16, 8, HEAD).transpose(1, 0, 2), "c")
        hops = []
        for ha_at in range(8):
            for z_at in range(16):
                for c_at in range(2):
                    there = (z_at + 2 * ha_at + c_at) % 16
                    hops.append(((ha_at * 16 + z_at) * 2 + c_at, (ha_at * 16 + there) * 2 + c_at))
        pair = lax.ppermute(pair, ("yh", "x", "z", "c"), hops)
    kv_mine, pair, enc_query = lax.optimization_barrier((kv_mine, pair, enc_query))
    with jax.named_scope("out_weight_over_plane"):
        w_mine = spread(pair, PLANE)
    with jax.named_scope("kv_weight_over_z"):
        some = 8
        up = [(i, (i + 1) % 16) for i in range(16)]
        down = [(i, (i + 15) % 16) for i in range(16)]
        kv_first = lax.ppermute(kv_mine[:some], "z", down)
        kv_last = lax.ppermute(kv_mine[some:], "z", up)
    with jax.named_scope("swap_kv_weight"):
        kvs = [kv_mine, kv_first, kv_last]
        kvs = kvs + [swap(kv) for kv in kvs]
    slot = (ha * sa_count + sa).reshape(1).astype(jnp.int32)
    context = encoder_attention(slot, span_ids, seg_lengths, enc_query, enc_key, enc_value)
    w_mine, kvs, context = lax.optimization_barrier((w_mine, kvs, context))
    with jax.named_scope("swap_out_weight"):
        w_other = swap(w_mine)
    place = jnp.stack([z, core, odd]).astype(jnp.int32)
    keyval = encode(place, norm_gain.reshape(1, D_ENC), context, enc_resid, w_mine, w_other, kvs)
    with jax.named_scope("exchange_keyval"):
        keyval = lax.all_to_all(keyval, HA, 0, 0, tiled=True)
    first = jnp.stack([sa, sa_count]).astype(jnp.int32)
    query = cross_query.reshape(QTAIL, GROUP, HEAD).transpose(1, 0, 2).reshape(GROUP * QTAIL, HEAD)
    parts = cross_attention(first, span_ids, seg_lengths, query, keyval)
    with jax.named_scope("exchange_partials"):
        parts = lax.all_to_all(parts, SA, 0, 0, tiled=True)
    return merge(parts).reshape(1, 1, GROUP * HEAD)


def solution(mesh):
    fine = Mesh(mesh.devices.reshape(2, 4, 16, 2, 2), PARTS)
    rows = P(PARTS, None)
    heads = P(None, HA, None)
    placed = (rows, rows, rows, rows, P(SA, None), P(), heads, heads, P(), P())
    return jax.shard_map(
        local, mesh=fine, in_specs=placed, out_specs=P(SA, HA, None), check_vma=False
    )
```

```python
import functools
import math

import jax
import jax.numpy as jnp
import numpy as np
from jax import lax
from jax.experimental import pallas as pl
from jax.experimental.pallas import tpu as pltpu
from jax.sharding import Mesh, PartitionSpec as P

D_ENC = 1024
ENC_HEADS = 16
ENC_HEAD = D_ENC // ENC_HEADS
KV_HEADS = 8
GROUP = 8
HEAD = 128
SEG_LEN = 256
QTAIL = 64
MASKED = -1e30

PARTS = ("yh", "x", "z", "yl", "c")
HA = ("yh", "x")
SA = ("z", "yl", "c")
PLANE = ("yh", "x", "yl")


def params(mebibytes=20):
    return pltpu.CompilerParams(vmem_limit_bytes=mebibytes * 1024 * 1024)


def dot(a, b):
    return jnp.dot(a, b, preferred_element_type=jnp.float32)


def dot_t(a, b):
    return lax.dot_general(a, b, (((1,), (1,)), ((), ())), preferred_element_type=jnp.float32)


def encoder_attention_kernel(slot_ref, span_ref, len_ref, q_ref, k_ref, v_ref, resid_ref, o_ref):
    o_ref[1] = resid_ref[...]
    valid = len_ref[span_ref[slot_ref[0]]]
    keep = lax.broadcasted_iota(jnp.int32, (1, SEG_LEN), 1) < valid
    bias = jnp.where(keep, 0.0, MASKED).astype(jnp.float32)
    low = lax.broadcasted_iota(jnp.int32, (SEG_LEN, 2 * ENC_HEAD), 1) < ENC_HEAD
    for pair in range(ENC_HEADS // 2):
        cols = slice(pair * 2 * ENC_HEAD, (pair + 1) * 2 * ENC_HEAD)
        q, k, v = q_ref[:, cols], k_ref[:, cols], v_ref[:, cols]
        zero = jnp.zeros_like(k)
        parts = []
        for mine in (low, jnp.logical_not(low)):
            scores = dot_t(q, jnp.where(mine, k, zero)) * (1.0 / math.sqrt(ENC_HEAD)) + bias
            expo = jnp.exp(scores - jnp.max(scores, axis=-1, keepdims=True))
            probs = (expo * (1.0 / jnp.sum(expo, axis=-1, keepdims=True))).astype(jnp.bfloat16)
            parts.append(dot(probs, v))
        o_ref[0, :, cols] = jnp.where(low, parts[0], parts[1]).astype(jnp.bfloat16)


def encoder_attention(slot, span_ids, seg_lengths, q, k, v, resid):
    smem = pl.BlockSpec(memory_space=pltpu.SMEM)
    vmem = pl.BlockSpec(memory_space=pltpu.VMEM)
    return pl.pallas_call(
        encoder_attention_kernel,
        out_shape=jax.ShapeDtypeStruct((2, SEG_LEN, D_ENC), jnp.bfloat16),
        in_specs=[smem, smem, smem, vmem, vmem, vmem, vmem],
        out_specs=vmem,
        compiler_params=params(),
        cost_estimate=pl.CostEstimate(
            flops=8 * SEG_LEN * SEG_LEN * D_ENC, bytes_accessed=8 * SEG_LEN * D_ENC,
            transcendentals=SEG_LEN * SEG_LEN * ENC_HEADS),
        name="encoder_attention",
    )(slot, span_ids, seg_lengths, q, k, v, resid)


def project_kernel(place_ref, gain_ref, ctx_ref, mine_ref, other_ref, o_ref, w_ref):
    z, core = place_ref[0], place_ref[1]
    for part_ref, at in ((mine_ref, core), (other_ref, 1 - core)):
        for ha in range(KV_HEADS):
            plane = lax.rem(z + 32 - 2 * ha - at, 16)
            for yl in range(2):
                for c in range(2):
                    row = pl.multiple_of(64 * plane + 32 * yl + 16 * c, 16)
                    w_ref[:, pl.ds(row, 16), :] = part_ref[ha * 2 + yl, c]
    ctx = ctx_ref[0]
    hidden = jnp.concatenate(
        [dot(ctx, jnp.concatenate([w_ref[2 * j], w_ref[2 * j + 1]], axis=1)) for j in range(4)], axis=1)
    hidden = hidden + ctx_ref[1].astype(jnp.float32)
    factor = lax.rsqrt(jnp.mean(hidden * hidden, axis=-1, keepdims=True) + 1e-05)
    encoded = (hidden * factor * gain_ref[...]).astype(jnp.bfloat16)
    for piece in range(4):
        o_ref[piece] = encoded[:, piece * 256:(piece + 1) * 256]


def project(place, gain, ctx, mine, other):
    smem = pl.BlockSpec(memory_space=pltpu.SMEM)
    vmem = pl.BlockSpec(memory_space=pltpu.VMEM)
    return pl.pallas_call(
        project_kernel,
        out_shape=jax.ShapeDtypeStruct((4, SEG_LEN, 256), jnp.bfloat16),
        in_specs=[smem] + [vmem] * 4,
        out_specs=vmem,
        scratch_shapes=[pltpu.VMEM((8, D_ENC, HEAD), jnp.bfloat16)],
        compiler_params=params(),
        cost_estimate=pl.CostEstimate(
            flops=2 * SEG_LEN * D_ENC * D_ENC, bytes_accessed=6 * D_ENC * D_ENC, transcendentals=SEG_LEN),
        name="project",
    )(place, gain, ctx, mine, other)


def keyval_kernel(place_ref, enc_ref, *refs):
    kv_refs, o_ref = refs[:8], refs[-1]
    core, odd = place_ref[1], place_ref[2]
    near, far = 2 * core, 2 - 2 * core
    pieces = [enc_ref[near + odd], enc_ref[near + 1 - odd], enc_ref[far + odd], enc_ref[far + 1 - odd]]

    def rows(ref, h):
        return jnp.concatenate(
            [jnp.concatenate([ref[2 * h + yl, :128], ref[2 * h + yl, 128:]], axis=1) for yl in range(2)], axis=0)

    for h in range(KV_HEADS):
        side, at = divmod(h, KV_HEADS // 2)
        total = dot(pieces[0], rows(kv_refs[side], at)) + dot(pieces[1], rows(kv_refs[2 + side], at))
        total += dot(pieces[2], rows(kv_refs[4 + side], at)) + dot(pieces[3], rows(kv_refs[6 + side], at))
        o_ref[h, :SEG_LEN] = total[:, :HEAD].astype(jnp.bfloat16)
        o_ref[h, SEG_LEN:] = total[:, HEAD:].astype(jnp.bfloat16)


def keys_and_values(place, encoded, kvs):
    smem = pl.BlockSpec(memory_space=pltpu.SMEM)
    vmem = pl.BlockSpec(memory_space=pltpu.VMEM)
    return pl.pallas_call(
        keyval_kernel,
        out_shape=jax.ShapeDtypeStruct((KV_HEADS, 2 * SEG_LEN, HEAD), jnp.bfloat16),
        in_specs=[smem] + [vmem] * 9,
        out_specs=vmem,
        compiler_params=params(),
        cost_estimate=pl.CostEstimate(
            flops=4 * SEG_LEN * D_ENC * D_ENC, bytes_accessed=5 * D_ENC * D_ENC, transcendentals=0),
        name="keys_and_values",
    )(place, encoded, *kvs)


def cross_kernel(slots, first_ref, span_ref, len_ref, q_ref, kv_ref, o_ref):
    scale = 1.0 / math.sqrt(HEAD)
    lane = lax.broadcasted_iota(jnp.int32, (1, SEG_LEN), 1)
    bias = []
    for s in range(slots):
        valid = len_ref[span_ref[first_ref[0] + s * first_ref[1]]]
        bias.append(jnp.where(lane < valid, 0.0, MASKED).astype(jnp.float32))
    bias = jnp.concatenate(bias, axis=1)
    keys = kv_ref[:, :SEG_LEN].reshape(slots * SEG_LEN, HEAD)
    values = kv_ref[:, SEG_LEN:].reshape(slots * SEG_LEN, HEAD)
    rows = 2 * QTAIL
    column = lax.broadcasted_iota(jnp.int32, (rows, HEAD), 1)
    levels = jnp.zeros((rows, HEAD), jnp.float32)

    def put(at, block):
        block = block.reshape(2, QTAIL, HEAD)
        o_ref[:, :, at * HEAD:(at + 1) * HEAD] = jnp.stack([block[0], block[1]], axis=1).astype(jnp.bfloat16)

    for b in range(GROUP // 2):
        q = q_ref[b * rows:(b + 1) * rows]
        scores = dot_t(q, keys) + bias
        top = jnp.max(scores, axis=-1, keepdims=True)
        expo = jnp.exp((scores - top) * scale)
        total = jnp.sum(expo, axis=-1, keepdims=True)
        put(b, dot(expo.astype(jnp.bfloat16), values) / total)
        level = jnp.broadcast_to(top * scale + jnp.log(total), (rows, HEAD))
        high = level.astype(jnp.bfloat16).astype(jnp.float32)
        middle = (level - high).astype(jnp.bfloat16).astype(jnp.float32)
        rest = level - high - middle
        for k, part in enumerate((high, middle, rest)):
            levels = jnp.where(column == 3 * b + k, part, levels)
    put(GROUP // 2, levels)


def cross_attention(first, span_ids, seg_lengths, q, kv):
    smem = pl.BlockSpec(memory_space=pltpu.SMEM)
    vmem = pl.BlockSpec(memory_space=pltpu.VMEM)
    slots = kv.shape[0]
    return pl.pallas_call(
        functools.partial(cross_kernel, slots),
        out_shape=jax.ShapeDtypeStruct((QTAIL, 2, 640), jnp.bfloat16),
        in_specs=[smem, smem, smem, vmem, vmem],
        out_specs=vmem,
        compiler_params=params(),
        name="cross_attention",
    )(first, span_ids, seg_lengths, q, kv)


def merge_kernel(part_ref, o_ref):
    for b in range(GROUP // 2):
        level = jnp.sum(part_ref[:, :, 512 + 3 * b:515 + 3 * b].astype(jnp.float32), axis=-1, keepdims=True)
        weight = jnp.exp(level - jnp.max(level, axis=0, keepdims=True))
        average = part_ref[:, :, HEAD * b:HEAD * (b + 1)].astype(jnp.float32)
        o_ref[2 * b:2 * b + 2] = jnp.sum(average * weight, axis=0) / jnp.sum(weight, axis=0)


def merge(parts):
    vmem = pl.BlockSpec(memory_space=pltpu.VMEM)
    return pl.pallas_call(
        merge_kernel,
        out_shape=jax.ShapeDtypeStruct((GROUP, HEAD), jnp.float32),
        in_specs=[vmem],
        out_specs=vmem,
        name="merge_partials",
    )(parts)


def spread(block, axes):
    count = lax.axis_size(axes)
    copies = jnp.broadcast_to(block[None], (count,) + block.shape)
    return lax.all_to_all(copies, axes, 0, 0, tiled=True)


def local(enc_query, enc_key, enc_value, enc_resid, out_weight, norm_gain, kv_weight, cross_query,
          span_ids, seg_lengths):
    ha = lax.axis_index(HA)
    sa = lax.axis_index(SA)
    sa_count = lax.axis_size(SA)
    core = lax.axis_index("c")

    yl, z = lax.axis_index("yl"), lax.axis_index("z")
    swap = functools.partial(lax.ppermute, axis_name="c", perm=[(0, 1), (1, 0)])

    odd = lax.rem(z, 2)

    with jax.named_scope("gather_kv_weight"):
        eighth = lax.dynamic_slice_in_dim(
            kv_weight.reshape(D_ENC, 2 * HEAD), core * 512 + odd * 256 + yl * 128, 128, 0)
        kv_mine = spread(jnp.concatenate([eighth[:, :HEAD], eighth[:, HEAD:]], axis=0), PLANE)
    with jax.named_scope("out_weight_over_z"):
        pair = lax.all_gather(out_weight.reshape(16, 8, HEAD).transpose(1, 0, 2), "c")
        hops = []
        for ha_at in range(8):
            for z_at in range(16):
                for c_at in range(2):
                    there = (z_at + 2 * ha_at + c_at) % 16
                    hops.append(((ha_at * 16 + z_at) * 2 + c_at, (ha_at * 16 + there) * 2 + c_at))
        pair = lax.ppermute(pair, ("yh", "x", "z", "c"), hops)
    slot = (ha * sa_count + sa).reshape(1).astype(jnp.int32)
    context = encoder_attention(slot, span_ids, seg_lengths, enc_query, enc_key, enc_value, enc_resid)
    kv_mine, pair, context = lax.optimization_barrier((kv_mine, pair, context))
    with jax.named_scope("out_weight_over_plane"):
        w_mine = spread(pair, PLANE)
    with jax.named_scope("kv_weight_over_z"):
        up = [(i, (i + 1) % 16) for i in range(16)]
        down = [(i, (i + 15) % 16) for i in range(16)]
        halves = kv_mine[:8], kv_mine[8:]
        near = list(halves) + [lax.ppermute(halves[0], "z", down), lax.ppermute(halves[1], "z", up)]
    with jax.named_scope("swap_weights"):
        far = [swap(half) for half in halves]
        w_mine, near, far = lax.optimization_barrier((w_mine, near, far))
        w_other = swap(w_mine)
        far = far + [swap(half) for half in near[2:]]
    place = jnp.stack([z, core, odd]).astype(jnp.int32)
    encoded = project(place, norm_gain.reshape(1, D_ENC), context, w_mine, w_other)
    keyval = keys_and_values(place, encoded, near + far)
    with jax.named_scope("exchange_keyval"):
        keyval = lax.all_to_all(keyval, HA, 0, 0, tiled=True)
    first = jnp.stack([sa, sa_count]).astype(jnp.int32)
    query = cross_query.reshape(QTAIL, GROUP, HEAD).transpose(1, 0, 2).reshape(GROUP * QTAIL, HEAD)
    parts = cross_attention(first, span_ids, seg_lengths, query, keyval)
    with jax.named_scope("exchange_partials"):
        parts = lax.all_to_all(parts, SA, 0, 0, tiled=True)
    return merge(parts).reshape(1, 1, GROUP * HEAD)


def solution(mesh):
    fine = Mesh(mesh.devices.reshape(2, 4, 16, 2, 2), PARTS)
    rows = P(PARTS, None)
    heads = P(None, HA, None)
    placed = (rows, rows, rows, rows, P(SA, None), P(), heads, heads, P(), P())
    return jax.shard_map(
        local, mesh=fine, in_specs=placed, out_specs=P(SA, HA, None), check_vma=False
    )
```

```python
import functools
import math

import jax
import jax.numpy as jnp
import numpy as np
from jax import lax
from jax.experimental import pallas as pl
from jax.experimental.pallas import tpu as pltpu
from jax.sharding import Mesh, PartitionSpec as P

D_ENC = 1024
ENC_HEADS = 16
ENC_HEAD = D_ENC // ENC_HEADS
KV_HEADS = 8
GROUP = 8
HEAD = 128
SEG_LEN = 256
QTAIL = 64
MASKED = -1e30

PARTS = ("yh", "x", "z", "yl", "c")
HA = ("yh", "x")
SA = ("z", "yl", "c")
PLANE = ("yh", "x", "yl")


def params(mebibytes=20):
    return pltpu.CompilerParams(vmem_limit_bytes=mebibytes * 1024 * 1024)


def dot(a, b):
    return jnp.dot(a, b, preferred_element_type=jnp.float32)


def dot_t(a, b):
    return lax.dot_general(a, b, (((1,), (1,)), ((), ())), preferred_element_type=jnp.float32)


def encoder_attention_kernel(slot_ref, span_ref, len_ref, q_ref, k_ref, v_ref, resid_ref, o_ref):
    o_ref[1] = resid_ref[...]
    valid = len_ref[span_ref[slot_ref[0]]]
    keep = lax.broadcasted_iota(jnp.int32, (1, SEG_LEN), 1) < valid
    bias = jnp.where(keep, 0.0, MASKED).astype(jnp.float32)
    low = lax.broadcasted_iota(jnp.int32, (SEG_LEN, 2 * ENC_HEAD), 1) < ENC_HEAD
    for pair in range(ENC_HEADS // 2):
        cols = slice(pair * 2 * ENC_HEAD, (pair + 1) * 2 * ENC_HEAD)
        q, k, v = q_ref[:, cols], k_ref[:, cols], v_ref[:, cols]
        zero = jnp.zeros_like(k)
        parts = []
        for mine in (low, jnp.logical_not(low)):
            scores = dot_t(q, jnp.where(mine, k, zero)) * (1.0 / math.sqrt(ENC_HEAD)) + bias
            expo = jnp.exp(scores - jnp.max(scores, axis=-1, keepdims=True))
            probs = (expo * (1.0 / jnp.sum(expo, axis=-1, keepdims=True))).astype(jnp.bfloat16)
            parts.append(dot(probs, v))
        o_ref[0, :, cols] = jnp.where(low, parts[0], parts[1]).astype(jnp.bfloat16)


def encoder_attention(slot, span_ids, seg_lengths, q, k, v, resid):
    smem = pl.BlockSpec(memory_space=pltpu.SMEM)
    vmem = pl.BlockSpec(memory_space=pltpu.VMEM)
    return pl.pallas_call(
        encoder_attention_kernel,
        out_shape=jax.ShapeDtypeStruct((2, SEG_LEN, D_ENC), jnp.bfloat16),
        in_specs=[smem, smem, smem, vmem, vmem, vmem, vmem],
        out_specs=vmem,
        compiler_params=params(),
        cost_estimate=pl.CostEstimate(
            flops=8 * SEG_LEN * SEG_LEN * D_ENC, bytes_accessed=8 * SEG_LEN * D_ENC,
            transcendentals=SEG_LEN * SEG_LEN * ENC_HEADS),
        name="encoder_attention",
    )(slot, span_ids, seg_lengths, q, k, v, resid)


def project_kernel(place_ref, gain_ref, ctx_ref, mine_ref, other_ref, o_ref, w_ref):
    z, core = place_ref[0], place_ref[1]
    for part_ref, at in ((mine_ref, core), (other_ref, 1 - core)):
        for ha in range(KV_HEADS):
            plane = lax.rem(z + 32 - 2 * ha - at, 16)
            for yl in range(2):
                for c in range(2):
                    row = pl.multiple_of(64 * plane + 32 * yl + 16 * c, 16)
                    w_ref[:, pl.ds(row, 16), :] = part_ref[ha * 2 + yl, c]
    ctx = ctx_ref[0]
    hidden = jnp.concatenate(
        [dot(ctx, jnp.concatenate([w_ref[2 * j], w_ref[2 * j + 1]], axis=1)) for j in range(4)], axis=1)
    hidden = hidden + ctx_ref[1].astype(jnp.float32)
    factor = lax.rsqrt(jnp.mean(hidden * hidden, axis=-1, keepdims=True) + 1e-05)
    encoded = (hidden * factor * gain_ref[...]).astype(jnp.bfloat16)
    for piece in range(4):
        o_ref[piece] = encoded[:, piece * 256:(piece + 1) * 256]


def project(place, gain, ctx, mine, other):
    smem = pl.BlockSpec(memory_space=pltpu.SMEM)
    vmem = pl.BlockSpec(memory_space=pltpu.VMEM)
    return pl.pallas_call(
        project_kernel,
        out_shape=jax.ShapeDtypeStruct((4, SEG_LEN, 256), jnp.bfloat16),
        in_specs=[smem] + [vmem] * 4,
        out_specs=vmem,
        scratch_shapes=[pltpu.VMEM((8, D_ENC, HEAD), jnp.bfloat16)],
        compiler_params=params(),
        cost_estimate=pl.CostEstimate(
            flops=2 * SEG_LEN * D_ENC * D_ENC, bytes_accessed=6 * D_ENC * D_ENC, transcendentals=SEG_LEN),
        name="project",
    )(place, gain, ctx, mine, other)


def keyval_kernel(place_ref, enc_ref, *refs):
    kv_refs, o_ref, kv_bufs, done_ref, in_sems, out_sems = refs[:8], refs[8], refs[9:17], refs[17], refs[18], refs[19]
    core, odd = place_ref[1], place_ref[2]
    copies = []
    for h in range(KV_HEADS):
        side, at = divmod(h, KV_HEADS // 2)
        copies.append([
            pltpu.make_async_copy(
                kv_refs[side + 2 * i].at[pl.ds(2 * at, 2)], kv_bufs[side + 2 * i].at[pl.ds(2 * at, 2)],
                in_sems.at[4 * h + i])
            for i in range(4)])
        for copy in copies[h]:
            copy.start()
    near, far = 2 * core, 2 - 2 * core
    pieces = [enc_ref[near + odd], enc_ref[near + 1 - odd], enc_ref[far + odd], enc_ref[far + 1 - odd]]

    def rows(ref, h):
        return jnp.concatenate(
            [jnp.concatenate([ref[2 * h + yl, :128], ref[2 * h + yl, 128:]], axis=1) for yl in range(2)], axis=0)

    sends = []
    for h in range(KV_HEADS):
        side, at = divmod(h, KV_HEADS // 2)
        total = 0.0
        for i in range(4):
            copies[h][i].wait()
            total += dot(pieces[i], rows(kv_bufs[side + 2 * i], at))
        done_ref[h, :SEG_LEN] = total[:, :HEAD].astype(jnp.bfloat16)
        done_ref[h, SEG_LEN:] = total[:, HEAD:].astype(jnp.bfloat16)
        sends.append(pltpu.make_async_copy(done_ref.at[h], o_ref.at[h], out_sems.at[h]))
        sends[h].start()
    for send in sends:
        send.wait()


def keys_and_values(place, encoded, kvs):
    smem = pl.BlockSpec(memory_space=pltpu.SMEM)
    vmem = pl.BlockSpec(memory_space=pltpu.VMEM)
    hbm = pl.BlockSpec(memory_space=pltpu.HBM)
    shape = jax.ShapeDtypeStruct((KV_HEADS, 2 * SEG_LEN, HEAD), jnp.bfloat16)
    return pl.pallas_call(
        keyval_kernel,
        out_shape=shape,
        in_specs=[smem, vmem] + [hbm] * 8,
        out_specs=hbm,
        scratch_shapes=[pltpu.VMEM(kv.shape, kv.dtype) for kv in kvs]
        + [pltpu.VMEM(shape.shape, shape.dtype), pltpu.SemaphoreType.DMA((4 * KV_HEADS,)),
           pltpu.SemaphoreType.DMA((KV_HEADS,))],
        compiler_params=params(47),
        cost_estimate=pl.CostEstimate(
            flops=4 * SEG_LEN * D_ENC * D_ENC, bytes_accessed=5 * D_ENC * D_ENC, transcendentals=0),
        name="keys_and_values",
    )(place, encoded, *kvs)


def cross_kernel(slots, first_ref, span_ref, len_ref, q_ref, kv_ref, o_ref):
    scale = 1.0 / math.sqrt(HEAD)
    lane = lax.broadcasted_iota(jnp.int32, (1, SEG_LEN), 1)
    bias = []
    for s in range(slots):
        valid = len_ref[span_ref[first_ref[0] + s * first_ref[1]]]
        bias.append(jnp.where(lane < valid, 0.0, MASKED).astype(jnp.float32))
    bias = jnp.concatenate(bias, axis=1)
    keys = kv_ref[:, :SEG_LEN].reshape(slots * SEG_LEN, HEAD)
    values = kv_ref[:, SEG_LEN:].reshape(slots * SEG_LEN, HEAD)
    rows = 2 * QTAIL
    column = lax.broadcasted_iota(jnp.int32, (rows, HEAD), 1)
    levels = jnp.zeros((rows, HEAD), jnp.float32)

    def put(at, block):
        block = block.reshape(2, QTAIL, HEAD)
        o_ref[:, :, at * HEAD:(at + 1) * HEAD] = jnp.stack([block[0], block[1]], axis=1).astype(jnp.bfloat16)

    for b in range(GROUP // 2):
        q = q_ref[b * rows:(b + 1) * rows]
        scores = dot_t(q, keys) + bias
        top = jnp.max(scores, axis=-1, keepdims=True)
        expo = jnp.exp((scores - top) * scale)
        total = jnp.sum(expo, axis=-1, keepdims=True)
        put(b, dot(expo.astype(jnp.bfloat16), values) / total)
        level = jnp.broadcast_to(top * scale + jnp.log(total), (rows, HEAD))
        high = level.astype(jnp.bfloat16).astype(jnp.float32)
        middle = (level - high).astype(jnp.bfloat16).astype(jnp.float32)
        rest = level - high - middle
        for k, part in enumerate((high, middle, rest)):
            levels = jnp.where(column == 3 * b + k, part, levels)
    put(GROUP // 2, levels)


def cross_attention(first, span_ids, seg_lengths, q, kv):
    smem = pl.BlockSpec(memory_space=pltpu.SMEM)
    vmem = pl.BlockSpec(memory_space=pltpu.VMEM)
    slots = kv.shape[0]
    return pl.pallas_call(
        functools.partial(cross_kernel, slots),
        out_shape=jax.ShapeDtypeStruct((QTAIL, 2, 640), jnp.bfloat16),
        in_specs=[smem, smem, smem, vmem, vmem],
        out_specs=vmem,
        compiler_params=params(),
        name="cross_attention",
    )(first, span_ids, seg_lengths, q, kv)


def merge_kernel(part_ref, o_ref):
    for b in range(GROUP // 2):
        level = jnp.sum(part_ref[:, :, 512 + 3 * b:515 + 3 * b].astype(jnp.float32), axis=-1, keepdims=True)
        weight = jnp.exp(level - jnp.max(level, axis=0, keepdims=True))
        average = part_ref[:, :, HEAD * b:HEAD * (b + 1)].astype(jnp.float32)
        o_ref[2 * b:2 * b + 2] = jnp.sum(average * weight, axis=0) / jnp.sum(weight, axis=0)


def merge(parts):
    vmem = pl.BlockSpec(memory_space=pltpu.VMEM)
    return pl.pallas_call(
        merge_kernel,
        out_shape=jax.ShapeDtypeStruct((GROUP, HEAD), jnp.float32),
        in_specs=[vmem],
        out_specs=vmem,
        name="merge_partials",
    )(parts)


def spread(block, axes):
    count = lax.axis_size(axes)
    copies = jnp.broadcast_to(block[None], (count,) + block.shape)
    return lax.all_to_all(copies, axes, 0, 0, tiled=True)


def local(enc_query, enc_key, enc_value, enc_resid, out_weight, norm_gain, kv_weight, cross_query,
          span_ids, seg_lengths):
    ha = lax.axis_index(HA)
    sa = lax.axis_index(SA)
    sa_count = lax.axis_size(SA)
    core = lax.axis_index("c")

    yl, z = lax.axis_index("yl"), lax.axis_index("z")
    swap = functools.partial(lax.ppermute, axis_name="c", perm=[(0, 1), (1, 0)])

    odd = lax.rem(z, 2)

    with jax.named_scope("pair_out_weight"):
        pair = lax.all_gather(out_weight.reshape(16, 8, HEAD).transpose(1, 0, 2), "c")
    with jax.named_scope("gather_kv_weight"):
        eighth = lax.dynamic_slice_in_dim(
            kv_weight.reshape(D_ENC, 2 * HEAD), core * 512 + odd * 256 + yl * 128, 128, 0)
        pair, eighth = lax.optimization_barrier((pair, eighth))
        kv_mine = spread(jnp.concatenate([eighth[:, :HEAD], eighth[:, HEAD:]], axis=0), PLANE)
    with jax.named_scope("out_weight_over_z"):
        hops = []
        for ha_at in range(8):
            for z_at in range(16):
                for c_at in range(2):
                    there = (z_at + 2 * ha_at + c_at) % 16
                    hops.append(((ha_at * 16 + z_at) * 2 + c_at, (ha_at * 16 + there) * 2 + c_at))
        pair = lax.ppermute(pair, ("yh", "x", "z", "c"), hops)
    slot = (ha * sa_count + sa).reshape(1).astype(jnp.int32)
    context = encoder_attention(slot, span_ids, seg_lengths, enc_query, enc_key, enc_value, enc_resid)
    kv_mine, context = lax.optimization_barrier((kv_mine, context))
    with jax.named_scope("out_weight_over_plane"):
        w_mine = spread(pair, PLANE)
    with jax.named_scope("kv_weight_over_z"):
        up = [(i, (i + 1) % 16) for i in range(16)]
        down = [(i, (i + 15) % 16) for i in range(16)]
        halves = kv_mine[:8], kv_mine[8:]
        near = list(halves) + [lax.ppermute(halves[0], "z", down), lax.ppermute(halves[1], "z", up)]
    with jax.named_scope("swap_weights"):
        far = [swap(half) for half in near]
        w_mine, near, far = lax.optimization_barrier((w_mine, near, far))
        w_other = swap(w_mine)
    place = jnp.stack([z, core, odd]).astype(jnp.int32)
    encoded = project(place, norm_gain.reshape(1, D_ENC), context, w_mine, w_other)
    keyval = keys_and_values(place, encoded, near + far)
    with jax.named_scope("exchange_keyval"):
        keyval = lax.all_to_all(keyval, HA, 0, 0, tiled=True)
    first = jnp.stack([sa, sa_count]).astype(jnp.int32)
    query = cross_query.reshape(QTAIL, GROUP, HEAD).transpose(1, 0, 2).reshape(GROUP * QTAIL, HEAD)
    parts = cross_attention(first, span_ids, seg_lengths, query, keyval)
    with jax.named_scope("exchange_partials"):
        parts = lax.all_to_all(parts, SA, 0, 0, tiled=True)
    return merge(parts).reshape(1, 1, GROUP * HEAD)


def solution(mesh):
    fine = Mesh(mesh.devices.reshape(2, 4, 16, 2, 2), PARTS)
    rows = P(PARTS, None)
    heads = P(None, HA, None)
    placed = (rows, rows, rows, rows, P(SA, None), P(), heads, heads, P(), P())
    return jax.shard_map(
        local, mesh=fine, in_specs=placed, out_specs=P(SA, HA, None), check_vma=False
    )
```

```python
import functools
import math

import jax
import jax.numpy as jnp
import numpy as np
from jax import lax
from jax.experimental import pallas as pl
from jax.experimental.pallas import tpu as pltpu
from jax.sharding import Mesh, PartitionSpec as P

D_ENC = 1024
ENC_HEADS = 16
ENC_HEAD = D_ENC // ENC_HEADS
KV_HEADS = 8
GROUP = 8
HEAD = 128
SEG_LEN = 256
QTAIL = 64
MASKED = -1e30

PARTS = ("yh", "x", "z", "yl", "c")
HA = ("yh", "x")
SA = ("z", "yl", "c")
PLANE = ("yh", "x", "yl")


def params(mebibytes=20):
    return pltpu.CompilerParams(vmem_limit_bytes=mebibytes * 1024 * 1024)


def dot(a, b):
    return jnp.dot(a, b, preferred_element_type=jnp.float32)


def dot_t(a, b):
    return lax.dot_general(a, b, (((1,), (1,)), ((), ())), preferred_element_type=jnp.float32)


def encoder_attention_kernel(slot_ref, span_ref, len_ref, q_ref, k_ref, v_ref, resid_ref, o_ref):
    o_ref[1] = resid_ref[...]
    valid = len_ref[span_ref[slot_ref[0]]]
    keep = lax.broadcasted_iota(jnp.int32, (1, SEG_LEN), 1) < valid
    bias = jnp.where(keep, 0.0, MASKED).astype(jnp.float32)
    low = lax.broadcasted_iota(jnp.int32, (SEG_LEN, 2 * ENC_HEAD), 1) < ENC_HEAD
    for pair in range(ENC_HEADS // 2):
        cols = slice(pair * 2 * ENC_HEAD, (pair + 1) * 2 * ENC_HEAD)
        q, k, v = q_ref[:, cols], k_ref[:, cols], v_ref[:, cols]
        zero = jnp.zeros_like(k)
        parts = []
        for mine in (low, jnp.logical_not(low)):
            scores = dot_t(q, jnp.where(mine, k, zero)) * (1.0 / math.sqrt(ENC_HEAD)) + bias
            expo = jnp.exp(scores - jnp.max(scores, axis=-1, keepdims=True))
            probs = (expo * (1.0 / jnp.sum(expo, axis=-1, keepdims=True))).astype(jnp.bfloat16)
            parts.append(dot(probs, v))
        o_ref[0, :, cols] = jnp.where(low, parts[0], parts[1]).astype(jnp.bfloat16)


def encoder_attention(slot, span_ids, seg_lengths, q, k, v, resid):
    smem = pl.BlockSpec(memory_space=pltpu.SMEM)
    vmem = pl.BlockSpec(memory_space=pltpu.VMEM)
    return pl.pallas_call(
        encoder_attention_kernel,
        out_shape=jax.ShapeDtypeStruct((2, SEG_LEN, D_ENC), jnp.bfloat16),
        in_specs=[smem, smem, smem, vmem, vmem, vmem, vmem],
        out_specs=vmem,
        compiler_params=params(),
        cost_estimate=pl.CostEstimate(
            flops=8 * SEG_LEN * SEG_LEN * D_ENC, bytes_accessed=8 * SEG_LEN * D_ENC,
            transcendentals=SEG_LEN * SEG_LEN * ENC_HEADS),
        name="encoder_attention",
    )(slot, span_ids, seg_lengths, q, k, v, resid)


def encode_kernel(place_ref, gain_ref, ctx_ref, mine_ref, other_ref, *refs):
    kv_refs, o_ref = refs[:6], refs[6]
    w_ref, enc_ref, done_ref = refs[7:10]
    kv_bufs, in_sems, out_sems = refs[10:14], refs[14], refs[15]
    z, core, odd = place_ref[0], place_ref[1], place_ref[2]
    copies = []
    for side in range(2):
        some = pl.ds(8 * side, 8)
        sources = [kv_refs[0].at[some], kv_refs[1].at[some], kv_refs[2 + side], kv_refs[4 + side]]
        copies.append([pltpu.make_async_copy(source, kv_bufs[i].at[some], in_sems.at[4 * side + i])
                       for i, source in enumerate(sources)])
    for side in range(2):
        for copy in copies[side]:
            copy.start()

    for part_ref, at in ((mine_ref, core), (other_ref, 1 - core)):
        for ha in range(KV_HEADS):
            plane = lax.rem(z + 32 - 2 * ha - at, 16)
            for yl in range(2):
                for c in range(2):
                    row = pl.multiple_of(64 * plane + 32 * yl + 16 * c, 16)
                    w_ref[:, pl.ds(row, 16), :] = part_ref[ha * 2 + yl, c]
    ctx = ctx_ref[0]
    hidden = jnp.concatenate(
        [dot(ctx, jnp.concatenate([w_ref[2 * j], w_ref[2 * j + 1]], axis=1)) for j in range(4)], axis=1)
    hidden = hidden + ctx_ref[1].astype(jnp.float32)
    factor = lax.rsqrt(jnp.mean(hidden * hidden, axis=-1, keepdims=True) + 1e-05)
    encoded = (hidden * factor * gain_ref[...]).astype(jnp.bfloat16)
    for piece in range(4):
        enc_ref[piece] = encoded[:, piece * 256:(piece + 1) * 256]
    near, far = 2 * core, 2 - 2 * core
    pieces = [enc_ref[near + odd], enc_ref[near + 1 - odd], enc_ref[far + odd], enc_ref[far + 1 - odd]]

    def rows(ref, h):
        return jnp.concatenate(
            [jnp.concatenate([ref[2 * h + yl, :128], ref[2 * h + yl, 128:]], axis=1) for yl in range(2)], axis=0)

    sends = []
    for h in range(KV_HEADS):
        if h % 4 == 0:
            for copy in copies[h // 4]:
                copy.wait()
        total = dot(pieces[0], rows(kv_bufs[0], h))
        for i in range(1, 4):
            total += dot(pieces[i], rows(kv_bufs[i], h))
        done_ref[h, :SEG_LEN] = total[:, :HEAD].astype(jnp.bfloat16)
        done_ref[h, SEG_LEN:] = total[:, HEAD:].astype(jnp.bfloat16)
        sends.append(pltpu.make_async_copy(done_ref.at[h], o_ref.at[h], out_sems.at[h]))
        sends[h].start()
    for send in sends:
        send.wait()


def encode(place, gain, ctx, mine, other, kvs):
    smem = pl.BlockSpec(memory_space=pltpu.SMEM)
    vmem = pl.BlockSpec(memory_space=pltpu.VMEM)
    hbm = pl.BlockSpec(memory_space=pltpu.HBM)
    shape = jax.ShapeDtypeStruct((KV_HEADS, 2 * SEG_LEN, HEAD), jnp.bfloat16)
    return pl.pallas_call(
        encode_kernel,
        out_shape=shape,
        in_specs=[smem] + [vmem] * 4 + [hbm] * 6,
        out_specs=hbm,
        scratch_shapes=[pltpu.VMEM((8, D_ENC, HEAD), jnp.bfloat16),
                        pltpu.VMEM((4, SEG_LEN, 256), jnp.bfloat16),
                        pltpu.VMEM(shape.shape, shape.dtype)]
        + [pltpu.VMEM(kvs[0].shape, kvs[0].dtype)] * 4
        + [pltpu.SemaphoreType.DMA((8,)), pltpu.SemaphoreType.DMA((KV_HEADS,))],
        compiler_params=params(47),
        cost_estimate=pl.CostEstimate(
            flops=6 * SEG_LEN * D_ENC * D_ENC, bytes_accessed=8 * D_ENC * D_ENC, transcendentals=SEG_LEN),
        name="encode_keyval",
    )(place, gain, ctx, mine, other, *kvs)


def cross_kernel(slots, first_ref, span_ref, len_ref, q_ref, kv_ref, o_ref):
    scale = 1.0 / math.sqrt(HEAD)
    lane = lax.broadcasted_iota(jnp.int32, (1, SEG_LEN), 1)
    bias = []
    for s in range(slots):
        valid = len_ref[span_ref[first_ref[0] + s * first_ref[1]]]
        bias.append(jnp.where(lane < valid, 0.0, MASKED).astype(jnp.float32))
    bias = jnp.concatenate(bias, axis=1)
    keys = kv_ref[:, :SEG_LEN].reshape(slots * SEG_LEN, HEAD)
    values = kv_ref[:, SEG_LEN:].reshape(slots * SEG_LEN, HEAD)
    rows = 2 * QTAIL
    column = lax.broadcasted_iota(jnp.int32, (rows, HEAD), 1)
    levels = jnp.zeros((rows, HEAD), jnp.float32)

    def put(at, block):
        block = block.reshape(2, QTAIL, HEAD)
        o_ref[:, :, at * HEAD:(at + 1) * HEAD] = jnp.stack([block[0], block[1]], axis=1).astype(jnp.bfloat16)

    for b in range(GROUP // 2):
        q = q_ref[b * rows:(b + 1) * rows]
        scores = dot_t(q, keys) + bias
        top = jnp.max(scores, axis=-1, keepdims=True)
        expo = jnp.exp((scores - top) * scale)
        total = jnp.sum(expo, axis=-1, keepdims=True)
        put(b, dot(expo.astype(jnp.bfloat16), values) / total)
        level = jnp.broadcast_to(top * scale + jnp.log(total), (rows, HEAD))
        high = level.astype(jnp.bfloat16).astype(jnp.float32)
        middle = (level - high).astype(jnp.bfloat16).astype(jnp.float32)
        rest = level - high - middle
        for k, part in enumerate((high, middle, rest)):
            levels = jnp.where(column == 3 * b + k, part, levels)
    put(GROUP // 2, levels)


def cross_attention(first, span_ids, seg_lengths, q, kv):
    smem = pl.BlockSpec(memory_space=pltpu.SMEM)
    vmem = pl.BlockSpec(memory_space=pltpu.VMEM)
    slots = kv.shape[0]
    return pl.pallas_call(
        functools.partial(cross_kernel, slots),
        out_shape=jax.ShapeDtypeStruct((QTAIL, 2, 640), jnp.bfloat16),
        in_specs=[smem, smem, smem, vmem, vmem],
        out_specs=vmem,
        compiler_params=params(),
        name="cross_attention",
    )(first, span_ids, seg_lengths, q, kv)


def merge_kernel(part_ref, o_ref):
    for b in range(GROUP // 2):
        level = jnp.sum(part_ref[:, :, 512 + 3 * b:515 + 3 * b].astype(jnp.float32), axis=-1, keepdims=True)
        weight = jnp.exp(level - jnp.max(level, axis=0, keepdims=True))
        average = part_ref[:, :, HEAD * b:HEAD * (b + 1)].astype(jnp.float32)
        o_ref[2 * b:2 * b + 2] = jnp.sum(average * weight, axis=0) / jnp.sum(weight, axis=0)


def merge(parts):
    vmem = pl.BlockSpec(memory_space=pltpu.VMEM)
    return pl.pallas_call(
        merge_kernel,
        out_shape=jax.ShapeDtypeStruct((GROUP, HEAD), jnp.float32),
        in_specs=[vmem],
        out_specs=vmem,
        name="merge_partials",
    )(parts)


def spread(block, axes):
    count = lax.axis_size(axes)
    copies = jnp.broadcast_to(block[None], (count,) + block.shape)
    return lax.all_to_all(copies, axes, 0, 0, tiled=True)


def local(enc_query, enc_key, enc_value, enc_resid, out_weight, norm_gain, kv_weight, cross_query,
          span_ids, seg_lengths):
    ha = lax.axis_index(HA)
    sa = lax.axis_index(SA)
    sa_count = lax.axis_size(SA)
    core = lax.axis_index("c")

    yl, z = lax.axis_index("yl"), lax.axis_index("z")
    swap = functools.partial(lax.ppermute, axis_name="c", perm=[(0, 1), (1, 0)])

    odd = lax.rem(z, 2)

    with jax.named_scope("pair_out_weight"):
        pair = lax.all_gather(out_weight.reshape(16, 8, HEAD).transpose(1, 0, 2), "c")
    with jax.named_scope("gather_kv_weight"):
        eighth = lax.dynamic_slice_in_dim(
            kv_weight.reshape(D_ENC, 2 * HEAD), core * 512 + odd * 256 + yl * 128, 128, 0)
        pair, eighth = lax.optimization_barrier((pair, eighth))
        kv_mine = spread(jnp.concatenate([eighth[:, :HEAD], eighth[:, HEAD:]], axis=0), PLANE)
    with jax.named_scope("out_weight_over_z"):
        hops = []
        for ha_at in range(8):
            for z_at in range(16):
                for c_at in range(2):
                    there = (z_at + 2 * ha_at + c_at) % 16
                    hops.append(((ha_at * 16 + z_at) * 2 + c_at, (ha_at * 16 + there) * 2 + c_at))
        pair = lax.ppermute(pair, ("yh", "x", "z", "c"), hops)
    slot = (ha * sa_count + sa).reshape(1).astype(jnp.int32)
    context = encoder_attention(slot, span_ids, seg_lengths, enc_query, enc_key, enc_value, enc_resid)
    kv_mine, pair, context = lax.optimization_barrier((kv_mine, pair, context))
    with jax.named_scope("out_weight_over_plane"):
        w_mine = spread(pair, PLANE)
    with jax.named_scope("kv_weight_over_z"):
        pairs = []
        for z_at in range(16):
            for c_at in range(2):
                there = (z_at + (1 if (z_at + c_at) % 2 == 0 else 15)) % 16
                pairs.append((2 * z_at + c_at, 2 * there + c_at))
        kv_next = lax.ppermute(kv_mine, ("z", "c"), pairs)
    with jax.named_scope("swap_weights"):
        kvs = [kv_mine, kv_next]
        kvs = kvs + [swap(part) for kv in kvs for part in (kv[:8], kv[8:])]
        w_mine, kvs = lax.optimization_barrier((w_mine, kvs))
        w_other = swap(w_mine)
    place = jnp.stack([z, core, odd]).astype(jnp.int32)
    keyval = encode(place, norm_gain.reshape(1, D_ENC), context, w_mine, w_other, kvs)
    with jax.named_scope("exchange_keyval"):
        keyval = lax.all_to_all(keyval, HA, 0, 0, tiled=True)
    first = jnp.stack([sa, sa_count]).astype(jnp.int32)
    query = cross_query.reshape(QTAIL, GROUP, HEAD).transpose(1, 0, 2).reshape(GROUP * QTAIL, HEAD)
    parts = cross_attention(first, span_ids, seg_lengths, query, keyval)
    with jax.named_scope("exchange_partials"):
        parts = lax.all_to_all(parts, SA, 0, 0, tiled=True)
    return merge(parts).reshape(1, 1, GROUP * HEAD)


def solution(mesh):
    fine = Mesh(mesh.devices.reshape(2, 4, 16, 2, 2), PARTS)
    rows = P(PARTS, None)
    heads = P(None, HA, None)
    placed = (rows, rows, rows, rows, P(SA, None), P(), heads, heads, P(), P())
    return jax.shard_map(
        local, mesh=fine, in_specs=placed, out_specs=P(SA, HA, None), check_vma=False
    )
```

```python
import functools
import math

import jax
import jax.numpy as jnp
import numpy as np
from jax import lax
from jax.experimental import pallas as pl
from jax.experimental.pallas import tpu as pltpu
from jax.sharding import Mesh, PartitionSpec as P

D_ENC = 1024
ENC_HEADS = 16
ENC_HEAD = D_ENC // ENC_HEADS
KV_HEADS = 8
GROUP = 8
HEAD = 128
SEG_LEN = 256
QTAIL = 64
MASKED = -1e30

PARTS = ("yh", "x", "z", "yl", "c")
HA = ("yh", "x")
SA = ("z", "yl", "c")
PLANE = ("yh", "x", "yl")


def params(mebibytes=20):
    return pltpu.CompilerParams(vmem_limit_bytes=mebibytes * 1024 * 1024)


def dot(a, b):
    return jnp.dot(a, b, preferred_element_type=jnp.float32)


def dot_t(a, b):
    return lax.dot_general(a, b, (((1,), (1,)), ((), ())), preferred_element_type=jnp.float32)


def encoder_attention_kernel(slot_ref, span_ref, len_ref, q_ref, k_ref, v_ref, o_ref):
    valid = len_ref[span_ref[slot_ref[0]]]
    keep = lax.broadcasted_iota(jnp.int32, (1, SEG_LEN), 1) < valid
    bias = jnp.where(keep, 0.0, MASKED).astype(jnp.float32)
    low = lax.broadcasted_iota(jnp.int32, (SEG_LEN, 2 * ENC_HEAD), 1) < ENC_HEAD
    scale = math.log2(math.e) / math.sqrt(ENC_HEAD)
    for pair in range(ENC_HEADS // 2):
        cols = slice(pair * 2 * ENC_HEAD, (pair + 1) * 2 * ENC_HEAD)
        q, k, v = q_ref[:, cols], k_ref[:, cols], v_ref[:, cols]
        zero = jnp.zeros_like(k)
        parts = []
        for mine in (low, jnp.logical_not(low)):
            scores = dot_t(q, jnp.where(mine, k, zero)) + bias
            expo = jnp.exp2((scores - jnp.max(scores, axis=-1, keepdims=True)) * scale)
            probs = (expo * (1.0 / jnp.sum(expo, axis=-1, keepdims=True))).astype(jnp.bfloat16)
            parts.append(dot(probs, v))
        o_ref[:, cols] = jnp.where(low, parts[0], parts[1]).astype(jnp.bfloat16)


def encoder_attention(slot, span_ids, seg_lengths, q, k, v):
    smem = pl.BlockSpec(memory_space=pltpu.SMEM)
    vmem = pl.BlockSpec(memory_space=pltpu.VMEM)
    return pl.pallas_call(
        encoder_attention_kernel,
        out_shape=jax.ShapeDtypeStruct((SEG_LEN, D_ENC), jnp.bfloat16),
        in_specs=[smem, smem, smem, vmem, vmem, vmem],
        out_specs=vmem,
        compiler_params=params(),
        cost_estimate=pl.CostEstimate(
            flops=8 * SEG_LEN * SEG_LEN * D_ENC, bytes_accessed=8 * SEG_LEN * D_ENC,
            transcendentals=SEG_LEN * SEG_LEN * ENC_HEADS),
        name="encoder_attention",
    )(slot, span_ids, seg_lengths, q, k, v)


def encode_kernel(place_ref, gain_ref, ctx_ref, resid_ref, mine_ref, other_ref, *refs):
    kv_refs, o_ref = refs[:6], refs[6]
    w_ref, enc_ref, done_ref = refs[7:10]
    kv_bufs, in_sems, out_sems = refs[10:14], refs[14], refs[15]
    z, core, odd = place_ref[0], place_ref[1], place_ref[2]
    copies = []
    for side in range(2):
        some = pl.ds(8 * side, 8)
        sources = [kv_refs[0].at[some], kv_refs[1].at[some], kv_refs[2 + side], kv_refs[4 + side]]
        copies.append([pltpu.make_async_copy(source, kv_bufs[i].at[some], in_sems.at[4 * side + i])
                       for i, source in enumerate(sources)])
    for side in range(2):
        for copy in copies[side]:
            copy.start()

    for part_ref, at in ((mine_ref, core), (other_ref, 1 - core)):
        for ha in range(KV_HEADS):
            plane = lax.rem(z + 32 - 2 * ha - at, 16)
            for yl in range(2):
                for c in range(2):
                    row = pl.multiple_of(64 * plane + 32 * yl + 16 * c, 16)
                    w_ref[:, pl.ds(row, 16), :] = part_ref[ha * 2 + yl, c]
    ctx = ctx_ref[...]
    hidden = jnp.concatenate(
        [dot(ctx, jnp.concatenate([w_ref[2 * j], w_ref[2 * j + 1]], axis=1)) for j in range(4)], axis=1)
    hidden = hidden + resid_ref[...].astype(jnp.float32)
    factor = lax.rsqrt(jnp.mean(hidden * hidden, axis=-1, keepdims=True) + 1e-05)
    encoded = (hidden * factor * gain_ref[...]).astype(jnp.bfloat16)
    for piece in range(4):
        enc_ref[piece] = encoded[:, piece * 256:(piece + 1) * 256]
    near, far = 2 * core, 2 - 2 * core
    pieces = [enc_ref[near + odd], enc_ref[near + 1 - odd], enc_ref[far + odd], enc_ref[far + 1 - odd]]

    def rows(ref, h):
        return jnp.concatenate(
            [jnp.concatenate([ref[2 * h + yl, :128], ref[2 * h + yl, 128:]], axis=1) for yl in range(2)], axis=0)

    sends = []
    for h in range(KV_HEADS):
        if h % 4 == 0:
            for copy in copies[h // 4]:
                copy.wait()
        total = dot(pieces[0], rows(kv_bufs[0], h))
        for i in range(1, 4):
            total += dot(pieces[i], rows(kv_bufs[i], h))
        done_ref[h, :SEG_LEN] = total[:, :HEAD].astype(jnp.bfloat16)
        done_ref[h, SEG_LEN:] = total[:, HEAD:].astype(jnp.bfloat16)
        sends.append(pltpu.make_async_copy(done_ref.at[h], o_ref.at[h], out_sems.at[h]))
        sends[h].start()
    for send in sends:
        send.wait()


def encode(place, gain, ctx, resid, mine, other, kvs):
    smem = pl.BlockSpec(memory_space=pltpu.SMEM)
    vmem = pl.BlockSpec(memory_space=pltpu.VMEM)
    hbm = pl.BlockSpec(memory_space=pltpu.HBM)
    shape = jax.ShapeDtypeStruct((KV_HEADS, 2 * SEG_LEN, HEAD), jnp.bfloat16)
    return pl.pallas_call(
        encode_kernel,
        out_shape=shape,
        in_specs=[smem] + [vmem] * 5 + [hbm] * 6,
        out_specs=hbm,
        scratch_shapes=[pltpu.VMEM((8, D_ENC, HEAD), jnp.bfloat16),
                        pltpu.VMEM((4, SEG_LEN, 256), jnp.bfloat16),
                        pltpu.VMEM(shape.shape, shape.dtype)]
        + [pltpu.VMEM(kvs[0].shape, kvs[0].dtype)] * 4
        + [pltpu.SemaphoreType.DMA((8,)), pltpu.SemaphoreType.DMA((KV_HEADS,))],
        compiler_params=params(47),
        cost_estimate=pl.CostEstimate(
            flops=6 * SEG_LEN * D_ENC * D_ENC, bytes_accessed=8 * D_ENC * D_ENC, transcendentals=SEG_LEN),
        name="encode_keyval",
    )(place, gain, ctx, resid, mine, other, *kvs)


def cross_kernel(slots, first_ref, span_ref, len_ref, q_ref, kv_ref, o_ref):
    scale = 1.0 / math.sqrt(HEAD)
    lane = lax.broadcasted_iota(jnp.int32, (1, SEG_LEN), 1)
    bias = []
    for s in range(slots):
        valid = len_ref[span_ref[first_ref[0] + s * first_ref[1]]]
        bias.append(jnp.where(lane < valid, 0.0, MASKED).astype(jnp.float32))
    bias = jnp.concatenate(bias, axis=1)
    keys = kv_ref[:, :SEG_LEN].reshape(slots * SEG_LEN, HEAD)
    values = kv_ref[:, SEG_LEN:].reshape(slots * SEG_LEN, HEAD)
    rows = 2 * QTAIL
    column = lax.broadcasted_iota(jnp.int32, (rows, HEAD), 1)
    levels = jnp.zeros((rows, HEAD), jnp.float32)

    def put(at, block):
        block = block.reshape(2, QTAIL, HEAD)
        o_ref[:, :, at * HEAD:(at + 1) * HEAD] = jnp.stack([block[0], block[1]], axis=1).astype(jnp.bfloat16)

    for b in range(GROUP // 2):
        q = q_ref[b * rows:(b + 1) * rows]
        scores = dot_t(q, keys) + bias
        top = jnp.max(scores, axis=-1, keepdims=True)
        expo = jnp.exp2((scores - top) * (scale * math.log2(math.e)))
        total = jnp.sum(expo, axis=-1, keepdims=True)
        put(b, dot(expo.astype(jnp.bfloat16), values) / total)
        level = jnp.broadcast_to(top * scale + jnp.log(total), (rows, HEAD))
        high = level.astype(jnp.bfloat16).astype(jnp.float32)
        middle = (level - high).astype(jnp.bfloat16).astype(jnp.float32)
        rest = level - high - middle
        for k, part in enumerate((high, middle, rest)):
            levels = jnp.where(column == 3 * b + k, part, levels)
    put(GROUP // 2, levels)


def cross_attention(first, span_ids, seg_lengths, q, kv):
    smem = pl.BlockSpec(memory_space=pltpu.SMEM)
    vmem = pl.BlockSpec(memory_space=pltpu.VMEM)
    slots = kv.shape[0]
    return pl.pallas_call(
        functools.partial(cross_kernel, slots),
        out_shape=jax.ShapeDtypeStruct((QTAIL, 2, 640), jnp.bfloat16),
        in_specs=[smem, smem, smem, vmem, vmem],
        out_specs=vmem,
        compiler_params=params(),
        name="cross_attention",
    )(first, span_ids, seg_lengths, q, kv)


def merge_kernel(part_ref, o_ref):
    pieces = part_ref[:, :, 4 * HEAD:].astype(jnp.float32)
    level = pieces + pltpu.roll(pieces, HEAD - 1, 2) + pltpu.roll(pieces, HEAD - 2, 2)
    weight = jnp.exp(level - jnp.max(level, axis=0, keepdims=True))
    total = jnp.sum(weight, axis=0)
    for b in range(GROUP // 2):
        average = part_ref[:, :, HEAD * b:HEAD * (b + 1)].astype(jnp.float32)
        at = slice(3 * b, 3 * b + 1)
        o_ref[2 * b:2 * b + 2] = jnp.sum(average * weight[:, :, at], axis=0) / total[:, at]


def merge(parts):
    vmem = pl.BlockSpec(memory_space=pltpu.VMEM)
    return pl.pallas_call(
        merge_kernel,
        out_shape=jax.ShapeDtypeStruct((GROUP, HEAD), jnp.float32),
        in_specs=[vmem],
        out_specs=vmem,
        name="merge_partials",
    )(parts)


def spread(block, axes):
    count = lax.axis_size(axes)
    copies = jnp.broadcast_to(block[None], (count,) + block.shape)
    return lax.all_to_all(copies, axes, 0, 0, tiled=True)


def local(enc_query, enc_key, enc_value, enc_resid, out_weight, norm_gain, kv_weight, cross_query,
          span_ids, seg_lengths):
    ha = lax.axis_index(HA)
    sa = lax.axis_index(SA)
    sa_count = lax.axis_size(SA)
    core = lax.axis_index("c")

    yl, z = lax.axis_index("yl"), lax.axis_index("z")
    swap = functools.partial(lax.ppermute, axis_name="c", perm=[(0, 1), (1, 0)])

    odd = lax.rem(z, 2)

    with jax.named_scope("pair_out_weight"):
        pair = lax.all_gather(out_weight.reshape(16, 8, HEAD).transpose(1, 0, 2), "c")
    with jax.named_scope("gather_kv_weight"):
        eighth = lax.dynamic_slice_in_dim(
            kv_weight.reshape(D_ENC, 2 * HEAD), core * 512 + odd * 256 + yl * 128, 128, 0)
        pair, eighth = lax.optimization_barrier((pair, eighth))
        kv_mine = spread(jnp.concatenate([eighth[:, :HEAD], eighth[:, HEAD:]], axis=0), PLANE)
    with jax.named_scope("out_weight_over_z"):
        hops = []
        for ha_at in range(8):
            for z_at in range(16):
                for c_at in range(2):
                    there = (z_at + 2 * ha_at + c_at) % 16
                    hops.append(((ha_at * 16 + z_at) * 2 + c_at, (ha_at * 16 + there) * 2 + c_at))
        pair = lax.ppermute(pair, ("yh", "x", "z", "c"), hops)
    slot = (ha * sa_count + sa).reshape(1).astype(jnp.int32)
    context = encoder_attention(slot, span_ids, seg_lengths, enc_query, enc_key, enc_value)
    kv_mine, pair, context = lax.optimization_barrier((kv_mine, pair, context))
    with jax.named_scope("out_weight_over_plane"):
        w_mine = spread(pair, PLANE)
    with jax.named_scope("kv_weight_over_z"):
        pairs = []
        for z_at in range(16):
            for c_at in range(2):
                there = (z_at + (1 if (z_at + c_at) % 2 == 0 else 15)) % 16
                pairs.append((2 * z_at + c_at, 2 * there + c_at))
        kv_next = lax.ppermute(kv_mine, ("z", "c"), pairs)
    with jax.named_scope("swap_weights"):
        kvs = [kv_mine, kv_next]
        kvs = kvs + [swap(part) for kv in kvs for part in (kv[:8], kv[8:])]
        w_mine, kvs = lax.optimization_barrier((w_mine, kvs))
        w_other = swap(w_mine)
    place = jnp.stack([z, core, odd]).astype(jnp.int32)
    keyval = encode(place, norm_gain.reshape(1, D_ENC), context, enc_resid, w_mine, w_other, kvs)
    with jax.named_scope("exchange_keyval"):
        keyval = lax.all_to_all(keyval, HA, 0, 0, tiled=True)
    first = jnp.stack([sa, sa_count]).astype(jnp.int32)
    query = cross_query.reshape(QTAIL, GROUP, HEAD).transpose(1, 0, 2).reshape(GROUP * QTAIL, HEAD)
    parts = cross_attention(first, span_ids, seg_lengths, query, keyval)
    with jax.named_scope("exchange_partials"):
        parts = lax.all_to_all(parts, SA, 0, 0, tiled=True)
    return merge(parts).reshape(1, 1, GROUP * HEAD)


def solution(mesh):
    fine = Mesh(mesh.devices.reshape(2, 4, 16, 2, 2), PARTS)
    rows = P(PARTS, None)
    heads = P(None, HA, None)
    placed = (rows, rows, rows, rows, P(SA, None), P(), heads, heads, P(), P())
    return jax.shard_map(
        local, mesh=fine, in_specs=placed, out_specs=P(SA, HA, None), check_vma=False
    )
```

```python
import functools
import math

import jax
import jax.numpy as jnp
import numpy as np
from jax import lax
from jax.experimental import pallas as pl
from jax.experimental.pallas import tpu as pltpu
from jax.sharding import Mesh, PartitionSpec as P

D_ENC = 1024
ENC_HEADS = 16
ENC_HEAD = D_ENC // ENC_HEADS
KV_HEADS = 8
GROUP = 8
HEAD = 128
SEG_LEN = 256
QTAIL = 64
MASKED = -1e30

PARTS = ("yh", "x", "z", "yl", "c")
HA = ("yh", "x")
SA = ("z", "yl", "c")
PLANE = ("yh", "x", "yl")


def params(mebibytes=20):
    return pltpu.CompilerParams(vmem_limit_bytes=mebibytes * 1024 * 1024)


def dot(a, b):
    return jnp.dot(a, b, preferred_element_type=jnp.float32)


def dot_t(a, b):
    return lax.dot_general(a, b, (((1,), (1,)), ((), ())), preferred_element_type=jnp.float32)


def encoder_attention_kernel(slot_ref, span_ref, len_ref, q_ref, k_ref, v_ref, o_ref):
    valid = len_ref[span_ref[slot_ref[0]]]
    keep = lax.broadcasted_iota(jnp.int32, (1, SEG_LEN), 1) < valid
    bias = jnp.where(keep, 0.0, MASKED).astype(jnp.float32)
    low = lax.broadcasted_iota(jnp.int32, (SEG_LEN, 2 * ENC_HEAD), 1) < ENC_HEAD
    scale = math.log2(math.e) / math.sqrt(ENC_HEAD)
    for pair in range(ENC_HEADS // 2):
        cols = slice(pair * 2 * ENC_HEAD, (pair + 1) * 2 * ENC_HEAD)
        q, k, v = q_ref[:, cols], k_ref[:, cols], v_ref[:, cols]
        zero = jnp.zeros_like(k)
        parts = []
        for mine in (low, jnp.logical_not(low)):
            scores = dot_t(q, jnp.where(mine, k, zero)) + bias
            expo = jnp.exp2((scores - jnp.max(scores, axis=-1, keepdims=True)) * scale)
            probs = (expo * (1.0 / jnp.sum(expo, axis=-1, keepdims=True))).astype(jnp.bfloat16)
            parts.append(dot(probs, v))
        o_ref[:, cols] = jnp.where(low, parts[0], parts[1]).astype(jnp.bfloat16)


def encoder_attention(slot, span_ids, seg_lengths, q, k, v):
    smem = pl.BlockSpec(memory_space=pltpu.SMEM)
    vmem = pl.BlockSpec(memory_space=pltpu.VMEM)
    return pl.pallas_call(
        encoder_attention_kernel,
        out_shape=jax.ShapeDtypeStruct((SEG_LEN, D_ENC), jnp.bfloat16),
        in_specs=[smem, smem, smem, vmem, vmem, vmem],
        out_specs=vmem,
        compiler_params=params(),
        cost_estimate=pl.CostEstimate(
            flops=8 * SEG_LEN * SEG_LEN * D_ENC, bytes_accessed=8 * SEG_LEN * D_ENC,
            transcendentals=SEG_LEN * SEG_LEN * ENC_HEADS),
        name="encoder_attention",
    )(slot, span_ids, seg_lengths, q, k, v)


def encode_kernel(place_ref, gain_ref, ctx_ref, resid_ref, mine_ref, other_ref, *refs):
    kv_refs, o_ref = refs[:6], refs[6]
    w_ref, enc_ref, done_ref = refs[7:10]
    kv_bufs, in_sems, out_sems = refs[10:14], refs[14], refs[15]
    z, core, odd = place_ref[0], place_ref[1], place_ref[2]
    copies = []
    for side in range(2):
        some = pl.ds(8 * side, 8)
        sources = [kv_refs[0].at[some], kv_refs[1].at[some], kv_refs[2 + side], kv_refs[4 + side]]
        copies.append([pltpu.make_async_copy(source, kv_bufs[i].at[some], in_sems.at[4 * side + i])
                       for i, source in enumerate(sources)])
    for side in range(2):
        for copy in copies[side]:
            copy.start()

    for part_ref, at in ((mine_ref, core), (other_ref, 1 - core)):
        for ha in range(KV_HEADS):
            plane = lax.rem(z + 32 - 2 * ha - at, 16)
            for yl in range(2):
                for c in range(2):
                    row = pl.multiple_of(64 * plane + 32 * yl + 16 * c, 16)
                    w_ref[:, pl.ds(row, 16), :] = part_ref[ha * 2 + yl, c]
    ctx = ctx_ref[...]
    hidden = jnp.concatenate(
        [dot(ctx, jnp.concatenate([w_ref[2 * j], w_ref[2 * j + 1]], axis=1)) for j in range(4)], axis=1)
    hidden = hidden + resid_ref[...].astype(jnp.float32)
    factor = lax.rsqrt(jnp.mean(hidden * hidden, axis=-1, keepdims=True) + 1e-05)
    encoded = (hidden * factor * gain_ref[...]).astype(jnp.bfloat16)
    for piece in range(4):
        enc_ref[piece] = encoded[:, piece * 256:(piece + 1) * 256]
    near, far = 2 * core, 2 - 2 * core
    pieces = [enc_ref[near + odd], enc_ref[near + 1 - odd], enc_ref[far + odd], enc_ref[far + 1 - odd]]

    def rows(ref, h):
        return jnp.concatenate(
            [jnp.concatenate([ref[2 * h + yl, :128], ref[2 * h + yl, 128:]], axis=1) for yl in range(2)], axis=0)

    sends = []
    for h in range(KV_HEADS):
        if h % 4 == 0:
            for copy in copies[h // 4]:
                copy.wait()
        total = dot(pieces[0], rows(kv_bufs[0], h))
        for i in range(1, 4):
            total += dot(pieces[i], rows(kv_bufs[i], h))
        done_ref[h, :SEG_LEN] = total[:, :HEAD].astype(jnp.bfloat16)
        done_ref[h, SEG_LEN:] = total[:, HEAD:].astype(jnp.bfloat16)
        sends.append(pltpu.make_async_copy(done_ref.at[h], o_ref.at[h], out_sems.at[h]))
        sends[h].start()
    for send in sends:
        send.wait()


def encode(place, gain, ctx, resid, mine, other, kvs):
    smem = pl.BlockSpec(memory_space=pltpu.SMEM)
    vmem = pl.BlockSpec(memory_space=pltpu.VMEM)
    hbm = pl.BlockSpec(memory_space=pltpu.HBM)
    shape = jax.ShapeDtypeStruct((KV_HEADS, 2 * SEG_LEN, HEAD), jnp.bfloat16)
    return pl.pallas_call(
        encode_kernel,
        out_shape=shape,
        in_specs=[smem] + [vmem] * 5 + [hbm] * 6,
        out_specs=hbm,
        scratch_shapes=[pltpu.VMEM((8, D_ENC, HEAD), jnp.bfloat16),
                        pltpu.VMEM((4, SEG_LEN, 256), jnp.bfloat16),
                        pltpu.VMEM(shape.shape, shape.dtype)]
        + [pltpu.VMEM(kvs[0].shape, kvs[0].dtype)] * 4
        + [pltpu.SemaphoreType.DMA((8,)), pltpu.SemaphoreType.DMA((KV_HEADS,))],
        compiler_params=params(48),
        cost_estimate=pl.CostEstimate(
            flops=6 * SEG_LEN * D_ENC * D_ENC, bytes_accessed=8 * D_ENC * D_ENC, transcendentals=SEG_LEN),
        name="encode_keyval",
    )(place, gain, ctx, resid, mine, other, *kvs)


def cross_kernel(slots, first_ref, span_ref, len_ref, q_ref, kv_ref, o_ref):
    scale = 1.0 / math.sqrt(HEAD)
    lane = lax.broadcasted_iota(jnp.int32, (1, SEG_LEN), 1)
    bias = []
    for s in range(slots):
        valid = len_ref[span_ref[first_ref[0] + s * first_ref[1]]]
        bias.append(jnp.where(lane < valid, 0.0, MASKED).astype(jnp.float32))
    bias = jnp.concatenate(bias, axis=1)
    keys = kv_ref[:, :SEG_LEN].reshape(slots * SEG_LEN, HEAD)
    values = kv_ref[:, SEG_LEN:].reshape(slots * SEG_LEN, HEAD)
    rows = 2 * QTAIL
    column = lax.broadcasted_iota(jnp.int32, (rows, HEAD), 1)
    levels = jnp.zeros((rows, HEAD), jnp.float32)

    def put(at, block):
        block = block.reshape(2, QTAIL, HEAD)
        o_ref[:, :, at * HEAD:(at + 1) * HEAD] = jnp.stack([block[0], block[1]], axis=1).astype(jnp.bfloat16)

    for b in range(GROUP // 2):
        q = q_ref[b * rows:(b + 1) * rows]
        scores = dot_t(q, keys) + bias
        top = jnp.max(scores, axis=-1, keepdims=True)
        expo = jnp.exp2((scores - top) * (scale * math.log2(math.e)))
        total = jnp.sum(expo, axis=-1, keepdims=True)
        put(b, dot(expo.astype(jnp.bfloat16), values) / total)
        level = jnp.broadcast_to(top * scale + jnp.log(total), (rows, HEAD))
        high = level.astype(jnp.bfloat16).astype(jnp.float32)
        middle = (level - high).astype(jnp.bfloat16).astype(jnp.float32)
        rest = level - high - middle
        for k, part in enumerate((high, middle, rest)):
            levels = jnp.where(column == 3 * b + k, part, levels)
    put(GROUP // 2, levels)


def cross_attention(first, span_ids, seg_lengths, q, kv):
    smem = pl.BlockSpec(memory_space=pltpu.SMEM)
    vmem = pl.BlockSpec(memory_space=pltpu.VMEM)
    slots = kv.shape[0]
    return pl.pallas_call(
        functools.partial(cross_kernel, slots),
        out_shape=jax.ShapeDtypeStruct((QTAIL, 2, 640), jnp.bfloat16),
        in_specs=[smem, smem, smem, vmem, vmem],
        out_specs=vmem,
        compiler_params=params(),
        name="cross_attention",
    )(first, span_ids, seg_lengths, q, kv)


def merge_kernel(part_ref, o_ref):
    pieces = part_ref[:, :, 4 * HEAD:].astype(jnp.float32)
    level = pieces + pltpu.roll(pieces, HEAD - 1, 2) + pltpu.roll(pieces, HEAD - 2, 2)
    weight = jnp.exp(level - jnp.max(level, axis=0, keepdims=True))
    total = jnp.sum(weight, axis=0)
    for b in range(GROUP // 2):
        average = part_ref[:, :, HEAD * b:HEAD * (b + 1)].astype(jnp.float32)
        at = slice(3 * b, 3 * b + 1)
        o_ref[2 * b:2 * b + 2] = jnp.sum(average * weight[:, :, at], axis=0) / total[:, at]


def merge(parts):
    vmem = pl.BlockSpec(memory_space=pltpu.VMEM)
    return pl.pallas_call(
        merge_kernel,
        out_shape=jax.ShapeDtypeStruct((GROUP, HEAD), jnp.float32),
        in_specs=[vmem],
        out_specs=vmem,
        name="merge_partials",
    )(parts)


def spread(block, axes):
    count = lax.axis_size(axes)
    copies = jnp.broadcast_to(block[None], (count,) + block.shape)
    return lax.all_to_all(copies, axes, 0, 0, tiled=True)


def local(enc_query, enc_key, enc_value, enc_resid, out_weight, norm_gain, kv_weight, cross_query,
          span_ids, seg_lengths):
    ha = lax.axis_index(HA)
    sa = lax.axis_index(SA)
    sa_count = lax.axis_size(SA)
    core = lax.axis_index("c")

    yl, z = lax.axis_index("yl"), lax.axis_index("z")
    swap = functools.partial(lax.ppermute, axis_name="c", perm=[(0, 1), (1, 0)])

    odd = lax.rem(z, 2)

    with jax.named_scope("pair_out_weight"):
        pair = lax.all_gather(out_weight.reshape(16, 8, HEAD).transpose(1, 0, 2), "c")
    with jax.named_scope("gather_kv_weight"):
        eighth = lax.dynamic_slice_in_dim(
            kv_weight.reshape(D_ENC, 2 * HEAD), core * 512 + odd * 256 + yl * 128, 128, 0)
        pair, eighth = lax.optimization_barrier((pair, eighth))
        kv_mine = spread(jnp.concatenate([eighth[:, :HEAD], eighth[:, HEAD:]], axis=0), PLANE)
    with jax.named_scope("out_weight_over_z"):
        hops = []
        for ha_at in range(8):
            for z_at in range(16):
                for c_at in range(2):
                    there = (z_at + 2 * ha_at + c_at) % 16
                    hops.append(((ha_at * 16 + z_at) * 2 + c_at, (ha_at * 16 + there) * 2 + c_at))
        pair = lax.ppermute(pair, ("yh", "x", "z", "c"), hops)
    slot = (ha * sa_count + sa).reshape(1).astype(jnp.int32)
    context = encoder_attention(slot, span_ids, seg_lengths, enc_query, enc_key, enc_value)
    kv_mine, pair = lax.optimization_barrier((kv_mine, pair))
    with jax.named_scope("out_weight_over_plane"):
        w_mine = spread(pair, PLANE)
    with jax.named_scope("kv_weight_over_z"):
        pairs = []
        for z_at in range(16):
            for c_at in range(2):
                there = (z_at + (1 if (z_at + c_at) % 2 == 0 else 15)) % 16
                pairs.append((2 * z_at + c_at, 2 * there + c_at))
        kv_next = lax.ppermute(kv_mine, ("z", "c"), pairs)
    with jax.named_scope("swap_weights"):
        kvs = [kv_mine, kv_next]
        kvs = kvs + [swap(part) for kv in kvs for part in (kv[:8], kv[8:])]
        w_mine, kvs = lax.optimization_barrier((w_mine, kvs))
        w_other = swap(w_mine)
    place = jnp.stack([z, core, odd]).astype(jnp.int32)
    keyval = encode(place, norm_gain.reshape(1, D_ENC), context, enc_resid, w_mine, w_other, kvs)
    with jax.named_scope("exchange_keyval"):
        keyval = lax.all_to_all(keyval, HA, 0, 0, tiled=True)
    first = jnp.stack([sa, sa_count]).astype(jnp.int32)
    query = cross_query.reshape(QTAIL, GROUP, HEAD).transpose(1, 0, 2).reshape(GROUP * QTAIL, HEAD)
    parts = cross_attention(first, span_ids, seg_lengths, query, keyval)
    with jax.named_scope("exchange_partials"):
        parts = lax.all_to_all(parts, SA, 0, 0, tiled=True)
    return merge(parts).reshape(1, 1, GROUP * HEAD)


def solution(mesh):
    fine = Mesh(mesh.devices.reshape(2, 4, 16, 2, 2), PARTS)
    rows = P(PARTS, None)
    heads = P(None, HA, None)
    placed = (rows, rows, rows, rows, P(SA, None), P(), heads, heads, P(), P())
    return jax.shard_map(
        local, mesh=fine, in_specs=placed, out_specs=P(SA, HA, None), check_vma=False
    )
```

```python
import functools
import math

import jax
import jax.numpy as jnp
import numpy as np
from jax import lax
from jax.experimental import pallas as pl
from jax.experimental.pallas import tpu as pltpu
from jax.sharding import Mesh, PartitionSpec as P

D_ENC = 1024
ENC_HEADS = 16
ENC_HEAD = D_ENC // ENC_HEADS
KV_HEADS = 8
GROUP = 8
HEAD = 128
SEG_LEN = 256
QTAIL = 64
MASKED = -1e30

PARTS = ("yh", "x", "z", "yl", "c")
HA = ("yh", "x")
SA = ("z", "yl", "c")
PLANE = ("yh", "x", "yl")


def params(mebibytes=20):
    return pltpu.CompilerParams(vmem_limit_bytes=mebibytes * 1024 * 1024)


def dot(a, b):
    return jnp.dot(a, b, preferred_element_type=jnp.float32)


def dot_t(a, b):
    return lax.dot_general(a, b, (((1,), (1,)), ((), ())), preferred_element_type=jnp.float32)


def encoder_attention_kernel(slot_ref, span_ref, len_ref, q_ref, k_ref, v_ref, o_ref):
    valid = len_ref[span_ref[slot_ref[0]]]
    keep = lax.broadcasted_iota(jnp.int32, (1, SEG_LEN), 1) < valid
    bias = jnp.where(keep, 0.0, MASKED).astype(jnp.float32)
    low = lax.broadcasted_iota(jnp.int32, (SEG_LEN, 2 * ENC_HEAD), 1) < ENC_HEAD
    scale = math.log2(math.e) / math.sqrt(ENC_HEAD)
    for pair in range(ENC_HEADS // 2):
        cols = slice(pair * 2 * ENC_HEAD, (pair + 1) * 2 * ENC_HEAD)
        q, k, v = q_ref[:, cols], k_ref[:, cols], v_ref[:, cols]
        zero = jnp.zeros_like(k)
        parts = []
        for mine in (low, jnp.logical_not(low)):
            scores = dot_t(q, jnp.where(mine, k, zero)) + bias
            expo = jnp.exp2((scores - jnp.max(scores, axis=-1, keepdims=True)) * scale)
            probs = (expo * (1.0 / jnp.sum(expo, axis=-1, keepdims=True))).astype(jnp.bfloat16)
            parts.append(dot(probs, v))
        o_ref[:, cols] = jnp.where(low, parts[0], parts[1]).astype(jnp.bfloat16)


def encoder_attention(slot, span_ids, seg_lengths, q, k, v):
    smem = pl.BlockSpec(memory_space=pltpu.SMEM)
    vmem = pl.BlockSpec(memory_space=pltpu.VMEM)
    return pl.pallas_call(
        encoder_attention_kernel,
        out_shape=jax.ShapeDtypeStruct((SEG_LEN, D_ENC), jnp.bfloat16),
        in_specs=[smem, smem, smem, vmem, vmem, vmem],
        out_specs=vmem,
        compiler_params=params(),
        cost_estimate=pl.CostEstimate(
            flops=8 * SEG_LEN * SEG_LEN * D_ENC, bytes_accessed=8 * SEG_LEN * D_ENC,
            transcendentals=SEG_LEN * SEG_LEN * ENC_HEADS),
        name="encoder_attention",
    )(slot, span_ids, seg_lengths, q, k, v)


def encode_kernel(place_ref, gain_ref, ctx_ref, resid_ref, mine_ref, other_ref, *refs):
    kv_refs, o_ref = refs[:6], refs[6]
    w_ref, enc_ref, done_ref = refs[7:10]
    kv_bufs, in_sems, out_sems = refs[10:14], refs[14], refs[15]
    z, core, odd = place_ref[0], place_ref[1], place_ref[2]
    copies = []
    for side in range(2):
        some = pl.ds(8 * side, 8)
        sources = [kv_refs[0].at[some], kv_refs[1].at[some], kv_refs[2 + side], kv_refs[4 + side]]
        copies.append([pltpu.make_async_copy(source, kv_bufs[i].at[some], in_sems.at[4 * side + i])
                       for i, source in enumerate(sources)])
    for side in range(2):
        for copy in copies[side]:
            copy.start()

    for part_ref, at in ((mine_ref, core), (other_ref, 1 - core)):
        for ha in range(KV_HEADS):
            plane = lax.rem(z + 32 - ha - 8 * at, 16)
            for yl in range(2):
                for c in range(2):
                    row = pl.multiple_of(64 * plane + 32 * yl + 16 * c, 16)
                    w_ref[:, pl.ds(row, 16), :] = part_ref[ha * 2 + yl, c]
    ctx = ctx_ref[...]
    hidden = jnp.concatenate(
        [dot(ctx, jnp.concatenate([w_ref[2 * j], w_ref[2 * j + 1]], axis=1)) for j in range(4)], axis=1)
    hidden = hidden + resid_ref[...].astype(jnp.float32)
    factor = lax.rsqrt(jnp.mean(hidden * hidden, axis=-1, keepdims=True) + 1e-05)
    encoded = (hidden * factor * gain_ref[...]).astype(jnp.bfloat16)
    for piece in range(4):
        enc_ref[piece] = encoded[:, piece * 256:(piece + 1) * 256]
    near, far = 2 * core, 2 - 2 * core
    pieces = [enc_ref[near + odd], enc_ref[near + 1 - odd], enc_ref[far + odd], enc_ref[far + 1 - odd]]

    def rows(ref, h):
        return jnp.concatenate(
            [jnp.concatenate([ref[2 * h + yl, :128], ref[2 * h + yl, 128:]], axis=1) for yl in range(2)], axis=0)

    sends = []
    for h in range(KV_HEADS):
        if h % 4 == 0:
            for copy in copies[h // 4]:
                copy.wait()
        total = dot(pieces[0], rows(kv_bufs[0], h))
        for i in range(1, 4):
            total += dot(pieces[i], rows(kv_bufs[i], h))
        done_ref[h, :SEG_LEN] = total[:, :HEAD].astype(jnp.bfloat16)
        done_ref[h, SEG_LEN:] = total[:, HEAD:].astype(jnp.bfloat16)
        sends.append(pltpu.make_async_copy(done_ref.at[h], o_ref.at[h], out_sems.at[h]))
        sends[h].start()
    for send in sends:
        send.wait()


def encode(place, gain, ctx, resid, mine, other, kvs):
    smem = pl.BlockSpec(memory_space=pltpu.SMEM)
    vmem = pl.BlockSpec(memory_space=pltpu.VMEM)
    hbm = pl.BlockSpec(memory_space=pltpu.HBM)
    shape = jax.ShapeDtypeStruct((KV_HEADS, 2 * SEG_LEN, HEAD), jnp.bfloat16)
    return pl.pallas_call(
        encode_kernel,
        out_shape=shape,
        in_specs=[smem] + [vmem] * 5 + [hbm] * 6,
        out_specs=hbm,
        scratch_shapes=[pltpu.VMEM((8, D_ENC, HEAD), jnp.bfloat16),
                        pltpu.VMEM((4, SEG_LEN, 256), jnp.bfloat16),
                        pltpu.VMEM(shape.shape, shape.dtype)]
        + [pltpu.VMEM(kvs[0].shape, kvs[0].dtype)] * 4
        + [pltpu.SemaphoreType.DMA((8,)), pltpu.SemaphoreType.DMA((KV_HEADS,))],
        compiler_params=params(47),
        cost_estimate=pl.CostEstimate(
            flops=6 * SEG_LEN * D_ENC * D_ENC, bytes_accessed=8 * D_ENC * D_ENC, transcendentals=SEG_LEN),
        name="encode_keyval",
    )(place, gain, ctx, resid, mine, other, *kvs)


def cross_kernel(slots, first_ref, span_ref, len_ref, q_ref, kv_ref, o_ref):
    scale = 1.0 / math.sqrt(HEAD)
    lane = lax.broadcasted_iota(jnp.int32, (1, SEG_LEN), 1)
    bias = []
    for s in range(slots):
        valid = len_ref[span_ref[first_ref[0] + s * first_ref[1]]]
        bias.append(jnp.where(lane < valid, 0.0, MASKED).astype(jnp.float32))
    bias = jnp.concatenate(bias, axis=1)
    keys = kv_ref[:, :SEG_LEN].reshape(slots * SEG_LEN, HEAD)
    values = kv_ref[:, SEG_LEN:].reshape(slots * SEG_LEN, HEAD)
    rows = 2 * QTAIL
    column = lax.broadcasted_iota(jnp.int32, (rows, HEAD), 1)
    levels = jnp.zeros((rows, HEAD), jnp.float32)

    def put(at, block):
        block = block.reshape(2, QTAIL, HEAD)
        o_ref[:, :, at * HEAD:(at + 1) * HEAD] = jnp.stack([block[0], block[1]], axis=1).astype(jnp.bfloat16)

    for b in range(GROUP // 2):
        q = q_ref[b * rows:(b + 1) * rows]
        scores = dot_t(q, keys) + bias
        top = jnp.max(scores, axis=-1, keepdims=True)
        expo = jnp.exp2((scores - top) * (scale * math.log2(math.e)))
        total = jnp.sum(expo, axis=-1, keepdims=True)
        put(b, dot(expo.astype(jnp.bfloat16), values) / total)
        level = jnp.broadcast_to(top * scale + jnp.log(total), (rows, HEAD))
        high = level.astype(jnp.bfloat16).astype(jnp.float32)
        middle = (level - high).astype(jnp.bfloat16).astype(jnp.float32)
        rest = level - high - middle
        for k, part in enumerate((high, middle, rest)):
            levels = jnp.where(column == 3 * b + k, part, levels)
    put(GROUP // 2, levels)


def cross_attention(first, span_ids, seg_lengths, q, kv):
    smem = pl.BlockSpec(memory_space=pltpu.SMEM)
    vmem = pl.BlockSpec(memory_space=pltpu.VMEM)
    slots = kv.shape[0]
    return pl.pallas_call(
        functools.partial(cross_kernel, slots),
        out_shape=jax.ShapeDtypeStruct((QTAIL, 2, 640), jnp.bfloat16),
        in_specs=[smem, smem, smem, vmem, vmem],
        out_specs=vmem,
        compiler_params=params(),
        name="cross_attention",
    )(first, span_ids, seg_lengths, q, kv)


def merge_kernel(part_ref, o_ref):
    pieces = part_ref[:, :, 4 * HEAD:].astype(jnp.float32)
    level = pieces + pltpu.roll(pieces, HEAD - 1, 2) + pltpu.roll(pieces, HEAD - 2, 2)
    weight = jnp.exp(level - jnp.max(level, axis=0, keepdims=True))
    total = jnp.sum(weight, axis=0)
    for b in range(GROUP // 2):
        average = part_ref[:, :, HEAD * b:HEAD * (b + 1)].astype(jnp.float32)
        at = slice(3 * b, 3 * b + 1)
        o_ref[2 * b:2 * b + 2] = jnp.sum(average * weight[:, :, at], axis=0) / total[:, at]


def merge(parts):
    vmem = pl.BlockSpec(memory_space=pltpu.VMEM)
    return pl.pallas_call(
        merge_kernel,
        out_shape=jax.ShapeDtypeStruct((GROUP, HEAD), jnp.float32),
        in_specs=[vmem],
        out_specs=vmem,
        name="merge_partials",
    )(parts)


def spread(block, axes):
    count = lax.axis_size(axes)
    copies = jnp.broadcast_to(block[None], (count,) + block.shape)
    return lax.all_to_all(copies, axes, 0, 0, tiled=True)


def local(enc_query, enc_key, enc_value, enc_resid, out_weight, norm_gain, kv_weight, cross_query,
          span_ids, seg_lengths):
    ha = lax.axis_index(HA)
    sa = lax.axis_index(SA)
    sa_count = lax.axis_size(SA)
    core = lax.axis_index("c")

    yl, z = lax.axis_index("yl"), lax.axis_index("z")
    swap = functools.partial(lax.ppermute, axis_name="c", perm=[(0, 1), (1, 0)])

    odd = lax.rem(z, 2)

    with jax.named_scope("pair_out_weight"):
        pair = lax.all_gather(out_weight.reshape(16, 8, HEAD).transpose(1, 0, 2), "c")
    with jax.named_scope("gather_kv_weight"):
        eighth = lax.dynamic_slice_in_dim(
            kv_weight.reshape(D_ENC, 2 * HEAD), core * 512 + odd * 256 + yl * 128, 128, 0)
        pair, eighth = lax.optimization_barrier((pair, eighth))
        kv_mine = spread(jnp.concatenate([eighth[:, :HEAD], eighth[:, HEAD:]], axis=0), PLANE)
    with jax.named_scope("out_weight_over_z"):
        hops = []
        for ha_at in range(8):
            for z_at in range(16):
                for c_at in range(2):
                    there = (z_at + ha_at + 8 * c_at) % 16
                    hops.append(((ha_at * 16 + z_at) * 2 + c_at, (ha_at * 16 + there) * 2 + c_at))
        pair = lax.ppermute(pair, ("yh", "x", "z", "c"), hops)
    slot = (ha * sa_count + sa).reshape(1).astype(jnp.int32)
    context = encoder_attention(slot, span_ids, seg_lengths, enc_query, enc_key, enc_value)
    kv_mine, pair, context = lax.optimization_barrier((kv_mine, pair, context))
    with jax.named_scope("out_weight_over_plane"):
        w_mine = spread(pair, PLANE)
    with jax.named_scope("kv_weight_over_z"):
        pairs = []
        for z_at in range(16):
            for c_at in range(2):
                there = (z_at + (1 if (z_at + c_at) % 2 == 0 else 15)) % 16
                pairs.append((2 * z_at + c_at, 2 * there + c_at))
        kv_next = lax.ppermute(kv_mine, ("z", "c"), pairs)
    with jax.named_scope("swap_weights"):
        kvs = [kv_mine, kv_next]
        kvs = kvs + [swap(part) for kv in kvs for part in (kv[:8], kv[8:])]
        w_mine, kvs = lax.optimization_barrier((w_mine, kvs))
        w_other = swap(w_mine)
    place = jnp.stack([z, core, odd]).astype(jnp.int32)
    keyval = encode(place, norm_gain.reshape(1, D_ENC), context, enc_resid, w_mine, w_other, kvs)
    with jax.named_scope("exchange_keyval"):
        keyval = lax.all_to_all(keyval, HA, 0, 0, tiled=True)
    first = jnp.stack([sa, sa_count]).astype(jnp.int32)
    query = cross_query.reshape(QTAIL, GROUP, HEAD).transpose(1, 0, 2).reshape(GROUP * QTAIL, HEAD)
    parts = cross_attention(first, span_ids, seg_lengths, query, keyval)
    with jax.named_scope("exchange_partials"):
        parts = lax.all_to_all(parts, SA, 0, 0, tiled=True)
    return merge(parts).reshape(1, 1, GROUP * HEAD)


def solution(mesh):
    fine = Mesh(mesh.devices.reshape(2, 4, 16, 2, 2), PARTS)
    rows = P(PARTS, None)
    heads = P(None, HA, None)
    placed = (rows, rows, rows, rows, P(SA, None), P(), heads, heads, P(), P())
    return jax.shard_map(
        local, mesh=fine, in_specs=placed, out_specs=P(SA, HA, None), check_vma=False
    )
```

```python
import functools
import math

import jax
import jax.numpy as jnp
import numpy as np
from jax import lax
from jax.experimental import pallas as pl
from jax.experimental.pallas import tpu as pltpu
from jax.sharding import Mesh, PartitionSpec as P

D_ENC = 1024
ENC_HEADS = 16
ENC_HEAD = D_ENC // ENC_HEADS
KV_HEADS = 8
GROUP = 8
HEAD = 128
SEG_LEN = 256
QTAIL = 64
MASKED = -1e30
CUT = 14

PARTS = ("yh", "x", "z", "yl", "c")
HA = ("yh", "x")
SA = ("z", "yl", "c")
PLANE = ("yh", "x", "yl")


def params(mebibytes=20):
    return pltpu.CompilerParams(vmem_limit_bytes=mebibytes * 1024 * 1024)


def dot(a, b):
    return jnp.dot(a, b, preferred_element_type=jnp.float32)


def dot_t(a, b):
    return lax.dot_general(a, b, (((1,), (1,)), ((), ())), preferred_element_type=jnp.float32)


def encoder_attention_kernel(slot_ref, span_ref, len_ref, q_ref, k_ref, v_ref, o_ref):
    valid = len_ref[span_ref[slot_ref[0]]]
    keep = lax.broadcasted_iota(jnp.int32, (1, SEG_LEN), 1) < valid
    bias = jnp.where(keep, 0.0, MASKED).astype(jnp.float32)
    low = lax.broadcasted_iota(jnp.int32, (SEG_LEN, 2 * ENC_HEAD), 1) < ENC_HEAD
    scale = math.log2(math.e) / math.sqrt(ENC_HEAD)
    for pair in range(ENC_HEADS // 2):
        cols = slice(pair * 2 * ENC_HEAD, (pair + 1) * 2 * ENC_HEAD)
        q, k, v = q_ref[:, cols], k_ref[:, cols], v_ref[:, cols]
        zero = jnp.zeros_like(k)
        parts = []
        for mine in (low, jnp.logical_not(low)):
            scores = dot_t(q, jnp.where(mine, k, zero)) + bias
            expo = jnp.exp2((scores - jnp.max(scores, axis=-1, keepdims=True)) * scale)
            probs = (expo * (1.0 / jnp.sum(expo, axis=-1, keepdims=True))).astype(jnp.bfloat16)
            parts.append(dot(probs, v))
        o_ref[:, cols] = jnp.where(low, parts[0], parts[1]).astype(jnp.bfloat16)


def encoder_attention(slot, span_ids, seg_lengths, q, k, v):
    smem = pl.BlockSpec(memory_space=pltpu.SMEM)
    vmem = pl.BlockSpec(memory_space=pltpu.VMEM)
    return pl.pallas_call(
        encoder_attention_kernel,
        out_shape=jax.ShapeDtypeStruct((SEG_LEN, D_ENC), jnp.bfloat16),
        in_specs=[smem, smem, smem, vmem, vmem, vmem],
        out_specs=vmem,
        compiler_params=params(),
        cost_estimate=pl.CostEstimate(
            flops=8 * SEG_LEN * SEG_LEN * D_ENC, bytes_accessed=8 * SEG_LEN * D_ENC,
            transcendentals=SEG_LEN * SEG_LEN * ENC_HEADS),
        name="encoder_attention",
    )(slot, span_ids, seg_lengths, q, k, v)


def encode_kernel(place_ref, gain_ref, ctx_ref, resid_ref, mine_ref, other_ref, *refs):
    kv_refs, o_ref = refs[:6], refs[6]
    w_ref, enc_ref, done_ref = refs[7:10]
    kv_bufs, in_sems, out_sems = refs[10:14], refs[14], refs[15]
    z, core, odd = place_ref[0], place_ref[1], place_ref[2]
    copies = []
    for side in range(2):
        some = pl.ds(8 * side, 8)
        moves = [(kv_refs[i].at[some], kv_bufs[i].at[some]) for i in range(2)]
        for i in range(2):
            first, last = kv_refs[2 + 2 * i], kv_refs[3 + 2 * i]
            if side == 0:
                moves.append((first.at[some], kv_bufs[2 + i].at[some]))
            else:
                moves.append((first.at[pl.ds(8, CUT - 8)], kv_bufs[2 + i].at[pl.ds(8, CUT - 8)]))
                moves.append((last, kv_bufs[2 + i].at[pl.ds(CUT, 16 - CUT)]))
        copies.append([pltpu.make_async_copy(source, target, in_sems.at[4 * side + i])
                       for i, (source, target) in enumerate(moves)])
    for side in range(2):
        for copy in copies[side]:
            copy.start()

    for part_ref, at in ((mine_ref, core), (other_ref, 1 - core)):
        for ha in range(KV_HEADS):
            plane = lax.rem(z + 32 - ha - 8 * at, 16)
            for yl in range(2):
                for c in range(2):
                    row = pl.multiple_of(64 * plane + 32 * yl + 16 * c, 16)
                    w_ref[:, pl.ds(row, 16), :] = part_ref[ha * 2 + yl, c]
    ctx = ctx_ref[...]
    hidden = jnp.concatenate(
        [dot(ctx, jnp.concatenate([w_ref[2 * j], w_ref[2 * j + 1]], axis=1)) for j in range(4)], axis=1)
    hidden = hidden + resid_ref[...].astype(jnp.float32)
    factor = lax.rsqrt(jnp.mean(hidden * hidden, axis=-1, keepdims=True) + 1e-05)
    encoded = (hidden * factor * gain_ref[...]).astype(jnp.bfloat16)
    for piece in range(4):
        enc_ref[piece] = encoded[:, piece * 256:(piece + 1) * 256]
    near, far = 2 * core, 2 - 2 * core
    pieces = [enc_ref[near + odd], enc_ref[near + 1 - odd], enc_ref[far + odd], enc_ref[far + 1 - odd]]

    def rows(ref, h):
        return jnp.concatenate(
            [jnp.concatenate([ref[2 * h + yl, :128], ref[2 * h + yl, 128:]], axis=1) for yl in range(2)], axis=0)

    sends = []
    for h in range(KV_HEADS):
        if h % 4 == 0:
            for copy in copies[h // 4]:
                copy.wait()
        total = dot(pieces[0], rows(kv_bufs[0], h))
        for i in range(1, 4):
            total += dot(pieces[i], rows(kv_bufs[i], h))
        done_ref[h, :SEG_LEN] = total[:, :HEAD].astype(jnp.bfloat16)
        done_ref[h, SEG_LEN:] = total[:, HEAD:].astype(jnp.bfloat16)
        sends.append(pltpu.make_async_copy(done_ref.at[h], o_ref.at[h], out_sems.at[h]))
        sends[h].start()
    for send in sends:
        send.wait()


def encode(place, gain, ctx, resid, mine, other, kvs):
    smem = pl.BlockSpec(memory_space=pltpu.SMEM)
    vmem = pl.BlockSpec(memory_space=pltpu.VMEM)
    hbm = pl.BlockSpec(memory_space=pltpu.HBM)
    shape = jax.ShapeDtypeStruct((KV_HEADS, 2 * SEG_LEN, HEAD), jnp.bfloat16)
    return pl.pallas_call(
        encode_kernel,
        out_shape=shape,
        in_specs=[smem] + [vmem] * 5 + [hbm] * 6,
        out_specs=hbm,
        scratch_shapes=[pltpu.VMEM((8, D_ENC, HEAD), jnp.bfloat16),
                        pltpu.VMEM((4, SEG_LEN, 256), jnp.bfloat16),
                        pltpu.VMEM(shape.shape, shape.dtype)]
        + [pltpu.VMEM(kvs[0].shape, kvs[0].dtype)] * 4
        + [pltpu.SemaphoreType.DMA((10,)), pltpu.SemaphoreType.DMA((KV_HEADS,))],
        compiler_params=params(47),
        cost_estimate=pl.CostEstimate(
            flops=6 * SEG_LEN * D_ENC * D_ENC, bytes_accessed=8 * D_ENC * D_ENC, transcendentals=SEG_LEN),
        name="encode_keyval",
    )(place, gain, ctx, resid, mine, other, *kvs)


def cross_kernel(slots, first_ref, span_ref, len_ref, q_ref, kv_ref, o_ref):
    scale = 1.0 / math.sqrt(HEAD)
    lane = lax.broadcasted_iota(jnp.int32, (1, SEG_LEN), 1)
    bias = []
    for s in range(slots):
        valid = len_ref[span_ref[first_ref[0] + s * first_ref[1]]]
        bias.append(jnp.where(lane < valid, 0.0, MASKED).astype(jnp.float32))
    bias = jnp.concatenate(bias, axis=1)
    keys = kv_ref[:, :SEG_LEN].reshape(slots * SEG_LEN, HEAD)
    values = kv_ref[:, SEG_LEN:].reshape(slots * SEG_LEN, HEAD)
    rows = 2 * QTAIL
    column = lax.broadcasted_iota(jnp.int32, (rows, HEAD), 1)
    levels = jnp.zeros((rows, HEAD), jnp.float32)

    def put(at, block):
        block = block.reshape(2, QTAIL, HEAD)
        o_ref[:, :, at * HEAD:(at + 1) * HEAD] = jnp.stack([block[0], block[1]], axis=1).astype(jnp.bfloat16)

    for b in range(GROUP // 2):
        q = q_ref[b * rows:(b + 1) * rows]
        scores = dot_t(q, keys) + bias
        top = jnp.max(scores, axis=-1, keepdims=True)
        expo = jnp.exp2((scores - top) * (scale * math.log2(math.e)))
        total = jnp.sum(expo, axis=-1, keepdims=True)
        put(b, dot(expo.astype(jnp.bfloat16), values) / total)
        level = jnp.broadcast_to(top * scale + jnp.log(total), (rows, HEAD))
        high = level.astype(jnp.bfloat16).astype(jnp.float32)
        middle = (level - high).astype(jnp.bfloat16).astype(jnp.float32)
        rest = level - high - middle
        for k, part in enumerate((high, middle, rest)):
            levels = jnp.where(column == 3 * b + k, part, levels)
    put(GROUP // 2, levels)


def cross_attention(first, span_ids, seg_lengths, q, kv):
    smem = pl.BlockSpec(memory_space=pltpu.SMEM)
    vmem = pl.BlockSpec(memory_space=pltpu.VMEM)
    slots = kv.shape[0]
    return pl.pallas_call(
        functools.partial(cross_kernel, slots),
        out_shape=jax.ShapeDtypeStruct((QTAIL, 2, 640), jnp.bfloat16),
        in_specs=[smem, smem, smem, vmem, vmem],
        out_specs=vmem,
        compiler_params=params(),
        name="cross_attention",
    )(first, span_ids, seg_lengths, q, kv)


def merge_kernel(part_ref, o_ref):
    pieces = part_ref[:, :, 4 * HEAD:].astype(jnp.float32)
    level = pieces + pltpu.roll(pieces, HEAD - 1, 2) + pltpu.roll(pieces, HEAD - 2, 2)
    weight = jnp.exp(level - jnp.max(level, axis=0, keepdims=True))
    total = jnp.sum(weight, axis=0)
    for b in range(GROUP // 2):
        average = part_ref[:, :, HEAD * b:HEAD * (b + 1)].astype(jnp.float32)
        at = slice(3 * b, 3 * b + 1)
        o_ref[2 * b:2 * b + 2] = jnp.sum(average * weight[:, :, at], axis=0) / total[:, at]


def merge(parts):
    vmem = pl.BlockSpec(memory_space=pltpu.VMEM)
    return pl.pallas_call(
        merge_kernel,
        out_shape=jax.ShapeDtypeStruct((GROUP, HEAD), jnp.float32),
        in_specs=[vmem],
        out_specs=vmem,
        name="merge_partials",
    )(parts)


def spread(block, axes):
    count = lax.axis_size(axes)
    copies = jnp.broadcast_to(block[None], (count,) + block.shape)
    return lax.all_to_all(copies, axes, 0, 0, tiled=True)


def local(enc_query, enc_key, enc_value, enc_resid, out_weight, norm_gain, kv_weight, cross_query,
          span_ids, seg_lengths):
    ha = lax.axis_index(HA)
    sa = lax.axis_index(SA)
    sa_count = lax.axis_size(SA)
    core = lax.axis_index("c")

    yl, z = lax.axis_index("yl"), lax.axis_index("z")
    swap = functools.partial(lax.ppermute, axis_name="c", perm=[(0, 1), (1, 0)])

    odd = lax.rem(z, 2)

    with jax.named_scope("pair_out_weight"):
        pair = lax.all_gather(out_weight.reshape(16, 8, HEAD).transpose(1, 0, 2), "c")
    with jax.named_scope("gather_kv_weight"):
        eighth = lax.dynamic_slice_in_dim(
            kv_weight.reshape(D_ENC, 2 * HEAD), core * 512 + odd * 256 + yl * 128, 128, 0)
        kv_mine = spread(jnp.concatenate([eighth[:, :HEAD], eighth[:, HEAD:]], axis=0), PLANE)
    with jax.named_scope("out_weight_over_z"):
        hops = []
        for ha_at in range(8):
            for z_at in range(16):
                for c_at in range(2):
                    there = (z_at + ha_at + 8 * c_at) % 16
                    hops.append(((ha_at * 16 + z_at) * 2 + c_at, (ha_at * 16 + there) * 2 + c_at))
        pair = lax.ppermute(pair, ("yh", "x", "z", "c"), hops)
    slot = (ha * sa_count + sa).reshape(1).astype(jnp.int32)
    context = encoder_attention(slot, span_ids, seg_lengths, enc_query, enc_key, enc_value)
    kv_mine, pair, context = lax.optimization_barrier((kv_mine, pair, context))
    with jax.named_scope("out_weight_over_plane"):
        w_mine = spread(pair, PLANE)
    with jax.named_scope("kv_weight_over_z"):
        pairs = []
        for z_at in range(16):
            for c_at in range(2):
                there = (z_at + (1 if (z_at + c_at) % 2 == 0 else 15)) % 16
                pairs.append((2 * z_at + c_at, 2 * there + c_at))
        kv_next = lax.ppermute(kv_mine, ("z", "c"), pairs)
    with jax.named_scope("swap_weights"):
        kvs = [kv_mine, kv_next]
        kvs = kvs + [swap(part) for kv in kvs for part in (kv[:CUT], kv[CUT:])]
        w_mine, kvs = lax.optimization_barrier((w_mine, kvs))
        w_other = swap(w_mine)
    place = jnp.stack([z, core, odd]).astype(jnp.int32)
    keyval = encode(place, norm_gain.reshape(1, D_ENC), context, enc_resid, w_mine, w_other, kvs)
    with jax.named_scope("exchange_keyval"):
        keyval = lax.all_to_all(keyval, HA, 0, 0, tiled=True)
    first = jnp.stack([sa, sa_count]).astype(jnp.int32)
    query = cross_query.reshape(QTAIL, GROUP, HEAD).transpose(1, 0, 2).reshape(GROUP * QTAIL, HEAD)
    parts = cross_attention(first, span_ids, seg_lengths, query, keyval)
    with jax.named_scope("exchange_partials"):
        parts = lax.all_to_all(parts, SA, 0, 0, tiled=True)
    return merge(parts).reshape(1, 1, GROUP * HEAD)


def solution(mesh):
    fine = Mesh(mesh.devices.reshape(2, 4, 16, 2, 2), PARTS)
    rows = P(PARTS, None)
    heads = P(None, HA, None)
    placed = (rows, rows, rows, rows, P(SA, None), P(), heads, heads, P(), P())
    return jax.shard_map(
        local, mesh=fine, in_specs=placed, out_specs=P(SA, HA, None), check_vma=False
    )
```

```python
import functools
import math

import jax
import jax.numpy as jnp
import numpy as np
from jax import lax
from jax.experimental import pallas as pl
from jax.experimental.pallas import tpu as pltpu
from jax.sharding import Mesh, PartitionSpec as P

D_ENC = 1024
ENC_HEADS = 16
ENC_HEAD = D_ENC // ENC_HEADS
KV_HEADS = 8
GROUP = 8
HEAD = 128
SEG_LEN = 256
QTAIL = 64
MASKED = -1e30

PARTS = ("yh", "x", "z", "yl", "c")
HA = ("yh", "x")
SA = ("z", "yl", "c")
PLANE = ("yh", "x", "yl")


def params(mebibytes=20):
    return pltpu.CompilerParams(vmem_limit_bytes=mebibytes * 1024 * 1024)


def dot(a, b):
    return jnp.dot(a, b, preferred_element_type=jnp.float32)


def dot_t(a, b):
    return lax.dot_general(a, b, (((1,), (1,)), ((), ())), preferred_element_type=jnp.float32)


def encoder_attention_kernel(slot_ref, span_ref, len_ref, q_ref, k_ref, v_ref, o_ref):
    valid = len_ref[span_ref[slot_ref[0]]]
    keep = lax.broadcasted_iota(jnp.int32, (1, SEG_LEN), 1) < valid
    bias = jnp.where(keep, 0.0, MASKED).astype(jnp.float32)
    low = lax.broadcasted_iota(jnp.int32, (SEG_LEN, 2 * ENC_HEAD), 1) < ENC_HEAD
    scale = math.log2(math.e) / math.sqrt(ENC_HEAD)
    for pair in range(ENC_HEADS // 2):
        cols = slice(pair * 2 * ENC_HEAD, (pair + 1) * 2 * ENC_HEAD)
        q, k, v = q_ref[:, cols], k_ref[:, cols], v_ref[:, cols]
        zero = jnp.zeros_like(k)
        parts = []
        for mine in (low, jnp.logical_not(low)):
            scores = dot_t(q, jnp.where(mine, k, zero)) + bias
            expo = jnp.exp2((scores - jnp.max(scores, axis=-1, keepdims=True)) * scale)
            probs = (expo * (1.0 / jnp.sum(expo, axis=-1, keepdims=True))).astype(jnp.bfloat16)
            parts.append(dot(probs, v))
        o_ref[:, cols] = jnp.where(low, parts[0], parts[1]).astype(jnp.bfloat16)


def encoder_attention(slot, span_ids, seg_lengths, q, k, v):
    smem = pl.BlockSpec(memory_space=pltpu.SMEM)
    vmem = pl.BlockSpec(memory_space=pltpu.VMEM)
    return pl.pallas_call(
        encoder_attention_kernel,
        out_shape=jax.ShapeDtypeStruct((SEG_LEN, D_ENC), jnp.bfloat16),
        in_specs=[smem, smem, smem, vmem, vmem, vmem],
        out_specs=vmem,
        compiler_params=params(),
        cost_estimate=pl.CostEstimate(
            flops=8 * SEG_LEN * SEG_LEN * D_ENC, bytes_accessed=8 * SEG_LEN * D_ENC,
            transcendentals=SEG_LEN * SEG_LEN * ENC_HEADS),
        name="encoder_attention",
    )(slot, span_ids, seg_lengths, q, k, v)


def encode_kernel(place_ref, gain_ref, ctx_ref, resid_ref, mine_ref, other_ref, *refs):
    kv_refs, o_ref = refs[:5], refs[5]
    w_ref, enc_ref, done_ref = refs[6:9]
    kv_bufs, in_sems, out_sems = refs[9:13], refs[13], refs[14]
    z, core, odd = place_ref[0], place_ref[1], place_ref[2]
    copies = []
    for side in range(2):
        some = pl.ds(8 * side, 8)
        sources = [kv_refs[0].at[some], kv_refs[1].at[some], kv_refs[2].at[some], kv_refs[3 + side]]
        copies.append([pltpu.make_async_copy(source, kv_bufs[i].at[some], in_sems.at[4 * side + i])
                       for i, source in enumerate(sources)])
    for side in range(2):
        for copy in copies[side]:
            copy.start()

    for part_ref, at in ((mine_ref, core), (other_ref, 1 - core)):
        for ha in range(KV_HEADS):
            plane = lax.rem(z + 32 - ha - 8 * at, 16)
            for yl in range(2):
                for c in range(2):
                    row = pl.multiple_of(64 * plane + 32 * yl + 16 * c, 16)
                    w_ref[:, pl.ds(row, 16), :] = part_ref[ha * 2 + yl, c]
    ctx = ctx_ref[...]
    hidden = jnp.concatenate(
        [dot(ctx, jnp.concatenate([w_ref[2 * j], w_ref[2 * j + 1]], axis=1)) for j in range(4)], axis=1)
    hidden = hidden + resid_ref[...].astype(jnp.float32)
    factor = lax.rsqrt(jnp.mean(hidden * hidden, axis=-1, keepdims=True) + 1e-05)
    encoded = (hidden * factor * gain_ref[...]).astype(jnp.bfloat16)
    for piece in range(4):
        enc_ref[piece] = encoded[:, piece * 256:(piece + 1) * 256]
    near, far = 2 * core, 2 - 2 * core
    pieces = [enc_ref[near + odd], enc_ref[near + 1 - odd], enc_ref[far + odd], enc_ref[far + 1 - odd]]

    def rows(ref, h):
        return jnp.concatenate(
            [jnp.concatenate([ref[2 * h + yl, :128], ref[2 * h + yl, 128:]], axis=1) for yl in range(2)], axis=0)

    sends = []
    for h in range(KV_HEADS):
        if h % 4 == 0:
            for copy in copies[h // 4]:
                copy.wait()
        total = dot(pieces[0], rows(kv_bufs[0], h))
        for i in range(1, 4):
            total += dot(pieces[i], rows(kv_bufs[i], h))
        done_ref[h, :SEG_LEN] = total[:, :HEAD].astype(jnp.bfloat16)
        done_ref[h, SEG_LEN:] = total[:, HEAD:].astype(jnp.bfloat16)
        sends.append(pltpu.make_async_copy(done_ref.at[h], o_ref.at[h], out_sems.at[h]))
        sends[h].start()
    for send in sends:
        send.wait()


def encode(place, gain, ctx, resid, mine, other, kvs):
    smem = pl.BlockSpec(memory_space=pltpu.SMEM)
    vmem = pl.BlockSpec(memory_space=pltpu.VMEM)
    hbm = pl.BlockSpec(memory_space=pltpu.HBM)
    shape = jax.ShapeDtypeStruct((KV_HEADS, 2 * SEG_LEN, HEAD), jnp.bfloat16)
    return pl.pallas_call(
        encode_kernel,
        out_shape=shape,
        in_specs=[smem] + [vmem] * 5 + [hbm] * 5,
        out_specs=hbm,
        scratch_shapes=[pltpu.VMEM((8, D_ENC, HEAD), jnp.bfloat16),
                        pltpu.VMEM((4, SEG_LEN, 256), jnp.bfloat16),
                        pltpu.VMEM(shape.shape, shape.dtype)]
        + [pltpu.VMEM(kvs[0].shape, kvs[0].dtype)] * 4
        + [pltpu.SemaphoreType.DMA((8,)), pltpu.SemaphoreType.DMA((KV_HEADS,))],
        compiler_params=params(48),
        cost_estimate=pl.CostEstimate(
            flops=6 * SEG_LEN * D_ENC * D_ENC, bytes_accessed=8 * D_ENC * D_ENC, transcendentals=SEG_LEN),
        name="encode_keyval",
    )(place, gain, ctx, resid, mine, other, *kvs)


def cross_kernel(slots, first_ref, span_ref, len_ref, q_ref, kv_ref, o_ref):
    scale = 1.0 / math.sqrt(HEAD)
    lane = lax.broadcasted_iota(jnp.int32, (1, SEG_LEN), 1)
    bias = []
    for s in range(slots):
        valid = len_ref[span_ref[first_ref[0] + s * first_ref[1]]]
        bias.append(jnp.where(lane < valid, 0.0, MASKED).astype(jnp.float32))
    bias = jnp.concatenate(bias, axis=1)
    keys = kv_ref[:, :SEG_LEN].reshape(slots * SEG_LEN, HEAD)
    values = kv_ref[:, SEG_LEN:].reshape(slots * SEG_LEN, HEAD)
    rows = 2 * QTAIL
    column = lax.broadcasted_iota(jnp.int32, (rows, HEAD), 1)
    levels = jnp.zeros((rows, HEAD), jnp.float32)

    def put(at, block):
        block = block.reshape(2, QTAIL, HEAD)
        o_ref[:, :, at * HEAD:(at + 1) * HEAD] = jnp.stack([block[0], block[1]], axis=1).astype(jnp.bfloat16)

    for b in range(GROUP // 2):
        q = q_ref[b * rows:(b + 1) * rows]
        scores = dot_t(q, keys) + bias
        top = jnp.max(scores, axis=-1, keepdims=True)
        expo = jnp.exp2((scores - top) * (scale * math.log2(math.e)))
        total = jnp.sum(expo, axis=-1, keepdims=True)
        put(b, dot(expo.astype(jnp.bfloat16), values) / total)
        level = jnp.broadcast_to(top * scale + jnp.log(total), (rows, HEAD))
        high = level.astype(jnp.bfloat16).astype(jnp.float32)
        middle = (level - high).astype(jnp.bfloat16).astype(jnp.float32)
        rest = level - high - middle
        for k, part in enumerate((high, middle, rest)):
            levels = jnp.where(column == 3 * b + k, part, levels)
    put(GROUP // 2, levels)


def cross_attention(first, span_ids, seg_lengths, q, kv):
    smem = pl.BlockSpec(memory_space=pltpu.SMEM)
    vmem = pl.BlockSpec(memory_space=pltpu.VMEM)
    slots = kv.shape[0]
    return pl.pallas_call(
        functools.partial(cross_kernel, slots),
        out_shape=jax.ShapeDtypeStruct((QTAIL, 2, 640), jnp.bfloat16),
        in_specs=[smem, smem, smem, vmem, vmem],
        out_specs=vmem,
        compiler_params=params(),
        name="cross_attention",
    )(first, span_ids, seg_lengths, q, kv)


def merge_kernel(part_ref, o_ref):
    pieces = part_ref[:, :, 4 * HEAD:].astype(jnp.float32)
    level = pieces + pltpu.roll(pieces, HEAD - 1, 2) + pltpu.roll(pieces, HEAD - 2, 2)
    weight = jnp.exp(level - jnp.max(level, axis=0, keepdims=True))
    total = jnp.sum(weight, axis=0)
    for b in range(GROUP // 2):
        average = part_ref[:, :, HEAD * b:HEAD * (b + 1)].astype(jnp.float32)
        at = slice(3 * b, 3 * b + 1)
        o_ref[2 * b:2 * b + 2] = jnp.sum(average * weight[:, :, at], axis=0) / total[:, at]


def merge(parts):
    vmem = pl.BlockSpec(memory_space=pltpu.VMEM)
    return pl.pallas_call(
        merge_kernel,
        out_shape=jax.ShapeDtypeStruct((GROUP, HEAD), jnp.float32),
        in_specs=[vmem],
        out_specs=vmem,
        name="merge_partials",
    )(parts)


def spread(block, axes):
    count = lax.axis_size(axes)
    copies = jnp.broadcast_to(block[None], (count,) + block.shape)
    return lax.all_to_all(copies, axes, 0, 0, tiled=True)


def local(enc_query, enc_key, enc_value, enc_resid, out_weight, norm_gain, kv_weight, cross_query,
          span_ids, seg_lengths):
    ha = lax.axis_index(HA)
    sa = lax.axis_index(SA)
    sa_count = lax.axis_size(SA)
    core = lax.axis_index("c")

    yl, z = lax.axis_index("yl"), lax.axis_index("z")
    swap = functools.partial(lax.ppermute, axis_name="c", perm=[(0, 1), (1, 0)])

    odd = lax.rem(z, 2)

    with jax.named_scope("pair_out_weight"):
        pair = lax.all_gather(out_weight.reshape(16, 8, HEAD).transpose(1, 0, 2), "c")
    with jax.named_scope("gather_kv_weight"):
        eighth = lax.dynamic_slice_in_dim(
            kv_weight.reshape(D_ENC, 2 * HEAD), core * 512 + odd * 256 + yl * 128, 128, 0)
        pair, eighth = lax.optimization_barrier((pair, eighth))
        kv_mine = spread(jnp.concatenate([eighth[:, :HEAD], eighth[:, HEAD:]], axis=0), PLANE)
    with jax.named_scope("out_weight_over_z"):
        hops = []
        for ha_at in range(8):
            for z_at in range(16):
                for c_at in range(2):
                    there = (z_at + ha_at + 8 * c_at) % 16
                    hops.append(((ha_at * 16 + z_at) * 2 + c_at, (ha_at * 16 + there) * 2 + c_at))
        pair = lax.ppermute(pair, ("yh", "x", "z", "c"), hops)
    slot = (ha * sa_count + sa).reshape(1).astype(jnp.int32)
    context = encoder_attention(slot, span_ids, seg_lengths, enc_query, enc_key, enc_value)
    kv_mine, pair, context = lax.optimization_barrier((kv_mine, pair, context))
    with jax.named_scope("out_weight_over_plane"):
        w_mine = spread(pair, PLANE)
    with jax.named_scope("kv_weight_over_z"):
        pairs = []
        for z_at in range(16):
            for c_at in range(2):
                there = (z_at + (1 if (z_at + c_at) % 2 == 0 else 15)) % 16
                pairs.append((2 * z_at + c_at, 2 * there + c_at))
        kv_next = lax.ppermute(kv_mine, ("z", "c"), pairs)
    with jax.named_scope("swap_weights"):
        far = [swap(kv_next[:8]), swap(kv_next[8:])]
        w_mine, far = lax.optimization_barrier((w_mine, far))
        w_other = swap(w_mine)
        kvs = [kv_mine, kv_next, swap(kv_mine)] + far
    place = jnp.stack([z, core, odd]).astype(jnp.int32)
    keyval = encode(place, norm_gain.reshape(1, D_ENC), context, enc_resid, w_mine, w_other, kvs)
    with jax.named_scope("exchange_keyval"):
        keyval = lax.all_to_all(keyval, HA, 0, 0, tiled=True)
    first = jnp.stack([sa, sa_count]).astype(jnp.int32)
    query = cross_query.reshape(QTAIL, GROUP, HEAD).transpose(1, 0, 2).reshape(GROUP * QTAIL, HEAD)
    parts = cross_attention(first, span_ids, seg_lengths, query, keyval)
    with jax.named_scope("exchange_partials"):
        parts = lax.all_to_all(parts, SA, 0, 0, tiled=True)
    return merge(parts).reshape(1, 1, GROUP * HEAD)


def solution(mesh):
    fine = Mesh(mesh.devices.reshape(2, 4, 16, 2, 2), PARTS)
    rows = P(PARTS, None)
    heads = P(None, HA, None)
    placed = (rows, rows, rows, rows, P(SA, None), P(), heads, heads, P(), P())
    return jax.shard_map(
        local, mesh=fine, in_specs=placed, out_specs=P(SA, HA, None), check_vma=False
    )
```

```python
import functools
import math

import jax
import jax.numpy as jnp
import numpy as np
from jax import lax
from jax.experimental import pallas as pl
from jax.experimental.pallas import tpu as pltpu
from jax.sharding import Mesh, PartitionSpec as P

D_ENC = 1024
ENC_HEADS = 16
ENC_HEAD = D_ENC // ENC_HEADS
KV_HEADS = 8
GROUP = 8
HEAD = 128
SEG_LEN = 256
QTAIL = 64
MASKED = -1e30

PARTS = ("yh", "x", "z", "yl", "c")
HA = ("yh", "x")
SA = ("z", "yl", "c")
PLANE = ("yh", "x", "yl")


def params(mebibytes=20):
    return pltpu.CompilerParams(vmem_limit_bytes=mebibytes * 1024 * 1024)


def dot(a, b):
    return jnp.dot(a, b, preferred_element_type=jnp.float32)


def dot_t(a, b):
    return lax.dot_general(a, b, (((1,), (1,)), ((), ())), preferred_element_type=jnp.float32)


def encoder_attention_kernel(slot_ref, span_ref, len_ref, q_ref, k_ref, v_ref, o_ref):
    valid = len_ref[span_ref[slot_ref[0]]]
    keep = lax.broadcasted_iota(jnp.int32, (1, SEG_LEN), 1) < valid
    bias = jnp.where(keep, 0.0, MASKED).astype(jnp.float32)
    low = lax.broadcasted_iota(jnp.int32, (SEG_LEN, 2 * ENC_HEAD), 1) < ENC_HEAD
    scale = math.log2(math.e) / math.sqrt(ENC_HEAD)
    for pair in range(ENC_HEADS // 2):
        cols = slice(pair * 2 * ENC_HEAD, (pair + 1) * 2 * ENC_HEAD)
        q, k, v = q_ref[:, cols], k_ref[:, cols], v_ref[:, cols]
        zero = jnp.zeros_like(k)
        parts = []
        for mine in (low, jnp.logical_not(low)):
            scores = dot_t(q, jnp.where(mine, k, zero)) + bias
            expo = jnp.exp2((scores - jnp.max(scores, axis=-1, keepdims=True)) * scale)
            probs = (expo * (1.0 / jnp.sum(expo, axis=-1, keepdims=True))).astype(jnp.bfloat16)
            parts.append(dot(probs, v))
        o_ref[:, cols] = jnp.where(low, parts[0], parts[1]).astype(jnp.bfloat16)


def encoder_attention(slot, span_ids, seg_lengths, q, k, v):
    smem = pl.BlockSpec(memory_space=pltpu.SMEM)
    vmem = pl.BlockSpec(memory_space=pltpu.VMEM)
    return pl.pallas_call(
        encoder_attention_kernel,
        out_shape=jax.ShapeDtypeStruct((SEG_LEN, D_ENC), jnp.bfloat16),
        in_specs=[smem, smem, smem, vmem, vmem, vmem],
        out_specs=vmem,
        compiler_params=params(),
        cost_estimate=pl.CostEstimate(
            flops=8 * SEG_LEN * SEG_LEN * D_ENC, bytes_accessed=8 * SEG_LEN * D_ENC,
            transcendentals=SEG_LEN * SEG_LEN * ENC_HEADS),
        name="encoder_attention",
    )(slot, span_ids, seg_lengths, q, k, v)


def encode_kernel(place_ref, gain_ref, ctx_ref, resid_ref, mine_ref, other_ref, *refs):
    kv_refs, o_ref = refs[:5], refs[5]
    w_ref, enc_ref, done_ref = refs[6:9]
    kv_bufs, in_sems, out_sems = refs[9:13], refs[13], refs[14]
    z, core, odd = place_ref[0], place_ref[1], place_ref[2]
    copies = []
    for side in range(2):
        some = pl.ds(8 * side, 8)
        sources = [kv_refs[0].at[some], kv_refs[1].at[some], kv_refs[2].at[some], kv_refs[3 + side]]
        copies.append([pltpu.make_async_copy(source, kv_bufs[i].at[some], in_sems.at[4 * side + i])
                       for i, source in enumerate(sources)])
    for side in range(2):
        for copy in copies[side]:
            copy.start()

    for part_ref, at in ((mine_ref, core), (other_ref, 1 - core)):
        for ha in range(KV_HEADS):
            plane = lax.rem(z + 32 - ha - 8 * at, 16)
            for yl in range(2):
                for c in range(2):
                    row = pl.multiple_of(64 * plane + 32 * yl + 16 * c, 16)
                    w_ref[:, pl.ds(row, 16), :] = part_ref[ha * 2 + yl, c]
    ctx = ctx_ref[...]
    hidden = jnp.concatenate(
        [dot(ctx, jnp.concatenate([w_ref[2 * j], w_ref[2 * j + 1]], axis=1)) for j in range(4)], axis=1)
    hidden = hidden + resid_ref[...].astype(jnp.float32)
    factor = lax.rsqrt(jnp.mean(hidden * hidden, axis=-1, keepdims=True) + 1e-05)
    encoded = (hidden * factor * gain_ref[...]).astype(jnp.bfloat16)
    for piece in range(4):
        enc_ref[piece] = encoded[:, piece * 256:(piece + 1) * 256]
    near, far = 2 * core, 2 - 2 * core
    pieces = [enc_ref[near + odd], enc_ref[near + 1 - odd], enc_ref[far + odd], enc_ref[far + 1 - odd]]

    def rows(ref, h):
        return jnp.concatenate(
            [jnp.concatenate([ref[2 * h + yl, :128], ref[2 * h + yl, 128:]], axis=1) for yl in range(2)], axis=0)

    sends = []
    for h in range(KV_HEADS):
        if h % 4 == 0:
            for copy in copies[h // 4]:
                copy.wait()
        total = dot(pieces[0], rows(kv_bufs[0], h))
        for i in range(1, 4):
            total += dot(pieces[i], rows(kv_bufs[i], h))
        done_ref[h, :SEG_LEN] = total[:, :HEAD].astype(jnp.bfloat16)
        done_ref[h, SEG_LEN:] = total[:, HEAD:].astype(jnp.bfloat16)
        sends.append(pltpu.make_async_copy(done_ref.at[h], o_ref.at[h], out_sems.at[h]))
        sends[h].start()
    for send in sends:
        send.wait()


def encode(place, gain, ctx, resid, mine, other, kvs):
    smem = pl.BlockSpec(memory_space=pltpu.SMEM)
    vmem = pl.BlockSpec(memory_space=pltpu.VMEM)
    hbm = pl.BlockSpec(memory_space=pltpu.HBM)
    shape = jax.ShapeDtypeStruct((KV_HEADS, 2 * SEG_LEN, HEAD), jnp.bfloat16)
    return pl.pallas_call(
        encode_kernel,
        out_shape=shape,
        in_specs=[smem] + [vmem] * 5 + [hbm] * 5,
        out_specs=hbm,
        scratch_shapes=[pltpu.VMEM((8, D_ENC, HEAD), jnp.bfloat16),
                        pltpu.VMEM((4, SEG_LEN, 256), jnp.bfloat16),
                        pltpu.VMEM(shape.shape, shape.dtype)]
        + [pltpu.VMEM(kvs[0].shape, kvs[0].dtype)] * 4
        + [pltpu.SemaphoreType.DMA((8,)), pltpu.SemaphoreType.DMA((KV_HEADS,))],
        compiler_params=params(48),
        cost_estimate=pl.CostEstimate(
            flops=6 * SEG_LEN * D_ENC * D_ENC, bytes_accessed=8 * D_ENC * D_ENC, transcendentals=SEG_LEN),
        name="encode_keyval",
    )(place, gain, ctx, resid, mine, other, *kvs)


def cross_kernel(slots, first_ref, span_ref, len_ref, q_ref, kv_ref, o_ref):
    scale = 1.0 / math.sqrt(HEAD)
    lane = lax.broadcasted_iota(jnp.int32, (1, SEG_LEN), 1)
    bias = []
    for s in range(slots):
        valid = len_ref[span_ref[first_ref[0] + s * first_ref[1]]]
        bias.append(jnp.where(lane < valid, 0.0, MASKED).astype(jnp.float32))
    bias = jnp.concatenate(bias, axis=1)
    keys = kv_ref[:, :SEG_LEN].reshape(slots * SEG_LEN, HEAD)
    values = kv_ref[:, SEG_LEN:].reshape(slots * SEG_LEN, HEAD)
    rows = 2 * QTAIL
    column = lax.broadcasted_iota(jnp.int32, (rows, HEAD), 1)
    levels = jnp.zeros((rows, HEAD), jnp.float32)

    def put(at, block):
        block = block.reshape(2, QTAIL, HEAD)
        o_ref[:, :, at * HEAD:(at + 1) * HEAD] = jnp.stack([block[0], block[1]], axis=1).astype(jnp.bfloat16)

    for b in range(GROUP // 2):
        q = q_ref[b * rows:(b + 1) * rows]
        scores = dot_t(q, keys) + bias
        top = jnp.max(scores, axis=-1, keepdims=True)
        expo = jnp.exp2((scores - top) * (scale * math.log2(math.e)))
        total = jnp.sum(expo, axis=-1, keepdims=True)
        put(b, dot(expo.astype(jnp.bfloat16), values) / total)
        level = jnp.broadcast_to(top * scale + jnp.log(total), (rows, HEAD))
        high = level.astype(jnp.bfloat16).astype(jnp.float32)
        middle = (level - high).astype(jnp.bfloat16).astype(jnp.float32)
        rest = level - high - middle
        for k, part in enumerate((high, middle, rest)):
            levels = jnp.where(column == 3 * b + k, part, levels)
    put(GROUP // 2, levels)


def cross_attention(first, span_ids, seg_lengths, q, kv):
    smem = pl.BlockSpec(memory_space=pltpu.SMEM)
    vmem = pl.BlockSpec(memory_space=pltpu.VMEM)
    slots = kv.shape[0]
    return pl.pallas_call(
        functools.partial(cross_kernel, slots),
        out_shape=jax.ShapeDtypeStruct((QTAIL, 2, 640), jnp.bfloat16),
        in_specs=[smem, smem, smem, vmem, vmem],
        out_specs=vmem,
        compiler_params=params(),
        name="cross_attention",
    )(first, span_ids, seg_lengths, q, kv)


def merge_kernel(part_ref, o_ref):
    pieces = part_ref[:, :, 4 * HEAD:].astype(jnp.float32)
    level = pieces + pltpu.roll(pieces, HEAD - 1, 2) + pltpu.roll(pieces, HEAD - 2, 2)
    weight = jnp.exp(level - jnp.max(level, axis=0, keepdims=True))
    total = jnp.sum(weight, axis=0)
    for b in range(GROUP // 2):
        average = part_ref[:, :, HEAD * b:HEAD * (b + 1)].astype(jnp.float32)
        at = slice(3 * b, 3 * b + 1)
        o_ref[2 * b:2 * b + 2] = jnp.sum(average * weight[:, :, at], axis=0) / total[:, at]


def merge(parts):
    vmem = pl.BlockSpec(memory_space=pltpu.VMEM)
    return pl.pallas_call(
        merge_kernel,
        out_shape=jax.ShapeDtypeStruct((GROUP, HEAD), jnp.float32),
        in_specs=[vmem],
        out_specs=vmem,
        name="merge_partials",
    )(parts)


def spread(block, axes):
    count = lax.axis_size(axes)
    copies = jnp.broadcast_to(block[None], (count,) + block.shape)
    return lax.all_to_all(copies, axes, 0, 0, tiled=True)


def local(enc_query, enc_key, enc_value, enc_resid, out_weight, norm_gain, kv_weight, cross_query,
          span_ids, seg_lengths):
    ha = lax.axis_index(HA)
    sa = lax.axis_index(SA)
    sa_count = lax.axis_size(SA)
    core = lax.axis_index("c")

    yl, z = lax.axis_index("yl"), lax.axis_index("z")
    swap = functools.partial(lax.ppermute, axis_name="c", perm=[(0, 1), (1, 0)])

    odd = lax.rem(z, 2)

    with jax.named_scope("pair_out_weight"):
        pair = lax.all_gather(out_weight.reshape(16, 8, HEAD).transpose(1, 0, 2), "c")
    with jax.named_scope("gather_kv_weight"):
        eighth = lax.dynamic_slice_in_dim(
            kv_weight.reshape(D_ENC, 2 * HEAD), core * 512 + odd * 256 + yl * 128, 128, 0)
        kv_mine = spread(jnp.concatenate([eighth[:, :HEAD], eighth[:, HEAD:]], axis=0), PLANE)
    with jax.named_scope("out_weight_over_z"):
        hops = []
        for ha_at in range(8):
            for z_at in range(16):
                for c_at in range(2):
                    there = (z_at + ha_at + 8 * c_at) % 16
                    hops.append(((ha_at * 16 + z_at) * 2 + c_at, (ha_at * 16 + there) * 2 + c_at))
        pair = lax.ppermute(pair, ("yh", "x", "z", "c"), hops)
    slot = (ha * sa_count + sa).reshape(1).astype(jnp.int32)
    context = encoder_attention(slot, span_ids, seg_lengths, enc_query, enc_key, enc_value)
    kv_mine, pair, context = lax.optimization_barrier((kv_mine, pair, context))
    with jax.named_scope("out_weight_over_plane"):
        w_mine = spread(pair, PLANE)
    with jax.named_scope("kv_weight_over_z"):
        pairs = []
        for z_at in range(16):
            for c_at in range(2):
                there = (z_at + (1 if (z_at + c_at) % 2 == 0 else 15)) % 16
                pairs.append((2 * z_at + c_at, 2 * there + c_at))
        kv_next = lax.ppermute(kv_mine, ("z", "c"), pairs)
    with jax.named_scope("swap_weights"):
        far = [swap(kv_next[:8]), swap(kv_next[8:])]
        w_mine, far = lax.optimization_barrier((w_mine, far))
        w_other = swap(w_mine)
        kvs = [kv_mine, kv_next, swap(kv_mine)] + far
    place = jnp.stack([z, core, odd]).astype(jnp.int32)
    keyval = encode(place, norm_gain.reshape(1, D_ENC), context, enc_resid, w_mine, w_other, kvs)
    with jax.named_scope("exchange_keyval"):
        keyval = lax.all_to_all(keyval, HA, 0, 0, tiled=True)
    first = jnp.stack([sa, sa_count]).astype(jnp.int32)
    query = cross_query.reshape(QTAIL, GROUP, HEAD).transpose(1, 0, 2).reshape(GROUP * QTAIL, HEAD)
    parts = cross_attention(first, span_ids, seg_lengths, query, keyval)
    with jax.named_scope("exchange_partials"):
        parts = lax.all_to_all(parts, SA, 0, 0, tiled=True)
    return merge(parts).reshape(1, 1, GROUP * HEAD)


def solution(mesh):
    fine = Mesh(mesh.devices.reshape(2, 4, 16, 2, 2), PARTS)
    rows = P(PARTS, None)
    heads = P(None, HA, None)
    placed = (rows, rows, rows, rows, P(SA, None), P(), heads, heads, P(), P())
    return jax.shard_map(
        local, mesh=fine, in_specs=placed, out_specs=P(SA, HA, None), check_vma=False
    )
```

```python
import functools
import math

import jax
import jax.numpy as jnp
import numpy as np
from jax import lax
from jax.experimental import pallas as pl
from jax.experimental.pallas import tpu as pltpu
from jax.sharding import Mesh, PartitionSpec as P

D_ENC = 1024
ENC_HEADS = 16
ENC_HEAD = D_ENC // ENC_HEADS
KV_HEADS = 8
GROUP = 8
HEAD = 128
SEG_LEN = 256
QTAIL = 64
MASKED = -1e30
SHIFTS = (0, 1, 15, 2, 14, 3, 13, 4)

PARTS = ("yh", "x", "z", "yl", "c")
HA = ("yh", "x")
SA = ("z", "yl", "c")
PLANE = ("yh", "x", "yl")


def params(mebibytes=20):
    return pltpu.CompilerParams(vmem_limit_bytes=mebibytes * 1024 * 1024)


def dot(a, b):
    return jnp.dot(a, b, preferred_element_type=jnp.float32)


def dot_t(a, b):
    return lax.dot_general(a, b, (((1,), (1,)), ((), ())), preferred_element_type=jnp.float32)


def encoder_attention_kernel(slot_ref, span_ref, len_ref, q_ref, k_ref, v_ref, o_ref):
    valid = len_ref[span_ref[slot_ref[0]]]
    keep = lax.broadcasted_iota(jnp.int32, (1, SEG_LEN), 1) < valid
    bias = jnp.where(keep, 0.0, MASKED).astype(jnp.float32)
    low = lax.broadcasted_iota(jnp.int32, (SEG_LEN, 2 * ENC_HEAD), 1) < ENC_HEAD
    scale = math.log2(math.e) / math.sqrt(ENC_HEAD)
    for pair in range(ENC_HEADS // 2):
        cols = slice(pair * 2 * ENC_HEAD, (pair + 1) * 2 * ENC_HEAD)
        q, k, v = q_ref[:, cols], k_ref[:, cols], v_ref[:, cols]
        zero = jnp.zeros_like(k)
        parts = []
        for mine in (low, jnp.logical_not(low)):
            scores = dot_t(q, jnp.where(mine, k, zero)) + bias
            expo = jnp.exp2((scores - jnp.max(scores, axis=-1, keepdims=True)) * scale)
            probs = (expo * (1.0 / jnp.sum(expo, axis=-1, keepdims=True))).astype(jnp.bfloat16)
            parts.append(dot(probs, v))
        o_ref[:, cols] = jnp.where(low, parts[0], parts[1]).astype(jnp.bfloat16)


def encoder_attention(slot, span_ids, seg_lengths, q, k, v):
    smem = pl.BlockSpec(memory_space=pltpu.SMEM)
    vmem = pl.BlockSpec(memory_space=pltpu.VMEM)
    return pl.pallas_call(
        encoder_attention_kernel,
        out_shape=jax.ShapeDtypeStruct((SEG_LEN, D_ENC), jnp.bfloat16),
        in_specs=[smem, smem, smem, vmem, vmem, vmem],
        out_specs=vmem,
        compiler_params=params(),
        cost_estimate=pl.CostEstimate(
            flops=8 * SEG_LEN * SEG_LEN * D_ENC, bytes_accessed=8 * SEG_LEN * D_ENC,
            transcendentals=SEG_LEN * SEG_LEN * ENC_HEADS),
        name="encoder_attention",
    )(slot, span_ids, seg_lengths, q, k, v)


def encode_kernel(place_ref, gain_ref, ctx_ref, resid_ref, mine_ref, other_ref, *refs):
    kv_refs, o_ref = refs[:5], refs[5]
    w_ref, enc_ref, done_ref = refs[6:9]
    kv_bufs, in_sems, out_sems = refs[9:13], refs[13], refs[14]
    z, core, odd = place_ref[0], place_ref[1], place_ref[2]
    copies = []
    for side in range(2):
        some = pl.ds(8 * side, 8)
        sources = [kv_refs[0].at[some], kv_refs[1].at[some], kv_refs[2].at[some], kv_refs[3 + side]]
        copies.append([pltpu.make_async_copy(source, kv_bufs[i].at[some], in_sems.at[4 * side + i])
                       for i, source in enumerate(sources)])
    for side in range(2):
        for copy in copies[side]:
            copy.start()

    for part_ref, at in ((mine_ref, core), (other_ref, 1 - core)):
        for ha in range(KV_HEADS):
            plane = lax.rem(z + 32 - SHIFTS[ha] - 8 * at, 16)
            for yl in range(2):
                for c in range(2):
                    row = pl.multiple_of(64 * plane + 32 * yl + 16 * c, 16)
                    w_ref[:, pl.ds(row, 16), :] = part_ref[ha * 2 + yl, c]
    ctx = ctx_ref[...]
    hidden = jnp.concatenate(
        [dot(ctx, jnp.concatenate([w_ref[2 * j], w_ref[2 * j + 1]], axis=1)) for j in range(4)], axis=1)
    hidden = hidden + resid_ref[...].astype(jnp.float32)
    factor = lax.rsqrt(jnp.mean(hidden * hidden, axis=-1, keepdims=True) + 1e-05)
    encoded = (hidden * factor * gain_ref[...]).astype(jnp.bfloat16)
    for piece in range(4):
        enc_ref[piece] = encoded[:, piece * 256:(piece + 1) * 256]
    near, far = 2 * core, 2 - 2 * core
    pieces = [enc_ref[near + odd], enc_ref[near + 1 - odd], enc_ref[far + odd], enc_ref[far + 1 - odd]]

    def rows(ref, h):
        return jnp.concatenate(
            [jnp.concatenate([ref[2 * h + yl, :128], ref[2 * h + yl, 128:]], axis=1) for yl in range(2)], axis=0)

    sends = []
    for h in range(KV_HEADS):
        if h % 4 == 0:
            for copy in copies[h // 4]:
                copy.wait()
        total = dot(pieces[0], rows(kv_bufs[0], h))
        for i in range(1, 4):
            total += dot(pieces[i], rows(kv_bufs[i], h))
        done_ref[h, :SEG_LEN] = total[:, :HEAD].astype(jnp.bfloat16)
        done_ref[h, SEG_LEN:] = total[:, HEAD:].astype(jnp.bfloat16)
        sends.append(pltpu.make_async_copy(done_ref.at[h], o_ref.at[h], out_sems.at[h]))
        sends[h].start()
    for send in sends:
        send.wait()


def encode(place, gain, ctx, resid, mine, other, kvs):
    smem = pl.BlockSpec(memory_space=pltpu.SMEM)
    vmem = pl.BlockSpec(memory_space=pltpu.VMEM)
    hbm = pl.BlockSpec(memory_space=pltpu.HBM)
    shape = jax.ShapeDtypeStruct((KV_HEADS, 2 * SEG_LEN, HEAD), jnp.bfloat16)
    return pl.pallas_call(
        encode_kernel,
        out_shape=shape,
        in_specs=[smem] + [vmem] * 5 + [hbm] * 5,
        out_specs=hbm,
        scratch_shapes=[pltpu.VMEM((8, D_ENC, HEAD), jnp.bfloat16),
                        pltpu.VMEM((4, SEG_LEN, 256), jnp.bfloat16),
                        pltpu.VMEM(shape.shape, shape.dtype)]
        + [pltpu.VMEM(kvs[0].shape, kvs[0].dtype)] * 4
        + [pltpu.SemaphoreType.DMA((8,)), pltpu.SemaphoreType.DMA((KV_HEADS,))],
        compiler_params=params(48),
        cost_estimate=pl.CostEstimate(
            flops=6 * SEG_LEN * D_ENC * D_ENC, bytes_accessed=8 * D_ENC * D_ENC, transcendentals=SEG_LEN),
        name="encode_keyval",
    )(place, gain, ctx, resid, mine, other, *kvs)


def cross_kernel(slots, first_ref, span_ref, len_ref, q_ref, kv_ref, o_ref):
    scale = 1.0 / math.sqrt(HEAD)
    lane = lax.broadcasted_iota(jnp.int32, (1, SEG_LEN), 1)
    bias = []
    for s in range(slots):
        valid = len_ref[span_ref[first_ref[0] + s * first_ref[1]]]
        bias.append(jnp.where(lane < valid, 0.0, MASKED).astype(jnp.float32))
    bias = jnp.concatenate(bias, axis=1)
    keys = kv_ref[:, :SEG_LEN].reshape(slots * SEG_LEN, HEAD)
    values = kv_ref[:, SEG_LEN:].reshape(slots * SEG_LEN, HEAD)
    rows = 2 * QTAIL
    column = lax.broadcasted_iota(jnp.int32, (rows, HEAD), 1)
    levels = jnp.zeros((rows, HEAD), jnp.float32)

    def put(at, block):
        block = block.reshape(2, QTAIL, HEAD)
        o_ref[:, :, at * HEAD:(at + 1) * HEAD] = jnp.stack([block[0], block[1]], axis=1).astype(jnp.bfloat16)

    for b in range(GROUP // 2):
        q = q_ref[b * rows:(b + 1) * rows]
        scores = dot_t(q, keys) + bias
        top = jnp.max(scores, axis=-1, keepdims=True)
        expo = jnp.exp2((scores - top) * (scale * math.log2(math.e)))
        total = jnp.sum(expo, axis=-1, keepdims=True)
        put(b, dot(expo.astype(jnp.bfloat16), values) / total)
        level = jnp.broadcast_to(top * scale + jnp.log(total), (rows, HEAD))
        high = level.astype(jnp.bfloat16).astype(jnp.float32)
        middle = (level - high).astype(jnp.bfloat16).astype(jnp.float32)
        rest = level - high - middle
        for k, part in enumerate((high, middle, rest)):
            levels = jnp.where(column == 3 * b + k, part, levels)
    put(GROUP // 2, levels)


def cross_attention(first, span_ids, seg_lengths, q, kv):
    smem = pl.BlockSpec(memory_space=pltpu.SMEM)
    vmem = pl.BlockSpec(memory_space=pltpu.VMEM)
    slots = kv.shape[0]
    return pl.pallas_call(
        functools.partial(cross_kernel, slots),
        out_shape=jax.ShapeDtypeStruct((QTAIL, 2, 640), jnp.bfloat16),
        in_specs=[smem, smem, smem, vmem, vmem],
        out_specs=vmem,
        compiler_params=params(),
        name="cross_attention",
    )(first, span_ids, seg_lengths, q, kv)


def merge_kernel(part_ref, o_ref):
    pieces = part_ref[:, :, 4 * HEAD:].astype(jnp.float32)
    level = pieces + pltpu.roll(pieces, HEAD - 1, 2) + pltpu.roll(pieces, HEAD - 2, 2)
    weight = jnp.exp(level - jnp.max(level, axis=0, keepdims=True))
    total = jnp.sum(weight, axis=0)
    for b in range(GROUP // 2):
        average = part_ref[:, :, HEAD * b:HEAD * (b + 1)].astype(jnp.float32)
        at = slice(3 * b, 3 * b + 1)
        o_ref[2 * b:2 * b + 2] = jnp.sum(average * weight[:, :, at], axis=0) / total[:, at]


def merge(parts):
    vmem = pl.BlockSpec(memory_space=pltpu.VMEM)
    return pl.pallas_call(
        merge_kernel,
        out_shape=jax.ShapeDtypeStruct((GROUP, HEAD), jnp.float32),
        in_specs=[vmem],
        out_specs=vmem,
        name="merge_partials",
    )(parts)


def spread(block, axes):
    count = lax.axis_size(axes)
    copies = jnp.broadcast_to(block[None], (count,) + block.shape)
    return lax.all_to_all(copies, axes, 0, 0, tiled=True)


def local(enc_query, enc_key, enc_value, enc_resid, out_weight, norm_gain, kv_weight, cross_query,
          span_ids, seg_lengths):
    ha = lax.axis_index(HA)
    sa = lax.axis_index(SA)
    sa_count = lax.axis_size(SA)
    core = lax.axis_index("c")

    yl, z = lax.axis_index("yl"), lax.axis_index("z")
    swap = functools.partial(lax.ppermute, axis_name="c", perm=[(0, 1), (1, 0)])

    odd = lax.rem(z, 2)

    with jax.named_scope("pair_out_weight"):
        pair = lax.all_gather(out_weight.reshape(16, 8, HEAD).transpose(1, 0, 2), "c")
    with jax.named_scope("gather_kv_weight"):
        eighth = lax.dynamic_slice_in_dim(
            kv_weight.reshape(D_ENC, 2 * HEAD), core * 512 + odd * 256 + yl * 128, 128, 0)
        pair, eighth = lax.optimization_barrier((pair, eighth))
        kv_mine = spread(jnp.concatenate([eighth[:, :HEAD], eighth[:, HEAD:]], axis=0), PLANE)
    with jax.named_scope("out_weight_over_z"):
        hops = []
        for ha_at in range(8):
            for z_at in range(16):
                for c_at in range(2):
                    there = (z_at + SHIFTS[ha_at] + 8 * c_at) % 16
                    hops.append(((ha_at * 16 + z_at) * 2 + c_at, (ha_at * 16 + there) * 2 + c_at))
        pair = lax.ppermute(pair, ("yh", "x", "z", "c"), hops)
    slot = (ha * sa_count + sa).reshape(1).astype(jnp.int32)
    context = encoder_attention(slot, span_ids, seg_lengths, enc_query, enc_key, enc_value)
    kv_mine, pair, context = lax.optimization_barrier((kv_mine, pair, context))
    with jax.named_scope("out_weight_over_plane"):
        w_mine = spread(pair, PLANE)
    with jax.named_scope("kv_weight_over_z"):
        pairs = []
        for z_at in range(16):
            for c_at in range(2):
                there = (z_at + (1 if (z_at + c_at) % 2 == 0 else 15)) % 16
                pairs.append((2 * z_at + c_at, 2 * there + c_at))
        kv_next = lax.ppermute(kv_mine, ("z", "c"), pairs)
    with jax.named_scope("swap_weights"):
        far = [swap(kv_next[:8]), swap(kv_next[8:])]
        w_mine, far = lax.optimization_barrier((w_mine, far))
        w_other = swap(w_mine)
        kvs = [kv_mine, kv_next, swap(kv_mine)] + far
    place = jnp.stack([z, core, odd]).astype(jnp.int32)
    keyval = encode(place, norm_gain.reshape(1, D_ENC), context, enc_resid, w_mine, w_other, kvs)
    with jax.named_scope("exchange_keyval"):
        keyval = lax.all_to_all(keyval, HA, 0, 0, tiled=True)
    first = jnp.stack([sa, sa_count]).astype(jnp.int32)
    query = cross_query.reshape(QTAIL, GROUP, HEAD).transpose(1, 0, 2).reshape(GROUP * QTAIL, HEAD)
    parts = cross_attention(first, span_ids, seg_lengths, query, keyval)
    with jax.named_scope("exchange_partials"):
        parts = lax.all_to_all(parts, SA, 0, 0, tiled=True)
    return merge(parts).reshape(1, 1, GROUP * HEAD)


def solution(mesh):
    fine = Mesh(mesh.devices.reshape(2, 4, 16, 2, 2), PARTS)
    rows = P(PARTS, None)
    heads = P(None, HA, None)
    placed = (rows, rows, rows, rows, P(SA, None), P(), heads, heads, P(), P())
    return jax.shard_map(
        local, mesh=fine, in_specs=placed, out_specs=P(SA, HA, None), check_vma=False
    )
```
